32 devices in a mesh: seq: 8 (over y, x, core), batch: 4 (over z).
Axes of the slice: x: 2, y: 2, z: 4, core: 2. Of those that a mesh axis runs over, the one named last changes fastest.
Arguments:
- tokens: bfloat16 [4, 4096, 768], P('batch', 'seq'), may hold values from -6 to 6
- norm1_gain: float32 [768], replicated, may hold values from 0.5 to 1.5
- norm1_bias: float32 [768], replicated, may hold values from -1.75 to 1.75
- query_weight: bfloat16 [768, 768], replicated, may hold values from -0.21875 to 0.21875
- key_weight: bfloat16 [768, 768], replicated, may hold values from -0.21875 to 0.21875
- value_weight: bfloat16 [768, 768], replicated, may hold values from -0.21875 to 0.21875
- shift_taps: float32 [4, 768], replicated, may hold values from -3 to 3
- ssm_coef: float32 [64, 768], replicated, may hold values from -0.0234375 to 0.0234375
- ssm_rate: float32 [64, 768], replicated, may hold values from 3e-05 to 0.04
- ssm_skip: float32 [768], replicated, may hold values from -6 to 6
- out_weight: bfloat16 [768, 768], replicated, may hold values from -0.21875 to 0.21875
- norm2_gain: float32 [768], replicated, may hold values from 0.5 to 1.5
- norm2_bias: float32 [768], replicated, may hold values from -1.75 to 1.75
- up_weight: bfloat16 [768, 3072], replicated, may hold values from -0.21875 to 0.21875
- down_weight: bfloat16 [3072, 768], replicated, may hold values from -0.109375 to 0.109375
- out_grad: bfloat16 [4, 4096, 768], P('batch', 'seq'), may hold values from -6 to 6
Outputs:
- mixed_out: bfloat16 [4, 4096, 768], P('batch', 'seq')
- tokens_grad: float32 [4, 4096, 768], P('batch', 'seq')
- norm1_gain_grad: float32 [768], replicated
- norm1_bias_grad: float32 [768], replicated
- query_weight_grad: float32 [768, 768], replicated
- key_weight_grad: float32 [768, 768], replicated
- value_weight_grad: float32 [768, 768], replicated
- shift_taps_grad: float32 [4, 768], replicated
- ssm_coef_grad: float32 [64, 768], replicated
- ssm_rate_grad: float32 [64, 768], replicated
- ssm_skip_grad: float32 [768], replicated
- out_weight_grad: float32 [768, 768], replicated
- norm2_gain_grad: float32 [768], replicated
- norm2_bias_grad: float32 [768], replicated
- up_weight_grad: float32 [768, 3072], replicated
- down_weight_grad: float32 [3072, 768], replicated
The draws below stay inside these ranges and needn't reach their ends.
All inputs are finite; a program needn't handle non-finite values.
Results may differ from the reference program's by a relative error of at most 0.0077.
Values sent between devices are 32-bit elements; how exact they have to be, the bound alone decides.
A program may use at most 256 MiB of HBM per device.

```python
import math
import jax
import jax.numpy as jnp
from jax import lax

D = 768
FF = 3072
STATE = 64
SHIFT = 4
LEN = 4096
SEQS = 4


def steps_of(own_key, shape, cuts, low, high):
    gain, own = 1.0, jax.random.fold_in(own_key, 6)
    for dim, shards_of in cuts:
        steps = jnp.exp(jax.random.uniform(jax.random.fold_in(own, dim), (shards_of,), jnp.float32, low / len(cuts), high / len(cuts)))
        gain = gain * jnp.repeat(steps, shape[dim] // shards_of).reshape([-1 if axis == dim else 1 for axis in range(len(shape))])
    return gain


def noise(own_key, dims, scale, bound, cuts=(), kind=jnp.bfloat16):
    array = scale * jax.random.normal(own_key, dims, jnp.float32)
    if cuts:
        array = array * steps_of(own_key, dims, cuts, -0.22, 0.18)
    return jnp.clip(array, -bound, bound).astype(kind)


def setup_inputs(seed: int = 0) -> dict:
    seeds = jax.random.split(jax.random.key(seed), 17)
    return {
        "tokens": noise(seeds[0], (SEQS, LEN, D), 1.0, 6.0, ((0, 4), (1, 8))),
        "norm1_gain": jnp.clip(1.0 + 0.1 * jax.random.normal(seeds[1], (D,), jnp.float32), 0.5, 1.5),
        "norm1_bias": noise(seeds[2], (D,), 0.3, 1.75, (), jnp.float32),
        "query_weight": noise(seeds[3], (D, D), D ** -0.5, 0.21875),
        "key_weight": noise(seeds[4], (D, D), D ** -0.5, 0.21875),
        "value_weight": noise(seeds[5], (D, D), D ** -0.5, 0.21875),
        "shift_taps": noise(seeds[6], (SHIFT, D), 0.5, 3.0, (), jnp.float32),
        "ssm_coef": noise(seeds[7], (STATE, D), (STATE * LEN // 4) ** -0.5, 0.0234375, (), jnp.float32),
        "ssm_rate": jnp.clip(jnp.exp(jax.random.uniform(seeds[8], (STATE, D), jnp.float32, math.log(2.9999999242136255e-05), math.log(0.04))), 2.9999999242136255e-05, 0.04),
        "ssm_skip": noise(seeds[9], (D,), 1.0, 6.0, (), jnp.float32),
        "out_weight": noise(seeds[10], (D, D), D ** -0.5, 0.21875),
        "norm2_gain": jnp.clip(1.0 + 0.1 * jax.random.normal(seeds[11], (D,), jnp.float32), 0.5, 1.5),
        "norm2_bias": noise(seeds[12], (D,), 0.3, 1.75, (), jnp.float32),
        "up_weight": noise(seeds[13], (D, FF), D ** -0.5, 0.21875),
        "down_weight": noise(seeds[14], (FF, D), FF ** -0.5, 0.109375),
        "out_grad": noise(seeds[15], (SEQS, LEN, D), 1.0, 6.0, ((0, 4), (1, 8))),
    }


@jax.custom_vjp
def low(v):
    return lax.optimization_barrier(v.astype(jnp.bfloat16)).astype(jnp.float32)

@jax.custom_vjp
def low_back(v):
    return v

def low_keep(v):
    return (low(v), None)

def low_pass(kept, grad):
    return (grad,)

def back_keep(v):
    return (v, None)

def back_low(kept, grad):
    return (low(grad),)
low.defvjp(low_keep, low_pass)
low_back.defvjp(back_keep, back_low)
epsilon = 1e-05
highest = lax.Precision.HIGHEST

def layer_norm(values, norm_gain, norm_bias):
    row_mean = lax.optimization_barrier(jnp.mean(values, axis=-1, keepdims=True))
    centered = values - row_mean
    spread = lax.optimization_barrier(jnp.mean(centered * centered, axis=-1, keepdims=True))
    return centered * lax.rsqrt(spread + epsilon) * norm_gain + norm_bias

def kernel_table(state_coef, state_rate, positions):
    channels = state_coef.shape[1]
    coef_blocks = state_coef.reshape(-1, 8, channels)
    rate_blocks = state_rate.reshape(-1, 8, channels)

    def add_block(running, members):
        decays = jnp.exp(-members[1][None] * positions[:, None, None])
        return (running + lax.optimization_barrier(jnp.sum(members[0][None] * decays, axis=1)), None)
    initial = jnp.zeros((positions.shape[0], channels), state_coef.dtype)
    running, unused = lax.scan(jax.checkpoint(add_block), initial, (coef_blocks, rate_blocks))
    return running

def shift_mix(key_rows, taps):
    tap_count = taps.shape[0]
    padded = jnp.pad(key_rows, ((tap_count - 1, 0), (0, 0)))
    running = jnp.zeros_like(key_rows)
    for offset in range(tap_count):
        lead_rows = tap_count - 1 - offset
        running = running + taps[offset] * padded[lead_rows:lead_rows + key_rows.shape[0]]
    return running

def long_mix(signal, kernel):
    length = signal.shape[0]
    spectrum = jnp.fft.rfft(signal, n=2 * length, axis=0) * jnp.fft.rfft(kernel, n=2 * length, axis=0)
    return jnp.fft.irfft(spectrum, n=2 * length, axis=0)[:length]

def reference(tokens, norm1_gain, norm1_bias, query_weight, key_weight, value_weight, shift_taps, ssm_coef, ssm_rate, ssm_skip, out_weight, norm2_gain, norm2_bias, up_weight, down_weight, out_grad):
    positions = jnp.arange(LEN, dtype=jnp.float32)

    def forward(inputs, gain_one, bias_one, w_query, w_key, w_value, taps, state_coef, state_rate, skip_gain, w_out, gain_two, bias_two, w_up, w_down):
        kernel = kernel_table(state_coef, state_rate, positions)

        def one_sequence(sequence):
            normed = low(layer_norm(sequence, gain_one, bias_one))
            queries = low_back(jnp.dot(normed, w_query, precision=highest))
            key_rows = low_back(jnp.dot(normed, w_key, precision=highest))
            value_rows = low_back(jnp.dot(normed, w_value, precision=highest))
            keys_mixed = shift_mix(key_rows, taps)
            product = keys_mixed * value_rows
            mixed_rows = long_mix(product, kernel) + skip_gain * product
            gated = low(queries * mixed_rows)
            attended = low_back(jnp.dot(gated, w_out, precision=highest))
            middle = sequence + attended
            normed_two = low(layer_norm(middle, gain_two, bias_two))
            hidden_pre = low_back(jnp.dot(normed_two, w_up, precision=highest))
            activated = low(jax.nn.gelu(hidden_pre))
            return middle + jnp.dot(activated, w_down, precision=highest)
        return lax.map(jax.checkpoint(one_sequence), inputs)
    floats = (tokens.astype(jnp.float32), norm1_gain.astype(jnp.float32), norm1_bias.astype(jnp.float32), query_weight.astype(jnp.float32), key_weight.astype(jnp.float32), value_weight.astype(jnp.float32), shift_taps.astype(jnp.float32), ssm_coef.astype(jnp.float32), ssm_rate.astype(jnp.float32), ssm_skip.astype(jnp.float32), out_weight.astype(jnp.float32), norm2_gain.astype(jnp.float32), norm2_bias.astype(jnp.float32), up_weight.astype(jnp.float32), down_weight.astype(jnp.float32))
    result, pullback = jax.vjp(forward, *floats)
    grads = pullback(out_grad.astype(jnp.float32))
    return (result.astype(jnp.bfloat16), grads[0], grads[1], grads[2], grads[3], grads[4], grads[5], grads[6], grads[7], grads[8], grads[9], grads[10], grads[11], grads[12], grads[13], grads[14])
```

```python
import functools

import jax
import jax.numpy as jnp
from jax import lax
from jax.experimental import pallas as pl
from jax.experimental.pallas import tpu as pltpu
from jax.sharding import PartitionSpec as P

epsilon = 1e-05
CHUNKS = 16
GROUP = 8
LANES = 128


def passed_along(value, axis, steps):
    count = lax.axis_size(axis)
    leading, last = (max(0, -steps), min(count, count - steps))
    return lax.ppermute(value, axis, [(source, source + steps) for source in range(leading, last)])


def standardize(values):
    row_mean = jnp.mean(values, axis=-1, keepdims=True)
    centered = values - row_mean
    spread = jnp.mean(centered * centered, axis=-1, keepdims=True)
    factor = lax.rsqrt(spread + epsilon)
    return centered * factor, factor


def norm_back(grads, gain, standard, factor):
    scaled = grads * gain
    return factor * (
        scaled
        - jnp.mean(scaled, axis=-1, keepdims=True)
        - standard * jnp.mean(scaled * standard, axis=-1, keepdims=True)
    )


def project(rows_low, weight):
    return jnp.dot(rows_low, weight, preferred_element_type=jnp.float32)


def project_back(grads_low, weight):
    return lax.dot_general(
        grads_low, weight, (((1,), (1,)), ((), ())), preferred_element_type=jnp.float32
    )


def weight_grad(rows_low, grads_low):
    return lax.dot_general(
        rows_low, grads_low, (((0,), (0,)), ((), ())), preferred_element_type=jnp.float32
    )


def block(ref, place):
    return ref[place * CHUNKS : (place + 1) * CHUNKS, :]


def chunk_rows(chunk, states):
    return pl.ds(chunk, states, stride=CHUNKS)


def state_sums(width, rows_ref, decay_ref, out_ref, group, places, weight, lead):
    decay = decay_ref[pl.ds(group * GROUP, GROUP), :][:, None, :]
    running = jnp.zeros((GROUP, CHUNKS, LANES), jnp.float32)
    for place in places:
        rows = block(rows_ref, place)
        if weight is not None:
            rows = rows * weight(place)
        running = decay * (running + rows[None]) if lead else decay * running + rows[None]
    return running


def forward_states(width, rows_ref, rate_ref, sums_ref, last_ref, decay_ref):
    states = rate_ref.shape[0]
    decay_ref[...] = jnp.exp(-rate_ref[...])

    def body(group, unused):
        running = state_sums(width, rows_ref, decay_ref, None, group, range(width), None, False)
        sums_ref[pl.ds(group * GROUP * CHUNKS, GROUP * CHUNKS), :] = running.reshape(-1, LANES)
        return unused

    lax.fori_loop(0, states // GROUP, body, 0)
    hop = jnp.exp(-width * rate_ref[...])
    held = jnp.zeros((states, LANES), jnp.float32)
    for chunk in range(CHUNKS):
        held = hop * held + sums_ref[chunk_rows(chunk, states), :]
    last_ref[...] = held


def forward_mix(
    width,
    rows_ref,
    sums_ref,
    entering_ref,
    rate_ref,
    coef_ref,
    skip_ref,
    mixed_ref,
    held_ref,
    kernel_ref,
    decay_ref,
    taps_ref,
):
    states = rate_ref.shape[0]
    decay_ref[...] = jnp.exp(-rate_ref[...])
    hop = jnp.exp(-width * rate_ref[...])
    held = entering_ref[...]
    for chunk in range(CHUNKS):
        held_ref[chunk_rows(chunk, states), :] = held
        held = hop * held + sums_ref[chunk_rows(chunk, states), :]
    lags = lax.broadcasted_iota(jnp.int32, (8, LANES), 0).astype(jnp.float32)

    def add_state(state, totals):
        rate = rate_ref[pl.ds(state, 1), :]
        term = coef_ref[pl.ds(state, 1), :] * jnp.exp(-rate * lags)
        step = jnp.exp(-8.0 * rate)
        out = []
        for total in totals:
            out.append(total + term)
            term = term * step
        return tuple(out)

    totals = lax.fori_loop(
        0, states, add_state, tuple(jnp.zeros((8, LANES), jnp.float32) for _ in range(width // 8))
    )
    kernel_ref[...] = jnp.concatenate(totals, axis=0)
    for lag in range(width):
        taps_ref[lag * CHUNKS : (lag + 1) * CHUNKS, :] = jnp.broadcast_to(
            kernel_ref[lag : lag + 1, :], (CHUNKS, LANES)
        )
    for start in range(0, width, 4):
        sums = [skip_ref[...] * block(rows_ref, start + i) for i in range(4)]
        for place in range(start + 4):
            rows = block(rows_ref, place)
            for i in range(4):
                if start + i >= place:
                    sums[i] = sums[i] + block(taps_ref, start + i - place) * rows
        for i in range(4):
            mixed_ref[(start + i) * CHUNKS : (start + i + 1) * CHUNKS, :] = sums[i]

    def body(group, unused):
        decay = decay_ref[pl.ds(group * GROUP, GROUP), :][:, None, :]
        coef = coef_ref[pl.ds(group * GROUP, GROUP), :][:, None, :]
        term = held_ref[pl.ds(group * GROUP * CHUNKS, GROUP * CHUNKS), :].reshape(
            GROUP, CHUNKS, LANES
        )
        term = term * (coef * decay)
        for place in range(width):
            mixed_ref[place * CHUNKS : (place + 1) * CHUNKS, :] += jnp.sum(term, axis=0)
            if place < width - 1:
                term = term * decay
        return unused

    lax.fori_loop(0, states // GROUP, body, 0)


def backward_states(width, grads_ref, rate_ref, sums_ref, first_ref, decay_ref):
    states = rate_ref.shape[0]
    decay_ref[...] = jnp.exp(-rate_ref[...])

    def body(group, unused):
        running = state_sums(
            width, grads_ref, decay_ref, None, group, range(width - 1, -1, -1), None, True
        )
        sums_ref[pl.ds(group * GROUP * CHUNKS, GROUP * CHUNKS), :] = running.reshape(-1, LANES)
        return unused

    lax.fori_loop(0, states // GROUP, body, 0)
    hop = jnp.exp(-width * rate_ref[...])
    held = jnp.zeros((states, LANES), jnp.float32)
    for chunk in range(CHUNKS - 1, -1, -1):
        held = hop * held + sums_ref[chunk_rows(chunk, states), :]
    first_ref[...] = held


def backward_mix(
    width,
    grads_ref,
    rows_ref,
    sums_ref,
    held_ref,
    entering_ref,
    rate_ref,
    coef_ref,
    skip_ref,
    kernel_ref,
    back_ref,
    coef_grad_ref,
    rate_grad_ref,
    decay_ref,
    hop_ref,
    taps_ref,
    after_ref,
    lag_ref,
):
    states = rate_ref.shape[0]
    decay_ref[...] = jnp.exp(-rate_ref[...])
    hop = jnp.exp(-width * rate_ref[...])
    hop_ref[...] = hop
    held = entering_ref[...]
    for chunk in range(CHUNKS - 1, -1, -1):
        after_ref[chunk_rows(chunk, states), :] = held
        held = hop * held + sums_ref[chunk_rows(chunk, states), :]
    for lag in range(width):
        taps_ref[lag * CHUNKS : (lag + 1) * CHUNKS, :] = jnp.broadcast_to(
            kernel_ref[lag : lag + 1, :], (CHUNKS, LANES)
        )
    for start in range(0, width, 4):
        sums = [skip_ref[...] * block(grads_ref, start + i) for i in range(4)]
        for place in range(start, width):
            grads = block(grads_ref, place)
            for i in range(4):
                if place >= start + i:
                    sums[i] = sums[i] + block(taps_ref, place - start - i) * grads
        for i in range(4):
            back_ref[(start + i) * CHUNKS : (start + i + 1) * CHUNKS, :] = sums[i]
    for start in range(0, width, 4):
        sums = [jnp.zeros((CHUNKS, LANES), jnp.float32) for i in range(4)]
        for place in range(start, width):
            grads = block(grads_ref, place)
            for i in range(4):
                if place >= start + i:
                    sums[i] = sums[i] + block(rows_ref, place - start - i) * grads
        for i in range(4):
            lag_ref[start + i : start + i + 1, :] = jnp.sum(sums[i], axis=0, keepdims=True)
    decay_all = decay_ref[...]
    near_coef = jnp.zeros((states, LANES), jnp.float32)
    near_rate = jnp.zeros((states, LANES), jnp.float32)
    for lag in range(width - 1, -1, -1):
        near_coef = near_coef * decay_all + lag_ref[lag : lag + 1, :]
        near_rate = near_rate * decay_all + float(lag) * lag_ref[lag : lag + 1, :]
    coef_grad_ref[...] = near_coef
    rate_grad_ref[...] = near_rate

    def body(group, unused):
        members = pl.ds(group * GROUP, GROUP)
        cells = pl.ds(group * GROUP * CHUNKS, GROUP * CHUNKS)
        cube = (GROUP, CHUNKS, LANES)
        decay = decay_ref[members, :][:, None, :]
        coef = coef_ref[members, :][:, None, :]
        after = after_ref[cells, :].reshape(cube)
        term = after * coef
        for place in range(width - 1, -1, -1):
            back_ref[place * CHUNKS : (place + 1) * CHUNKS, :] += jnp.sum(term, axis=0)
            if place > 0:
                term = term * decay
        held = held_ref[cells, :].reshape(cube)
        coef_grad_ref[members, :] += jnp.sum(held * sums_ref[cells, :].reshape(cube), axis=1)
        slope = state_sums(
            width,
            rows_ref,
            decay_ref,
            None,
            group,
            range(width),
            lambda place: float(width - 1 - place),
            False,
        )
        total = after * (float(width) * hop_ref[members, :][:, None, :] * held + slope)
        slope = state_sums(
            width,
            grads_ref,
            decay_ref,
            None,
            group,
            range(width - 1, -1, -1),
            lambda place: float(place + 1),
            True,
        )
        total = total + held * slope
        rate_grad_ref[members, :] += jnp.sum(total, axis=1)
        return unused

    lax.fori_loop(0, states // GROUP, body, 0)
    rate_grad_ref[...] = -coef_ref[...] * rate_grad_ref[...]


def per_lanes(body, out_rows, scratch, *arrays):
    channels = arrays[0].shape[1]
    scratch = [pltpu.VMEM((rows, LANES), jnp.float32) for rows in scratch]
    return pl.pallas_call(
        body,
        grid=(channels // LANES,),
        in_specs=[pl.BlockSpec((array.shape[0], LANES), lambda i: (0, i)) for array in arrays],
        out_specs=[pl.BlockSpec((rows, LANES), lambda i: (0, i)) for rows in out_rows],
        out_shape=[jax.ShapeDtypeStruct((rows, channels), jnp.float32) for rows in out_rows],
        scratch_shapes=scratch,
        compiler_params=pltpu.CompilerParams(vmem_limit_bytes=40 * 2**20),
    )(*arrays)


def carried(own, rate, row_count, forward):
    count = lax.axis_size("seq")
    place = lax.axis_index("seq")
    every = lax.all_gather(own, "seq", axis=0)
    source = jnp.arange(count)
    hops = place - 1 - source if forward else source - 1 - place
    decays = jnp.exp(-rate[None] * (row_count * jnp.maximum(hops, 0)).astype(jnp.float32)[:, None, None])
    return jnp.sum(jnp.where(hops[:, None, None] >= 0, every * decays, 0.0), axis=0)


def on_device(
    tokens,
    norm1_gain,
    norm1_bias,
    query_weight,
    key_weight,
    value_weight,
    shift_taps,
    ssm_coef,
    ssm_rate,
    ssm_skip,
    out_weight,
    norm2_gain,
    norm2_bias,
    up_weight,
    down_weight,
    out_grad,
):
    unused, row_count, channels = tokens.shape
    width = row_count // CHUNKS
    states = ssm_rate.shape[0]
    tap_count = shift_taps.shape[0]
    halo = tap_count - 1

    def mixed_order(values):
        return values.reshape(CHUNKS, width, channels).swapaxes(0, 1).reshape(row_count, channels)

    def token_order(values):
        return values.reshape(width, CHUNKS, channels).swapaxes(0, 1).reshape(1, row_count, channels)

    low = jnp.bfloat16
    inputs = mixed_order(tokens).astype(jnp.float32)
    out_grad = mixed_order(out_grad)
    standard_one, factor_one = standardize(inputs)
    normed_low = (standard_one * norm1_gain + norm1_bias).astype(low)
    key_rows = project(normed_low, key_weight)
    key_blocks = key_rows.reshape(width, CHUNKS, channels)
    before = passed_along(key_blocks[width - halo :, CHUNKS - 1], "seq", 1)
    value_rows = project(normed_low, value_weight)
    queries = project(normed_low, query_weight)
    head = jnp.concatenate([before[:, None], key_blocks[width - halo :, : CHUNKS - 1]], axis=1)
    extended = jnp.concatenate([head.reshape(halo * CHUNKS, channels), key_rows], 0)

    def delayed(offset):
        start = (halo - offset) * CHUNKS
        return extended[start : start + row_count]

    keys_mixed = sum(shift_taps[offset] * delayed(offset) for offset in range(tap_count))
    product = keys_mixed * value_rows
    skip_row = ssm_skip[None]
    cells = states * CHUNKS
    sums, last = per_lanes(
        functools.partial(forward_states, width), [cells, states], [states], product, ssm_rate
    )
    entering = carried(last, ssm_rate, row_count, True)
    mixed_rows, held, kernel = per_lanes(
        functools.partial(forward_mix, width),
        [row_count, cells, width],
        [states, row_count],
        product,
        sums,
        entering,
        ssm_rate,
        ssm_coef,
        skip_row,
    )
    gated_rows = (queries * mixed_rows).astype(low)
    middle = inputs + project(gated_rows, out_weight)
    standard_two, factor_two = standardize(middle)
    normed_two_low = (standard_two * norm2_gain + norm2_bias).astype(low)
    hidden_pre = project(normed_two_low, up_weight)
    activated, gelu_pull = jax.vjp(jax.nn.gelu, hidden_pre)
    activated_low = activated.astype(low)
    mixed_out = (middle + project(activated_low, down_weight)).astype(low)
    grad_down = weight_grad(activated_low, out_grad)
    grad_hidden = gelu_pull(project_back(out_grad, down_weight))[0].astype(low)
    grad_up = weight_grad(normed_two_low, grad_hidden)
    grad_normed_two = project_back(grad_hidden, up_weight)
    grad_gain_two = jnp.sum(grad_normed_two * standard_two, axis=0)
    grad_bias_two = jnp.sum(grad_normed_two, axis=0)
    grad_middle = out_grad.astype(jnp.float32) + norm_back(
        grad_normed_two, norm2_gain, standard_two, factor_two
    )
    grad_attended = grad_middle.astype(low)
    grad_out_weight = weight_grad(gated_rows, grad_attended)
    grad_gated = project_back(grad_attended, out_weight)
    grad_queries = (grad_gated * mixed_rows).astype(low)
    grad_mixed = grad_gated * queries
    grad_skip = jnp.sum(grad_mixed * product, axis=0)
    grad_sums, first = per_lanes(
        functools.partial(backward_states, width), [cells, states], [states], grad_mixed, ssm_rate
    )
    grad_entering = carried(first, ssm_rate, row_count, False)
    grad_product, grad_coef, grad_rate = per_lanes(
        functools.partial(backward_mix, width),
        [row_count, states, states],
        [states, states, row_count, cells, width],
        grad_mixed,
        product,
        grad_sums,
        held,
        grad_entering,
        ssm_rate,
        ssm_coef,
        skip_row,
        kernel,
    )
    grad_keys_mixed = grad_product * value_rows
    grad_values = (grad_product * keys_mixed).astype(low)
    grad_blocks = grad_keys_mixed.reshape(width, CHUNKS, channels)
    after = passed_along(grad_blocks[:halo, 0], "seq", -1)
    tail = jnp.concatenate([grad_blocks[:halo, 1:], after[:, None]], axis=1)
    grad_extended = jnp.concatenate([grad_keys_mixed, tail.reshape(halo * CHUNKS, channels)], 0)
    grad_keys = sum(
        shift_taps[offset] * grad_extended[offset * CHUNKS : offset * CHUNKS + row_count]
        for offset in range(tap_count)
    ).astype(low)
    grad_taps = jnp.stack(
        [jnp.sum(grad_keys_mixed * delayed(offset), axis=0) for offset in range(tap_count)]
    )
    grad_query_weight = weight_grad(normed_low, grad_queries)
    grad_key_weight = weight_grad(normed_low, grad_keys)
    grad_value_weight = weight_grad(normed_low, grad_values)
    grad_normed = (
        project_back(grad_queries, query_weight)
        + project_back(grad_keys, key_weight)
        + project_back(grad_values, value_weight)
    )
    grad_gain_one = jnp.sum(grad_normed * standard_one, axis=0)
    grad_bias_one = jnp.sum(grad_normed, axis=0)
    grad_inputs = grad_middle + norm_back(grad_normed, norm1_gain, standard_one, factor_one)
    summed = lax.psum(
        (
            grad_gain_one,
            grad_bias_one,
            grad_query_weight,
            grad_key_weight,
            grad_value_weight,
            grad_taps,
            grad_coef,
            grad_rate,
            grad_skip,
            grad_out_weight,
            grad_gain_two,
            grad_bias_two,
            grad_up,
            grad_down,
        ),
        ("seq", "batch"),
    )
    return (token_order(mixed_out), token_order(grad_inputs)) + tuple(summed)


def solution(mesh):
    placed = (P("batch", "seq", None),) + (P(),) * 14 + (P("batch", "seq", None),)
    return jax.shard_map(
        on_device,
        mesh=mesh,
        in_specs=placed,
        out_specs=(P("batch", "seq", None),) * 2 + (P(),) * 14,
        check_vma=False,
    )
```

```python
import functools

import jax
import jax.numpy as jnp
from jax import lax
from jax.experimental import pallas as pl
from jax.experimental.pallas import tpu as pltpu
from jax.sharding import PartitionSpec as P

epsilon = 1e-05
CHUNKS = 16
GROUP = 8
LANES = 128


def passed_along(value, axis, steps):
    count = lax.axis_size(axis)
    leading, last = (max(0, -steps), min(count, count - steps))
    return lax.ppermute(value, axis, [(source, source + steps) for source in range(leading, last)])


def standardize(values):
    row_mean = jnp.mean(values, axis=-1, keepdims=True)
    centered = values - row_mean
    spread = jnp.mean(centered * centered, axis=-1, keepdims=True)
    factor = lax.rsqrt(spread + epsilon)
    return centered * factor, factor


def norm_back(grads, gain, standard, factor):
    scaled = grads * gain
    return factor * (
        scaled
        - jnp.mean(scaled, axis=-1, keepdims=True)
        - standard * jnp.mean(scaled * standard, axis=-1, keepdims=True)
    )


def project(rows_low, weight):
    return jnp.dot(rows_low, weight, preferred_element_type=jnp.float32)


def project_back(grads_low, weight):
    return lax.dot_general(
        grads_low, weight, (((1,), (1,)), ((), ())), preferred_element_type=jnp.float32
    )


def weight_grad(rows_low, grads_low):
    return lax.dot_general(
        rows_low, grads_low, (((0,), (0,)), ((), ())), preferred_element_type=jnp.float32
    )


def block(ref, place):
    return ref[place * CHUNKS : (place + 1) * CHUNKS, :]


def chunk_rows(chunk, states):
    return pl.ds(chunk, states, stride=CHUNKS)


def state_sums(width, rows_ref, decay_ref, out_ref, group, places, weight, lead):
    decay = decay_ref[pl.ds(group * GROUP, GROUP), :][:, None, :]
    running = jnp.zeros((GROUP, CHUNKS, LANES), jnp.float32)
    for place in places:
        rows = block(rows_ref, place)
        if weight is not None:
            rows = rows * weight(place)
        running = decay * (running + rows[None]) if lead else decay * running + rows[None]
    return running


def forward_states(width, rows_ref, rate_ref, sums_ref, last_ref, decay_ref):
    states = rate_ref.shape[0]
    decay_ref[...] = jnp.exp(-rate_ref[...])

    def body(group, unused):
        running = state_sums(width, rows_ref, decay_ref, None, group, range(width), None, False)
        sums_ref[pl.ds(group * GROUP * CHUNKS, GROUP * CHUNKS), :] = running.reshape(-1, LANES)
        return unused

    lax.fori_loop(0, states // GROUP, body, 0)
    hop = jnp.exp(-width * rate_ref[...])
    held = jnp.zeros((states, LANES), jnp.float32)
    for chunk in range(CHUNKS):
        held = hop * held + sums_ref[chunk_rows(chunk, states), :]
    last_ref[...] = held


def forward_mix(
    width,
    rows_ref,
    sums_ref,
    entering_ref,
    rate_ref,
    coef_ref,
    skip_ref,
    mixed_ref,
    held_ref,
    kernel_ref,
    decay_ref,
    taps_ref,
):
    states = rate_ref.shape[0]
    decay_ref[...] = jnp.exp(-rate_ref[...])
    hop = jnp.exp(-width * rate_ref[...])
    held = entering_ref[...]
    for chunk in range(CHUNKS):
        held_ref[chunk_rows(chunk, states), :] = held
        held = hop * held + sums_ref[chunk_rows(chunk, states), :]
    lags = lax.broadcasted_iota(jnp.int32, (8, LANES), 0).astype(jnp.float32)

    def add_state(state, totals):
        rate = rate_ref[pl.ds(state, 1), :]
        term = coef_ref[pl.ds(state, 1), :] * jnp.exp(-rate * lags)
        step = jnp.exp(-8.0 * rate)
        out = []
        for total in totals:
            out.append(total + term)
            term = term * step
        return tuple(out)

    totals = lax.fori_loop(
        0, states, add_state, tuple(jnp.zeros((8, LANES), jnp.float32) for _ in range(width // 8))
    )
    kernel_ref[...] = jnp.concatenate(totals, axis=0)
    for lag in range(width):
        taps_ref[lag * CHUNKS : (lag + 1) * CHUNKS, :] = jnp.broadcast_to(
            kernel_ref[lag : lag + 1, :], (CHUNKS, LANES)
        )
    for start in range(0, width, 4):
        sums = [skip_ref[...] * block(rows_ref, start + i) for i in range(4)]
        for place in range(start + 4):
            rows = block(rows_ref, place)
            for i in range(4):
                if start + i >= place:
                    sums[i] = sums[i] + block(taps_ref, start + i - place) * rows
        for i in range(4):
            mixed_ref[(start + i) * CHUNKS : (start + i + 1) * CHUNKS, :] = sums[i]

    def body(group, unused):
        decay = decay_ref[pl.ds(group * GROUP, GROUP), :][:, None, :]
        coef = coef_ref[pl.ds(group * GROUP, GROUP), :][:, None, :]
        term = held_ref[pl.ds(group * GROUP * CHUNKS, GROUP * CHUNKS), :].reshape(
            GROUP, CHUNKS, LANES
        )
        term = term * (coef * decay)
        for place in range(width):
            mixed_ref[place * CHUNKS : (place + 1) * CHUNKS, :] += jnp.sum(term, axis=0)
            if place < width - 1:
                term = term * decay
        return unused

    lax.fori_loop(0, states // GROUP, body, 0)


def backward_states(width, grads_ref, rate_ref, sums_ref, first_ref, decay_ref):
    states = rate_ref.shape[0]
    decay_ref[...] = jnp.exp(-rate_ref[...])

    def body(group, unused):
        running = state_sums(
            width, grads_ref, decay_ref, None, group, range(width - 1, -1, -1), None, True
        )
        sums_ref[pl.ds(group * GROUP * CHUNKS, GROUP * CHUNKS), :] = running.reshape(-1, LANES)
        return unused

    lax.fori_loop(0, states // GROUP, body, 0)
    hop = jnp.exp(-width * rate_ref[...])
    held = jnp.zeros((states, LANES), jnp.float32)
    for chunk in range(CHUNKS - 1, -1, -1):
        held = hop * held + sums_ref[chunk_rows(chunk, states), :]
    first_ref[...] = held


def backward_mix(
    width,
    grads_ref,
    rows_ref,
    sums_ref,
    held_ref,
    entering_ref,
    rate_ref,
    coef_ref,
    skip_ref,
    kernel_ref,
    back_ref,
    coef_grad_ref,
    rate_grad_ref,
    decay_ref,
    hop_ref,
    taps_ref,
    after_ref,
    lag_ref,
):
    states = rate_ref.shape[0]
    decay_ref[...] = jnp.exp(-rate_ref[...])
    hop = jnp.exp(-width * rate_ref[...])
    hop_ref[...] = hop
    held = entering_ref[...]
    for chunk in range(CHUNKS - 1, -1, -1):
        after_ref[chunk_rows(chunk, states), :] = held
        held = hop * held + sums_ref[chunk_rows(chunk, states), :]
    for lag in range(width):
        taps_ref[lag * CHUNKS : (lag + 1) * CHUNKS, :] = jnp.broadcast_to(
            kernel_ref[lag : lag + 1, :], (CHUNKS, LANES)
        )
    for start in range(0, width, 4):
        sums = [skip_ref[...] * block(grads_ref, start + i) for i in range(4)]
        for place in range(start, width):
            grads = block(grads_ref, place)
            for i in range(4):
                if place >= start + i:
                    sums[i] = sums[i] + block(taps_ref, place - start - i) * grads
        for i in range(4):
            back_ref[(start + i) * CHUNKS : (start + i + 1) * CHUNKS, :] = sums[i]
    for start in range(0, width, 4):
        sums = [jnp.zeros((CHUNKS, LANES), jnp.float32) for i in range(4)]
        for place in range(start, width):
            grads = block(grads_ref, place)
            for i in range(4):
                if place >= start + i:
                    sums[i] = sums[i] + block(rows_ref, place - start - i) * grads
        for i in range(4):
            lag_ref[start + i : start + i + 1, :] = jnp.sum(sums[i], axis=0, keepdims=True)
    decay_all = decay_ref[...]
    near_coef = jnp.zeros((states, LANES), jnp.float32)
    near_rate = jnp.zeros((states, LANES), jnp.float32)
    for lag in range(width - 1, -1, -1):
        near_coef = near_coef * decay_all + lag_ref[lag : lag + 1, :]
        near_rate = near_rate * decay_all + float(lag) * lag_ref[lag : lag + 1, :]
    coef_grad_ref[...] = near_coef
    rate_grad_ref[...] = near_rate

    def body(group, unused):
        members = pl.ds(group * GROUP, GROUP)
        cells = pl.ds(group * GROUP * CHUNKS, GROUP * CHUNKS)
        cube = (GROUP, CHUNKS, LANES)
        decay = decay_ref[members, :][:, None, :]
        coef = coef_ref[members, :][:, None, :]
        after = after_ref[cells, :].reshape(cube)
        term = after * coef
        for place in range(width - 1, -1, -1):
            back_ref[place * CHUNKS : (place + 1) * CHUNKS, :] += jnp.sum(term, axis=0)
            if place > 0:
                term = term * decay
        held = held_ref[cells, :].reshape(cube)
        coef_grad_ref[members, :] += jnp.sum(held * sums_ref[cells, :].reshape(cube), axis=1)
        slope = state_sums(
            width,
            rows_ref,
            decay_ref,
            None,
            group,
            range(width),
            lambda place: float(width - 1 - place),
            False,
        )
        total = after * (float(width) * hop_ref[members, :][:, None, :] * held + slope)
        slope = state_sums(
            width,
            grads_ref,
            decay_ref,
            None,
            group,
            range(width - 1, -1, -1),
            lambda place: float(place + 1),
            True,
        )
        total = total + held * slope
        rate_grad_ref[members, :] += jnp.sum(total, axis=1)
        return unused

    lax.fori_loop(0, states // GROUP, body, 0)
    rate_grad_ref[...] = -coef_ref[...] * rate_grad_ref[...]


def per_lanes(body, out_rows, scratch, *arrays):
    channels = arrays[0].shape[1]
    scratch = [pltpu.VMEM((rows, LANES), jnp.float32) for rows in scratch]
    return pl.pallas_call(
        body,
        grid=(channels // LANES,),
        in_specs=[pl.BlockSpec((array.shape[0], LANES), lambda i: (0, i)) for array in arrays],
        out_specs=[pl.BlockSpec((rows, LANES), lambda i: (0, i)) for rows in out_rows],
        out_shape=[jax.ShapeDtypeStruct((rows, channels), jnp.float32) for rows in out_rows],
        scratch_shapes=scratch,
        compiler_params=pltpu.CompilerParams(vmem_limit_bytes=40 * 2**20),
    )(*arrays)


def carried(own, rate, row_count, forward):
    count = lax.axis_size("seq")
    place = lax.axis_index("seq")
    every = lax.all_gather(own, "seq", axis=0)
    source = jnp.arange(count)
    hops = place - 1 - source if forward else source - 1 - place
    decays = jnp.exp(-rate[None] * (row_count * jnp.maximum(hops, 0)).astype(jnp.float32)[:, None, None])
    return jnp.sum(jnp.where(hops[:, None, None] >= 0, every * decays, 0.0), axis=0)


MESH = pl.DeviceIdType.MESH


def add_rows(out_ref, out_start, a_ref, a_start, b_ref, b_start, rows):
    columns = out_ref.shape[1]
    size = 8
    for option in (16, 24, 32, 48, 64):
        if rows % option == 0 and option * columns <= 64 * 1024:
            size = option

    def body(i, unused):
        at = i * size
        out_ref[pl.ds(pl.multiple_of(out_start + at, 8), size), :] = (
            a_ref[pl.ds(pl.multiple_of(a_start + at, 8), size), :]
            + b_ref[pl.ds(pl.multiple_of(b_start + at, 8), size), :]
        )
        return unused

    lax.fori_loop(0, rows // size, body, 0)


class Lane:
    def __init__(self, array, start, rows, columns, bits, line_first):
        self.array, self.start, self.rows, self.columns = array, start, rows, columns
        self.bits, self.line_first = bits, line_first

    def buffers(self, line):
        half = self.rows // 2
        unit = half // line if self.line_first else half >> len(self.bits)
        counts = [half, half]
        size = half // line if self.line_first else half
        for unused in self.bits:
            size //= 2
            counts.append(size)
        counts.append(unit * (line + 1 if self.line_first else max(1, line // 2)))
        return [pltpu.VMEM((count, self.columns), jnp.float32) for count in counts]

    def copies(self, line):
        chain = 4 * line + 1 if self.line_first else line
        return 4 + 2 * len(self.bits) + chain


def lane_steps(lane, line, source, target, buffers, send_sems, recv_sems, first_sem, pending):
    acc, fin = buffers[:2]
    landing = buffers[2 : 2 + len(lane.bits)]
    chain = buffers[-1]
    me = lax.axis_index("seq")
    z = lax.axis_index("batch")
    half = lane.rows // 2
    core = me % 2
    counter = [first_sem]

    def fresh():
        counter[0] += 1
        return counter[0] - 1

    def remote(src, dst, index, device):
        return pltpu.make_async_remote_copy(
            src_ref=src,
            dst_ref=dst,
            send_sem=send_sems.at[index],
            recv_sem=recv_sems.at[index],
            device_id=device,
            device_id_type=MESH,
        )

    def rows_of(ref, start, count):
        if not isinstance(start, int):
            start = pl.multiple_of(start, 8)
        return ref.at[pl.ds(start, count), :]

    def side(bit):
        return (me // bit) % 2

    def partner(bit):
        return (me + bit * (1 - 2 * side(bit)), z)

    mine = lane.start + core * half
    other = lane.start + (1 - core) * half
    load_index, swap_index = fresh(), fresh()
    load = pltpu.make_async_copy(rows_of(source, mine, half), acc, recv_sems.at[load_index])
    swap = remote(rows_of(source, other, half), fin, swap_index, partner(1))

    def begin():
        load.start()
        swap.start()

    def add_swap():
        load.wait()
        swap.wait_recv()
        add_rows(acc, 0, acc, 0, fin, 0, half)

    pending.append(swap.wait_send)
    steps = [[begin], [add_swap]]

    def join(function):
        steps[-1].append(function)

    def step(function):
        steps.append([function])

    def neighbours_sum(base, size, final):
        starts = [base]
        for place, bit in enumerate(lane.bits):
            size //= 2
            start = starts[-1]
            copy = remote(
                rows_of(acc, start + (1 - side(bit)) * size, size),
                landing[place],
                fresh(),
                partner(bit),
            )
            own = start + side(bit) * size
            last = place == len(lane.bits) - 1
            join(copy.start)
            pending.append(copy.wait_send)

            def receive(copy=copy, own=own, size=size, place=place, last=last):
                copy.wait_recv()
                add_rows(fin if final and last else acc, own, acc, own, landing[place], 0, size)

            step(receive)
            starts.append(own)
        return starts, size

    def neighbours_spread(starts, size):
        for place in range(len(lane.bits) - 1, -1, -1):
            bit = lane.bits[place]
            start = starts[place + 1]
            copy = remote(
                rows_of(fin, start, size), rows_of(fin, start, size), fresh(), partner(bit)
            )
            join(copy.start)
            pending.append(copy.wait_send)
            step(copy.wait_recv)
            size *= 2

    if not lane.line_first:
        starts, size = neighbours_sum(0, half, False)
        at = starts[-1]
        depth = jnp.minimum(z, line - 1 - z)
        lower = z < line // 2
        inward = (me, jnp.where(lower, z + 1, z - 1))
        outward = (me, jnp.where(lower, z - 1, z + 1))
        across = (me, line - 1 - z)
        middle = line // 2 - 1

        def on(level, function):
            def guarded():
                pl.when(depth == level)(function)

            return guarded

        for level in range(middle):
            copy = remote(
                rows_of(acc, at, size), rows_of(chain, level * size, size), fresh(), inward
            )
            join(on(level, copy.start))
            pending.append(on(level, copy.wait_send))

            def receive(copy=copy, level=level):
                copy.wait_recv()
                add_rows(acc, at, acc, at, chain, level * size, size)

            step(on(level + 1, receive))
        copy = remote(rows_of(acc, at, size), rows_of(chain, middle * size, size), fresh(), across)
        join(on(middle, copy.start))
        pending.append(on(middle, copy.wait_send))

        def receive_across(copy=copy):
            copy.wait_recv()
            add_rows(fin, at, acc, at, chain, middle * size, size)

        step(on(middle, receive_across))
        for level in range(middle - 1, -1, -1):
            copy = remote(rows_of(fin, at, size), rows_of(fin, at, size), fresh(), outward)
            join(on(level + 1, copy.start))
            pending.append(on(level + 1, copy.wait_send))
            step(on(level, copy.wait_recv))
        neighbours_spread(starts, size)
    else:
        unit = half // line
        slots = [fresh() for unused in range(line + 1)]
        outs = [[fresh() for unused in range(2)] for unused in range(line)]
        spreads = [fresh() for unused in range(line)]

        def on(place, function):
            def guarded():
                pl.when(z == place)(function)

            return guarded

        def beside(place):
            return (me, place - 1 if place > 0 else place + 1)

        def hop(place, member, step_to):
            slot = line if step_to < 0 and member == place - 1 else member
            return remote(
                rows_of(acc, member * unit, unit),
                rows_of(chain, slot * unit, unit),
                slots[slot],
                (me, place + step_to),
            )

        def arrived(place, slot, member):
            remote(
                rows_of(acc, member * unit, unit),
                rows_of(chain, slot * unit, unit),
                slots[slot],
                beside(place),
            ).wait_recv()
            add_rows(acc, member * unit, acc, member * unit, chain, slot * unit, unit)

        for turn in range(line - 1):

            def rightward(place=turn):
                for member in range(line - 1, place, -1):
                    if place > 0:
                        arrived(place, member, member)
                    hop(place, member, 1).start()

            def leftward(place=line - 1 - turn):
                for member in range(place):
                    if place < line - 1:
                        arrived(place, member, member)
                    hop(place, member, -1).start()

            if turn > 0:
                step(on(turn, rightward))
            else:
                join(on(turn, rightward))
            join(on(line - 1 - turn, leftward))

        def collect(place):
            if place > 0:
                arrived(place, place, place)
            if place < line - 1:
                arrived(place, line, place)

        def collect_all():
            for place in range(line):
                on(place, functools.partial(collect, place))()

        step(collect_all)

        def sent(place):
            for member in range(line - 1, place, -1):
                hop(place, member, 1).wait_send()
            for member in range(place):
                hop(place, member, -1).wait_send()

        for place in range(line):
            pending.append(on(place, functools.partial(sent, place)))
        base = z * unit
        starts, size = neighbours_sum(base, unit, True)
        neighbours_spread(starts, size)

        def spread_at(place, distance, receive, send):
            members = {place - distance, place + distance}
            for member in sorted(members):
                if not 0 <= member < line:
                    continue
                if receive and distance > 0:
                    remote(
                        rows_of(fin, member * unit, unit),
                        rows_of(fin, member * unit, unit),
                        spreads[member],
                        beside(place),
                    ).wait_recv()
                if not send:
                    continue
                for step_to in (1, -1):
                    going = member <= place if step_to > 0 else member >= place
                    if going and 0 <= place + step_to < line:
                        yield member, step_to

        def pass_on(place, member, step_to):
            return pltpu.make_async_remote_copy(
                src_ref=rows_of(fin, member * unit, unit),
                dst_ref=rows_of(fin, member * unit, unit),
                send_sem=send_sems.at[outs[member][0 if step_to > 0 else 1]],
                recv_sem=recv_sems.at[spreads[member]],
                device_id=(me, place + step_to),
                device_id_type=MESH,
            )

        for distance in range(line):

            def forward(place, distance):
                for member, step_to in spread_at(place, distance, True, True):
                    pass_on(place, member, step_to).start()

            def forward_all(distance=distance):
                for place in range(line):
                    on(place, functools.partial(forward, place, distance))()

            if distance == 0:
                join(forward_all)
            else:
                step(forward_all)

        def passed(place):
            for distance in range(line):
                for member, step_to in spread_at(place, distance, False, True):
                    pass_on(place, member, step_to).wait_send()

        for place in range(line):
            pending.append(on(place, functools.partial(passed, place)))

    keep_index, give_index = fresh(), fresh()
    keep = pltpu.make_async_copy(fin, rows_of(target, mine, half), recv_sems.at[keep_index])
    give = remote(fin, rows_of(target, mine, half), give_index, partner(1))
    join(keep.start)
    join(give.start)
    pending.append(keep.wait)
    pending.append(give.wait)
    assert counter[0] - first_sem <= lane.copies(line)
    return steps


def turn_order(lengths, order):
    if [order.count(place) for place in range(len(lengths))] == lengths:
        return order
    turns = range(max(lengths))
    return [place for turn in turns for place, length in enumerate(lengths) if turn < length]


def all_sum_body(count, line, bits, lanes, order, *refs):
    sources, targets = refs[:count], refs[count : 2 * count]
    send_sems, recv_sems = refs[-2:]
    buffers = list(refs[2 * count : -2])
    me = lax.axis_index("seq")
    z = lax.axis_index("batch")
    barrier = pltpu.get_barrier_semaphore()
    for bit in bits:
        pl.semaphore_signal(
            barrier,
            inc=1,
            device_id=(me + bit * (1 - 2 * ((me // bit) % 2)), z),
            device_id_type=MESH,
        )

    @pl.when(z > 0)
    def left():
        pl.semaphore_signal(barrier, inc=1, device_id=(me, z - 1), device_id_type=MESH)

    @pl.when(z < line - 1)
    def right():
        pl.semaphore_signal(barrier, inc=1, device_id=(me, z + 1), device_id_type=MESH)

    pl.semaphore_wait(
        barrier, len(bits) + jnp.where(z > 0, 1, 0) + jnp.where(z < line - 1, 1, 0)
    )
    pending = []
    programs = []
    first = 0
    for lane in lanes:
        own = [buffers.pop(0) for unused in lane.buffers(line)]
        programs.append(
            lane_steps(
                lane,
                line,
                sources[lane.array],
                targets[lane.array],
                own,
                send_sems,
                recv_sems,
                first,
                pending,
            )
        )
        first += lane.copies(line)
    for place in turn_order([len(program) for program in programs], order):
        for function in programs[place].pop(0):
            function()
    for wait in pending:
        wait()


def all_sum(arrays, plan, order):
    size, line = lax.axis_size("seq"), lax.axis_size("batch")
    bits = [1 << place for place in range(size.bit_length() - 1)]
    lanes = []
    for index, array in enumerate(arrays):
        rows = array.shape[0] // len(plan[index])
        for piece, (flipped, line_first) in enumerate(plan[index]):
            if rows % (8 * size * line):
                line_first = False
            path = bits[:0:-1] if flipped else bits[1:]
            lanes.append(Lane(index, piece * rows, rows, array.shape[1], path, line_first))
    scratch = [buffer for lane in lanes for buffer in lane.buffers(line)]
    copies = sum(lane.copies(line) for lane in lanes)
    return pl.pallas_call(
        functools.partial(all_sum_body, len(arrays), line, bits, lanes, order),
        out_shape=[jax.ShapeDtypeStruct(array.shape, jnp.float32) for array in arrays],
        in_specs=[pl.BlockSpec(memory_space=pltpu.HBM)] * len(arrays),
        out_specs=[pl.BlockSpec(memory_space=pltpu.HBM)] * len(arrays),
        scratch_shapes=scratch
        + [pltpu.SemaphoreType.DMA((copies,)), pltpu.SemaphoreType.DMA((copies,))],
        compiler_params=pltpu.CompilerParams(
            collective_id=0, has_side_effects=True, vmem_limit_bytes=62 * 2**20
        ),
    )(*arrays)


PLAN = [
    [(False, True), (False, False), (False, True), (False, False)],
    [(False, False), (True, False), (True, False)],
    [(False, False)],
    [(True, False)],
    [(True, False)],
    [(False, True)],
    [(False, False)],
]
ORDER = [
    11, 1, 0, 5, 7, 4, 2, 10, 9, 3, 6, 8, 11, 1, 0, 11, 5, 11, 7, 4, 2, 10, 1, 9, 0, 3, 6, 8, 5,
    11, 0, 7, 1, 0, 11, 11, 2, 2, 9, 4, 2, 10, 3, 10, 6, 10, 5, 0, 1, 8, 9, 1, 5, 2, 7, 11, 9,
    1, 6, 5, 4, 10, 7, 9, 3, 8, 0, 5, 2, 6, 11, 7, 9, 1, 10, 4, 5, 0, 6, 2, 7, 10, 3, 9, 4, 6,
    8, 3, 4, 1, 5, 8, 0, 3, 2, 7, 10, 8, 6, 0, 9, 2, 4, 7, 10, 3, 8, 0, 2, 10, 6, 4, 0, 2, 8, 3,
    10,
]


def on_device(
    tokens,
    norm1_gain,
    norm1_bias,
    query_weight,
    key_weight,
    value_weight,
    shift_taps,
    ssm_coef,
    ssm_rate,
    ssm_skip,
    out_weight,
    norm2_gain,
    norm2_bias,
    up_weight,
    down_weight,
    out_grad,
):
    unused, row_count, channels = tokens.shape
    width = row_count // CHUNKS
    states = ssm_rate.shape[0]
    tap_count = shift_taps.shape[0]
    halo = tap_count - 1

    def mixed_order(values):
        return values.reshape(CHUNKS, width, channels).swapaxes(0, 1).reshape(row_count, channels)

    def token_order(values):
        return values.reshape(width, CHUNKS, channels).swapaxes(0, 1).reshape(1, row_count, channels)

    low = jnp.bfloat16
    inputs = mixed_order(tokens).astype(jnp.float32)
    out_grad = mixed_order(out_grad)
    standard_one, factor_one = standardize(inputs)
    normed_low = (standard_one * norm1_gain + norm1_bias).astype(low)
    key_rows = project(normed_low, key_weight)
    key_blocks = key_rows.reshape(width, CHUNKS, channels)
    before = passed_along(key_blocks[width - halo :, CHUNKS - 1], "seq", 1)
    value_rows = project(normed_low, value_weight)
    queries = project(normed_low, query_weight)
    head = jnp.concatenate([before[:, None], key_blocks[width - halo :, : CHUNKS - 1]], axis=1)
    extended = jnp.concatenate([head.reshape(halo * CHUNKS, channels), key_rows], 0)

    def delayed(offset):
        start = (halo - offset) * CHUNKS
        return extended[start : start + row_count]

    keys_mixed = sum(shift_taps[offset] * delayed(offset) for offset in range(tap_count))
    product = keys_mixed * value_rows
    skip_row = ssm_skip[None]
    cells = states * CHUNKS
    sums, last = per_lanes(
        functools.partial(forward_states, width), [cells, states], [states], product, ssm_rate
    )
    entering = carried(last, ssm_rate, row_count, True)
    mixed_rows, held, kernel = per_lanes(
        functools.partial(forward_mix, width),
        [row_count, cells, width],
        [states, row_count],
        product,
        sums,
        entering,
        ssm_rate,
        ssm_coef,
        skip_row,
    )
    gated_rows = (queries * mixed_rows).astype(low)
    middle = inputs + project(gated_rows, out_weight)
    standard_two, factor_two = standardize(middle)
    normed_two_low = (standard_two * norm2_gain + norm2_bias).astype(low)
    hidden_pre = project(normed_two_low, up_weight)
    activated, gelu_pull = jax.vjp(jax.nn.gelu, hidden_pre)
    activated_low = activated.astype(low)
    mixed_out = (middle + project(activated_low, down_weight)).astype(low)
    grad_down = weight_grad(activated_low, out_grad)
    grad_hidden = gelu_pull(project_back(out_grad, down_weight))[0].astype(low)
    grad_up = weight_grad(normed_two_low, grad_hidden)
    grad_normed_two = project_back(grad_hidden, up_weight)
    grad_gain_two = jnp.sum(grad_normed_two * standard_two, axis=0)
    grad_bias_two = jnp.sum(grad_normed_two, axis=0)
    grad_middle = out_grad.astype(jnp.float32) + norm_back(
        grad_normed_two, norm2_gain, standard_two, factor_two
    )
    grad_attended = grad_middle.astype(low)
    grad_out_weight = weight_grad(gated_rows, grad_attended)
    grad_gated = project_back(grad_attended, out_weight)
    grad_queries = (grad_gated * mixed_rows).astype(low)
    grad_mixed = grad_gated * queries
    grad_skip = jnp.sum(grad_mixed * product, axis=0)
    grad_sums, first = per_lanes(
        functools.partial(backward_states, width), [cells, states], [states], grad_mixed, ssm_rate
    )
    grad_entering = carried(first, ssm_rate, row_count, False)
    grad_product, grad_coef, grad_rate = per_lanes(
        functools.partial(backward_mix, width),
        [row_count, states, states],
        [states, states, row_count, cells, width],
        grad_mixed,
        product,
        grad_sums,
        held,
        grad_entering,
        ssm_rate,
        ssm_coef,
        skip_row,
        kernel,
    )
    grad_keys_mixed = grad_product * value_rows
    grad_values = (grad_product * keys_mixed).astype(low)
    grad_blocks = grad_keys_mixed.reshape(width, CHUNKS, channels)
    after = passed_along(grad_blocks[:halo, 0], "seq", -1)
    tail = jnp.concatenate([grad_blocks[:halo, 1:], after[:, None]], axis=1)
    grad_extended = jnp.concatenate([grad_keys_mixed, tail.reshape(halo * CHUNKS, channels)], 0)
    grad_keys = sum(
        shift_taps[offset] * grad_extended[offset * CHUNKS : offset * CHUNKS + row_count]
        for offset in range(tap_count)
    ).astype(low)
    grad_taps = jnp.stack(
        [jnp.sum(grad_keys_mixed * delayed(offset), axis=0) for offset in range(tap_count)]
    )
    grad_query_weight = weight_grad(normed_low, grad_queries)
    grad_key_weight = weight_grad(normed_low, grad_keys)
    grad_value_weight = weight_grad(normed_low, grad_values)
    grad_normed = (
        project_back(grad_queries, query_weight)
        + project_back(grad_keys, key_weight)
        + project_back(grad_values, value_weight)
    )
    grad_gain_one = jnp.sum(grad_normed * standard_one, axis=0)
    grad_bias_one = jnp.sum(grad_normed, axis=0)
    grad_inputs = grad_middle + norm_back(grad_normed, norm1_gain, standard_one, factor_one)
    small = jnp.concatenate(
        [
            grad_gain_one[None],
            grad_bias_one[None],
            grad_taps,
            grad_coef,
            grad_rate,
            grad_skip[None],
            grad_gain_two[None],
            grad_bias_two[None],
        ],
        axis=0,
    )
    small_rows = small.shape[0]
    unit = 8 * lax.axis_size("seq")
    small = jnp.pad(small, ((0, -small_rows % unit), (0, 0)))
    (
        grad_down,
        grad_up,
        grad_query_weight,
        grad_key_weight,
        grad_value_weight,
        grad_out_weight,
        small,
    ) = all_sum(
        [
            grad_down,
            grad_up,
            grad_query_weight,
            grad_key_weight,
            grad_value_weight,
            grad_out_weight,
            small,
        ],
        PLAN,
        ORDER,
    )
    first = 2 + tap_count
    second = first + 2 * states
    return (
        token_order(mixed_out),
        token_order(grad_inputs),
        small[0],
        small[1],
        grad_query_weight,
        grad_key_weight,
        grad_value_weight,
        small[2:first],
        small[first : first + states],
        small[first + states : second],
        small[second],
        grad_out_weight,
        small[second + 1],
        small[second + 2],
        grad_up,
        grad_down,
    )


def solution(mesh):
    placed = (P("batch", "seq", None),) + (P(),) * 14 + (P("batch", "seq", None),)
    return jax.shard_map(
        on_device,
        mesh=mesh,
        in_specs=placed,
        out_specs=(P("batch", "seq", None),) * 2 + (P(),) * 14,
        check_vma=False,
    )
```

```python
import functools

import jax
import jax.numpy as jnp
from jax import lax
from jax.experimental import pallas as pl
from jax.experimental.pallas import tpu as pltpu
from jax.sharding import PartitionSpec as P

epsilon = 1e-05
CHUNKS = 16
GROUP = 8
LANES = 128


def passed_along(value, axis, steps):
    count = lax.axis_size(axis)
    leading, last = (max(0, -steps), min(count, count - steps))
    return lax.ppermute(value, axis, [(source, source + steps) for source in range(leading, last)])


def standardize(values):
    row_mean = jnp.mean(values, axis=-1, keepdims=True)
    centered = values - row_mean
    spread = jnp.mean(centered * centered, axis=-1, keepdims=True)
    factor = lax.rsqrt(spread + epsilon)
    return centered * factor, factor


def norm_back(grads, gain, standard, factor):
    scaled = grads * gain
    return factor * (
        scaled
        - jnp.mean(scaled, axis=-1, keepdims=True)
        - standard * jnp.mean(scaled * standard, axis=-1, keepdims=True)
    )


def project(rows_low, weight):
    return jnp.dot(rows_low, weight, preferred_element_type=jnp.float32)


def project_back(grads_low, weight):
    return lax.dot_general(
        grads_low, weight, (((1,), (1,)), ((), ())), preferred_element_type=jnp.float32
    )


def weight_grad(rows_low, grads_low):
    return lax.dot_general(
        rows_low, grads_low, (((0,), (0,)), ((), ())), preferred_element_type=jnp.float32
    )


def block(ref, place):
    return ref[place * CHUNKS : (place + 1) * CHUNKS, :]


def chunk_rows(chunk, states):
    return pl.ds(chunk, states, stride=CHUNKS)


def state_sums(width, rows_ref, decay_ref, out_ref, group, places, weight, lead):
    decay = decay_ref[pl.ds(group * GROUP, GROUP), :][:, None, :]
    running = jnp.zeros((GROUP, CHUNKS, LANES), jnp.float32)
    for place in places:
        rows = block(rows_ref, place)
        if weight is not None:
            rows = rows * weight(place)
        running = decay * (running + rows[None]) if lead else decay * running + rows[None]
    return running


def forward_states(width, rows_ref, rate_ref, sums_ref, last_ref, decay_ref):
    states = rate_ref.shape[0]
    decay_ref[...] = jnp.exp(-rate_ref[...])

    def body(group, unused):
        running = state_sums(width, rows_ref, decay_ref, None, group, range(width), None, False)
        sums_ref[pl.ds(group * GROUP * CHUNKS, GROUP * CHUNKS), :] = running.reshape(-1, LANES)
        return unused

    lax.fori_loop(0, states // GROUP, body, 0)
    hop = jnp.exp(-width * rate_ref[...])
    held = jnp.zeros((states, LANES), jnp.float32)
    for chunk in range(CHUNKS):
        held = hop * held + sums_ref[chunk_rows(chunk, states), :]
    last_ref[...] = held


def forward_near(
    width, rows_ref, rate_ref, coef_ref, skip_ref, mixed_ref, kernel_ref, taps_ref
):
    states = rate_ref.shape[0]
    lags = lax.broadcasted_iota(jnp.int32, (8, LANES), 0).astype(jnp.float32)

    def add_states(group, totals):
        members = pl.ds(pl.multiple_of(group * GROUP, GROUP), GROUP)
        rates, coefs = rate_ref[members, :], coef_ref[members, :]
        steps = jnp.exp(-8.0 * rates)
        totals = list(totals)
        for i in range(GROUP):
            term = coefs[i : i + 1] * jnp.exp(-rates[i : i + 1] * lags)
            for place in range(width // 8):
                totals[place] = totals[place] + term
                term = term * steps[i : i + 1]
        return tuple(totals)

    zero = jnp.zeros((8, LANES), jnp.float32)
    totals = lax.fori_loop(0, states // GROUP, add_states, (zero,) * (width // 8))
    kernel_ref[...] = jnp.concatenate(totals, axis=0)
    for lag in range(width):
        taps_ref[lag * CHUNKS : (lag + 1) * CHUNKS, :] = jnp.broadcast_to(
            kernel_ref[lag : lag + 1, :], (CHUNKS, LANES)
        )
    for start in range(0, width, 4):
        sums = [skip_ref[...] * block(rows_ref, start + i) for i in range(4)]
        for place in range(start + 4):
            rows = block(rows_ref, place)
            for i in range(4):
                if start + i >= place:
                    sums[i] = sums[i] + block(taps_ref, start + i - place) * rows
        for i in range(4):
            mixed_ref[(start + i) * CHUNKS : (start + i + 1) * CHUNKS, :] = sums[i]


def forward_far(
    width, sums_ref, entering_ref, rate_ref, coef_ref, mixed_ref, held_ref, decay_ref
):
    states = rate_ref.shape[0]
    decay_ref[...] = jnp.exp(-rate_ref[...])
    hop = jnp.exp(-width * rate_ref[...])
    held = entering_ref[...]
    for chunk in range(CHUNKS):
        held_ref[chunk_rows(chunk, states), :] = held
        held = hop * held + sums_ref[chunk_rows(chunk, states), :]

    def body(group, unused):
        decay = decay_ref[pl.ds(group * GROUP, GROUP), :][:, None, :]
        coef = coef_ref[pl.ds(group * GROUP, GROUP), :][:, None, :]
        term = held_ref[pl.ds(group * GROUP * CHUNKS, GROUP * CHUNKS), :].reshape(
            GROUP, CHUNKS, LANES
        )
        term = term * (coef * decay)
        for place in range(width):
            mixed_ref[place * CHUNKS : (place + 1) * CHUNKS, :] += jnp.sum(term, axis=0)
            if place < width - 1:
                term = term * decay
        return unused

    lax.fori_loop(0, states // GROUP, body, 0)


def backward_states(width, grads_ref, rate_ref, sums_ref, first_ref, decay_ref):
    states = rate_ref.shape[0]
    decay_ref[...] = jnp.exp(-rate_ref[...])

    def body(group, unused):
        running = state_sums(
            width, grads_ref, decay_ref, None, group, range(width - 1, -1, -1), None, True
        )
        sums_ref[pl.ds(group * GROUP * CHUNKS, GROUP * CHUNKS), :] = running.reshape(-1, LANES)
        return unused

    lax.fori_loop(0, states // GROUP, body, 0)
    hop = jnp.exp(-width * rate_ref[...])
    held = jnp.zeros((states, LANES), jnp.float32)
    for chunk in range(CHUNKS - 1, -1, -1):
        held = hop * held + sums_ref[chunk_rows(chunk, states), :]
    first_ref[...] = held


def backward_near(
    width,
    grads_ref,
    rows_ref,
    sums_ref,
    entering_ref,
    rate_ref,
    skip_ref,
    kernel_ref,
    back_ref,
    coef_grad_ref,
    rate_grad_ref,
    decay_ref,
    hop_ref,
    taps_ref,
    after_ref,
    lag_ref,
):
    states = rate_ref.shape[0]
    hop = jnp.exp(-width * rate_ref[...])
    hop_ref[...] = hop
    held = entering_ref[...]
    for chunk in range(CHUNKS - 1, -1, -1):
        after_ref[chunk_rows(chunk, states), :] = held
        held = hop * held + sums_ref[chunk_rows(chunk, states), :]
    for lag in range(width):
        taps_ref[lag * CHUNKS : (lag + 1) * CHUNKS, :] = jnp.broadcast_to(
            kernel_ref[lag : lag + 1, :], (CHUNKS, LANES)
        )
    for start in range(0, width, 4):
        sums = [skip_ref[...] * block(grads_ref, start + i) for i in range(4)]
        for place in range(start, width):
            grads = block(grads_ref, place)
            for i in range(4):
                if place >= start + i:
                    sums[i] = sums[i] + block(taps_ref, place - start - i) * grads
        for i in range(4):
            back_ref[(start + i) * CHUNKS : (start + i + 1) * CHUNKS, :] = sums[i]
    for start in range(0, width, 4):
        sums = [jnp.zeros((CHUNKS, LANES), jnp.float32) for i in range(4)]
        for place in range(start, width):
            grads = block(grads_ref, place)
            for i in range(4):
                if place >= start + i:
                    sums[i] = sums[i] + block(rows_ref, place - start - i) * grads
        for i in range(4):
            lag_ref[start + i : start + i + 1, :] = jnp.sum(sums[i], axis=0, keepdims=True)
    decay_all = decay_ref[...]
    near_coef = jnp.zeros((states, LANES), jnp.float32)
    near_rate = jnp.zeros((states, LANES), jnp.float32)
    for lag in range(width - 1, -1, -1):
        near_coef = near_coef * decay_all + lag_ref[lag : lag + 1, :]
        near_rate = near_rate * decay_all + float(lag) * lag_ref[lag : lag + 1, :]
    coef_grad_ref[...] = near_coef
    rate_grad_ref[...] = near_rate


def backward_far(
    width,
    grads_ref,
    rows_ref,
    sums_ref,
    held_ref,
    coef_ref,
    back_ref,
    coef_grad_ref,
    rate_grad_ref,
    decay_ref,
    hop_ref,
    after_ref,
    groups,
):
    def body(group, unused):
        members = pl.ds(group * GROUP, GROUP)
        cells = pl.ds(group * GROUP * CHUNKS, GROUP * CHUNKS)
        cube = (GROUP, CHUNKS, LANES)
        decay = decay_ref[members, :][:, None, :]
        coef = coef_ref[members, :][:, None, :]
        after = after_ref[cells, :].reshape(cube)
        term = after * coef
        for place in range(width - 1, -1, -1):
            back_ref[place * CHUNKS : (place + 1) * CHUNKS, :] += jnp.sum(term, axis=0)
            if place > 0:
                term = term * decay
        held = held_ref[cells, :].reshape(cube)
        coef_grad_ref[members, :] += jnp.sum(held * sums_ref[cells, :].reshape(cube), axis=1)
        slope = state_sums(
            width,
            rows_ref,
            decay_ref,
            None,
            group,
            range(width),
            lambda place: float(width - 1 - place),
            False,
        )
        total = after * (float(width) * hop_ref[members, :][:, None, :] * held + slope)
        slope = state_sums(
            width,
            grads_ref,
            decay_ref,
            None,
            group,
            range(width - 1, -1, -1),
            lambda place: float(place + 1),
            True,
        )
        total = total + held * slope
        rate_grad_ref[members, :] += jnp.sum(total, axis=1)
        return unused

    lax.fori_loop(groups.start, groups.stop, body, 0)


MESH = pl.DeviceIdType.MESH


def add_rows(out_ref, out_start, a_ref, a_start, b_ref, b_start, rows):
    columns = out_ref.shape[1]
    size = 8
    for option in (16, 24, 32, 48, 64):
        if rows % option == 0 and option * columns <= 64 * 1024:
            size = option

    def body(i, unused):
        at = i * size
        out_ref[pl.ds(pl.multiple_of(out_start + at, 8), size), :] = (
            a_ref[pl.ds(pl.multiple_of(a_start + at, 8), size), :]
            + b_ref[pl.ds(pl.multiple_of(b_start + at, 8), size), :]
        )
        return unused

    lax.fori_loop(0, rows // size, body, 0)


class Lane:
    def __init__(self, array, start, rows, columns, bits, line_first, in_place):
        self.array, self.start, self.rows, self.columns = array, start, rows, columns
        self.bits, self.line_first, self.in_place = bits, line_first, in_place

    def buffers(self, line):
        half = self.rows // 2
        unit = half // line if self.line_first else half >> len(self.bits)
        counts = [half] if self.in_place else [half, half]
        size = half // line if self.line_first else half
        for unused in self.bits:
            size //= 2
            counts.append(size)
        counts.append(unit * (line + 1 if self.line_first else max(1, line // 2)))
        return [pltpu.VMEM((count, self.columns), jnp.float32) for count in counts]

    def copies(self, line):
        chain = 4 * line + 1 if self.line_first else line
        return 4 + 2 * len(self.bits) + chain


def lane_steps(lane, line, source, target, buffers, send_sems, recv_sems, first_sem, pending):
    if lane.in_place:
        buffers = [source] + buffers
    acc, fin = buffers[:2]
    landing = buffers[2 : 2 + len(lane.bits)]
    chain = buffers[-1]
    me = lax.axis_index("seq")
    z = lax.axis_index("batch")
    half = lane.rows // 2
    core = me % 2
    counter = [first_sem]

    def fresh():
        counter[0] += 1
        return counter[0] - 1

    def remote(src, dst, index, device):
        return pltpu.make_async_remote_copy(
            src_ref=src,
            dst_ref=dst,
            send_sem=send_sems.at[index],
            recv_sem=recv_sems.at[index],
            device_id=device,
            device_id_type=MESH,
        )

    def rows_of(ref, start, count):
        if not isinstance(start, int):
            start = pl.multiple_of(start, 8)
        return ref.at[pl.ds(start, count), :]

    def side(bit):
        return (me // bit) % 2

    def partner(bit):
        return (me + bit * (1 - 2 * side(bit)), z)

    mine = lane.start + core * half
    other = lane.start + (1 - core) * half
    base_row = mine if lane.in_place else 0
    swap = remote(rows_of(source, other, half), fin, fresh(), partner(1))
    if lane.in_place:
        begin = swap.start

        def add_swap():
            swap.wait_recv()
            add_rows(acc, mine, acc, mine, fin, 0, half)

    else:
        load = pltpu.make_async_copy(rows_of(source, mine, half), acc, recv_sems.at[fresh()])

        def begin():
            load.start()
            swap.start()

        def add_swap():
            load.wait()
            swap.wait_recv()
            add_rows(acc, 0, acc, 0, fin, 0, half)

    pending.append(swap.wait_send)
    steps = [[begin], [add_swap]]

    def join(function):
        steps[-1].append(function)

    def step(function):
        steps.append([function])

    def neighbours_sum(base, size, final):
        starts = [base]
        for place, bit in enumerate(lane.bits):
            size //= 2
            start = starts[-1]
            copy = remote(
                rows_of(acc, base_row + start + (1 - side(bit)) * size, size),
                landing[place],
                fresh(),
                partner(bit),
            )
            own = start + side(bit) * size
            last = place == len(lane.bits) - 1
            join(copy.start)
            pending.append(copy.wait_send)

            def receive(copy=copy, own=own, size=size, place=place, last=last):
                copy.wait_recv()
                out, out_row = (fin, own) if final and last else (acc, base_row + own)
                add_rows(out, out_row, acc, base_row + own, landing[place], 0, size)

            step(receive)
            starts.append(own)
        return starts, size

    def neighbours_spread(starts, size):
        for place in range(len(lane.bits) - 1, -1, -1):
            bit = lane.bits[place]
            start = starts[place + 1]
            copy = remote(
                rows_of(fin, start, size), rows_of(fin, start, size), fresh(), partner(bit)
            )
            join(copy.start)
            pending.append(copy.wait_send)
            step(copy.wait_recv)
            size *= 2

    if not lane.line_first:
        starts, size = neighbours_sum(0, half, False)
        at = starts[-1]
        depth = jnp.minimum(z, line - 1 - z)
        lower = z < line // 2
        inward = (me, jnp.where(lower, z + 1, z - 1))
        outward = (me, jnp.where(lower, z - 1, z + 1))
        across = (me, line - 1 - z)
        middle = line // 2 - 1

        def on(level, function):
            def guarded():
                pl.when(depth == level)(function)

            return guarded

        for level in range(middle):
            copy = remote(
                rows_of(acc, base_row + at, size), rows_of(chain, level * size, size), fresh(), inward
            )
            join(on(level, copy.start))
            pending.append(on(level, copy.wait_send))

            def receive(copy=copy, level=level):
                copy.wait_recv()
                add_rows(acc, base_row + at, acc, base_row + at, chain, level * size, size)

            step(on(level + 1, receive))
        copy = remote(rows_of(acc, base_row + at, size), rows_of(chain, middle * size, size), fresh(), across)
        join(on(middle, copy.start))
        pending.append(on(middle, copy.wait_send))

        def receive_across(copy=copy):
            copy.wait_recv()
            add_rows(fin, at, acc, base_row + at, chain, middle * size, size)

        step(on(middle, receive_across))
        for level in range(middle - 1, -1, -1):
            copy = remote(rows_of(fin, at, size), rows_of(fin, at, size), fresh(), outward)
            join(on(level + 1, copy.start))
            pending.append(on(level + 1, copy.wait_send))
            step(on(level, copy.wait_recv))
        neighbours_spread(starts, size)
    else:
        unit = half // line
        slots = [fresh() for unused in range(line + 1)]
        outs = [[fresh() for unused in range(2)] for unused in range(line)]
        spreads = [fresh() for unused in range(line)]

        def on(place, function):
            def guarded():
                pl.when(z == place)(function)

            return guarded

        def beside(place):
            return (me, place - 1 if place > 0 else place + 1)

        def hop(place, member, step_to):
            slot = line if step_to < 0 and member == place - 1 else member
            return remote(
                rows_of(acc, base_row + member * unit, unit),
                rows_of(chain, slot * unit, unit),
                slots[slot],
                (me, place + step_to),
            )

        def arrived(place, slot, member):
            remote(
                rows_of(acc, base_row + member * unit, unit),
                rows_of(chain, slot * unit, unit),
                slots[slot],
                beside(place),
            ).wait_recv()
            row = base_row + member * unit
            add_rows(acc, row, acc, row, chain, slot * unit, unit)

        for turn in range(line - 1):

            def rightward(place=turn):
                for member in range(line - 1, place, -1):
                    if place > 0:
                        arrived(place, member, member)
                    hop(place, member, 1).start()

            def leftward(place=line - 1 - turn):
                for member in range(place):
                    if place < line - 1:
                        arrived(place, member, member)
                    hop(place, member, -1).start()

            if turn > 0:
                step(on(turn, rightward))
            else:
                join(on(turn, rightward))
            join(on(line - 1 - turn, leftward))

        def collect(place):
            if place > 0:
                arrived(place, place, place)
            if place < line - 1:
                arrived(place, line, place)

        def collect_all():
            for place in range(line):
                on(place, functools.partial(collect, place))()

        step(collect_all)

        def sent(place):
            for member in range(line - 1, place, -1):
                hop(place, member, 1).wait_send()
            for member in range(place):
                hop(place, member, -1).wait_send()

        for place in range(line):
            pending.append(on(place, functools.partial(sent, place)))
        base = z * unit
        starts, size = neighbours_sum(base, unit, True)
        neighbours_spread(starts, size)

        def spread_at(place, distance, receive, send):
            members = {place - distance, place + distance}
            for member in sorted(members):
                if not 0 <= member < line:
                    continue
                if receive and distance > 0:
                    remote(
                        rows_of(fin, member * unit, unit),
                        rows_of(fin, member * unit, unit),
                        spreads[member],
                        beside(place),
                    ).wait_recv()
                if not send:
                    continue
                for step_to in (1, -1):
                    going = member <= place if step_to > 0 else member >= place
                    if going and 0 <= place + step_to < line:
                        yield member, step_to

        def pass_on(place, member, step_to):
            return pltpu.make_async_remote_copy(
                src_ref=rows_of(fin, member * unit, unit),
                dst_ref=rows_of(fin, member * unit, unit),
                send_sem=send_sems.at[outs[member][0 if step_to > 0 else 1]],
                recv_sem=recv_sems.at[spreads[member]],
                device_id=(me, place + step_to),
                device_id_type=MESH,
            )

        for distance in range(line):

            def forward(place, distance):
                for member, step_to in spread_at(place, distance, True, True):
                    pass_on(place, member, step_to).start()

            def forward_all(distance=distance):
                for place in range(line):
                    on(place, functools.partial(forward, place, distance))()

            if distance == 0:
                join(forward_all)
            else:
                step(forward_all)

        def passed(place):
            for distance in range(line):
                for member, step_to in spread_at(place, distance, False, True):
                    pass_on(place, member, step_to).wait_send()

        for place in range(line):
            pending.append(on(place, functools.partial(passed, place)))

    keep_index, give_index = fresh(), fresh()
    keep = pltpu.make_async_copy(fin, rows_of(target, mine, half), recv_sems.at[keep_index])
    give = remote(fin, rows_of(target, mine, half), give_index, partner(1))
    join(keep.start)
    join(give.start)
    pending.append(keep.wait)
    pending.append(give.wait)
    assert counter[0] - first_sem <= lane.copies(line)
    return steps


def turn_order(lengths, order):
    if [order.count(place) for place in range(len(lengths))] == lengths:
        return order
    last = len(lengths) - 1
    turns = range(max(lengths[:-1], default=0))
    lanes = [place for turn in turns for place in range(last) if turn < lengths[place]]
    return [last] * lengths[last] + lanes


class Loop:
    def __init__(self, count, *parts):
        self.count, self.parts = count, parts

    def steps(self):
        return self.count * len(self.parts)


def call_all(functions):
    for function in functions:
        function()


def run_loop(loop, between):
    parts = len(loop.parts)

    def body(i, unused):
        for place, part in enumerate(loop.parts):
            part(i)
            for turn in range(loop.count):
                functions = between[turn * parts + place]
                if functions:
                    pl.when(i == turn)(functools.partial(call_all, functions))
        return unused

    lax.fori_loop(0, loop.count, body, 0)


def run_programs(programs, work, order):
    lengths = [len(program) for program in programs]
    lengths.append(sum(item.steps() if isinstance(item, Loop) else 1 for item in work))
    order = turn_order(lengths, order)
    programs, work = [list(program) for program in programs], list(work)
    last = len(programs)
    at = 0
    while at < len(order):
        if order[at] != last:
            call_all(programs[order[at]].pop(0))
            at += 1
            continue
        item = work.pop(0)
        at += 1
        if not isinstance(item, Loop):
            item()
            continue
        between = [[]]
        while len(between) < item.steps():
            if order[at] == last:
                between.append([])
            else:
                between[-1] += programs[order[at]].pop(0)
            at += 1
        run_loop(item, between + [[]])


def state_exchange(bits, row_count, rate, totals, arrivals, entering, sends, receives, forward):
    me, z = lax.axis_index("seq"), lax.axis_index("batch")

    def copy(level):
        bit = bits[level]
        return pltpu.make_async_remote_copy(
            src_ref=totals[level],
            dst_ref=arrivals[level],
            send_sem=sends.at[level],
            recv_sem=receives.at[level],
            device_id=(me + bit * (1 - 2 * ((me // bit) % 2)), z),
            device_id_type=MESH,
        )

    def arrive(level):
        bit = bits[level]
        copy(level).wait_recv()
        place = me % bit
        after = (me // bit) % 2 == (1 if forward else 0)
        hops = (row_count * (place if forward else bit - 1 - place)).astype(jnp.float32)
        term = jnp.exp(-rate[...] * hops) * arrivals[level][...]
        term = jnp.where(after, term, 0.0)
        entering[...] = term if level == 0 else entering[...] + term
        if level + 1 < len(bits):
            far = jnp.exp(-float(row_count * bit) * rate[...])
            ours, theirs = totals[level][...], arrivals[level][...]
            totals[level + 1][...] = jnp.where(after, ours + far * theirs, theirs + far * ours)
            copy(level + 1).start()

    return copy, arrive


def forward_body(row_count, bits, *refs):
    width = row_count // CHUNKS
    product, rate, coef, skip, mixed, held, kernel, sums, taps, decay, entering = refs[:11]
    levels = len(bits)
    totals, arrivals = refs[11 : 11 + levels], refs[11 + levels : 11 + 2 * levels]
    sends, receives = refs[-2:]
    tiles = product.shape[1] // LANES
    me, z = lax.axis_index("seq"), lax.axis_index("batch")
    barrier = pltpu.get_barrier_semaphore()
    for bit in bits:
        pl.semaphore_signal(
            barrier,
            inc=1,
            device_id=(me + bit * (1 - 2 * ((me // bit) % 2)), z),
            device_id_type=MESH,
        )
    pl.semaphore_wait(barrier, levels)
    copy, arrive = state_exchange(
        bits, row_count, rate, totals, arrivals, entering, sends, receives, True
    )

    def columns(tile):
        return pl.ds(pl.multiple_of(tile * LANES, LANES), LANES)

    def states_tile(tile):
        here = columns(tile)
        forward_states(
            width, product.at[:, here], rate.at[:, here], sums.at[tile], totals[0].at[:, here], decay
        )

    def near_tile(tile):
        here = columns(tile)
        forward_near(
            width,
            product.at[:, here],
            rate.at[:, here],
            coef.at[:, here],
            skip.at[:, here],
            mixed.at[:, here],
            kernel.at[:, here],
            taps,
        )

    def far_tile(tile):
        here = columns(tile)
        forward_far(
            width,
            sums.at[tile],
            entering.at[:, here],
            rate.at[:, here],
            coef.at[:, here],
            mixed.at[:, here],
            held.at[tile],
            decay,
        )

    run_loop(Loop(tiles, states_tile), [[] for unused in range(tiles)])
    copy(0).start()
    between = [[] for unused in range(tiles)]
    for level in range(levels):
        between[(level + 1) * tiles // levels - 1].append(functools.partial(arrive, level))
    run_loop(Loop(tiles, near_tile), between)
    run_loop(Loop(tiles, far_tile), [[] for unused in range(tiles)])
    for level in range(levels):
        copy(level).wait_send()


def forward_mixing(row_count, product, rate, coef, skip):
    size = lax.axis_size("seq")
    bits = [1 << place for place in range(size.bit_length() - 1)]
    states, channels = rate.shape
    tiles, width = channels // LANES, row_count // CHUNKS
    whole = pl.BlockSpec(memory_space=pltpu.VMEM)
    scratch = [(tiles, states * CHUNKS, LANES), (row_count, LANES), (states, LANES)]
    scratch += [(states, channels)] * (1 + 2 * len(bits))
    shapes = [(row_count, channels), (tiles, states * CHUNKS, LANES), (width, channels)]
    return pl.pallas_call(
        functools.partial(forward_body, row_count, bits),
        out_shape=[jax.ShapeDtypeStruct(shape, jnp.float32) for shape in shapes],
        in_specs=[whole] * 4,
        out_specs=[whole] * 3,
        scratch_shapes=[pltpu.VMEM(shape, jnp.float32) for shape in scratch]
        + [pltpu.SemaphoreType.DMA((len(bits),))] * 2,
        compiler_params=pltpu.CompilerParams(
            collective_id=1, has_side_effects=True, vmem_limit_bytes=40 * 2**20
        ),
    )(product, rate, coef, skip)


NAMES = ["down", "up", "out", "grad_mixed", "product", "held", "values", "keys_mixed", "key_rows"]
NAMES += ["standard", "factor", "grad_middle", "query_weight", "key_weight", "value_weight"]
RESIDENT = ["rate", "coef", "skip", "taps", "kernel", "gain", "normed_turned", "grad_queries"]
RESIDENT += ["small"]
ROWS_AT_ONCE = 64


def backward_body(row_count, size, line, bits, lanes, order, *refs):
    width = row_count // CHUNKS
    counts = [len(NAMES) + len(RESIDENT), 8]
    given = dict(zip(NAMES + RESIDENT, refs[: counts[0]]))
    results = refs[counts[0] : sum(counts)]
    rest = list(refs[sum(counts) :])
    send_sems, recv_sems, load_sems, swap_send, swap_recv = rest[-5:]
    rest = rest[:-5]

    def take(count):
        taken = rest[:count]
        del rest[:count]
        return taken

    (grad_query, grad_value, grad_key, small) = take(4)
    (lanes_g, lanes_x, lanes_back, lanes_taps, lanes_other) = take(5)
    (lanes_held, lanes_sums, lanes_after) = take(3)
    (decay, hop, lag, first) = take(4)
    (grad_keys_mixed, values_low, keys_low, weight, entering) = take(5)
    (block_a, block_b, block_c, block_f, edge_out, edge_in) = take(6)
    levels = len(bits)
    totals, arrivals = take(levels), take(levels)

    me = lax.axis_index("seq")
    z = lax.axis_index("batch")
    channels = small.shape[1]
    tiles = channels // LANES
    rate, coef = given["rate"], given["coef"]
    states = rate.shape[0]
    tap_count = given["taps"].shape[0]
    halo = tap_count - 1

    barrier = pltpu.get_barrier_semaphore()

    def greet(device):
        pl.semaphore_signal(barrier, inc=1, device_id=device, device_id_type=MESH)

    for bit in bits:
        greet((me + bit * (1 - 2 * ((me // bit) % 2)), z))
    pl.when(z > 0)(lambda: greet((me, z - 1)))
    pl.when(z < line - 1)(lambda: greet((me, z + 1)))
    pl.when(me > 0)(lambda: greet((me - 1, z)))
    pl.when(me < size - 1)(lambda: greet((me + 1, z)))
    pl.semaphore_wait(
        barrier,
        len(bits)
        + jnp.where(z > 0, 1, 0)
        + jnp.where(z < line - 1, 1, 0)
        + jnp.where(me > 0, 1, 0)
        + jnp.where(me < size - 1, 1, 0),
    )

    def columns(tile):
        return pl.ds(pl.multiple_of(tile * LANES, LANES), LANES)

    def fetch(*pairs):
        copies = [
            pltpu.make_async_copy(source, target, load_sems.at[i])
            for i, (source, target) in enumerate(pairs)
        ]
        for copy in copies:
            copy.start()
        for copy in copies:
            copy.wait()

    exchange, arrive = state_exchange(
        bits, row_count, rate, totals, arrivals, entering, swap_send, swap_recv, False
    )

    def states_of(tile, target):
        backward_states(width, lanes_g, rate.at[:, columns(tile)], lanes_sums, target, decay)

    def first_tile(tile):
        fetch((given["grad_mixed"].at[:, columns(tile)], lanes_g))
        states_of(tile, totals[0].at[:, columns(tile)])

    def weight_sum(target, grads):
        def body(i):
            rows = pl.ds(pl.multiple_of(i * 256, 256), 256)
            target[rows, :] = jnp.dot(
                given["normed_turned"][rows, :], grads[...], preferred_element_type=jnp.float32
            )

        return Loop(channels // 256, body)

    def second_fetch(tile):
        here = columns(tile)
        fetch(
            (given["grad_mixed"].at[:, here], lanes_g),
            (given["product"].at[:, here], lanes_x),
            (given["held"].at[tile], lanes_held),
            (given["values"].at[:, here], lanes_other.at[:row_count]),
        )
        states_of(tile, first)

    def second_near(tile):
        here = columns(tile)
        backward_near(
            width,
            lanes_g,
            lanes_x,
            lanes_sums,
            entering.at[:, here],
            rate.at[:, here],
            given["skip"].at[:, here],
            given["kernel"].at[:, here],
            lanes_back,
            small.at[0:states, here],
            small.at[states : 2 * states, here],
            decay,
            hop,
            lanes_taps,
            lanes_after,
            lag,
        )

    def second_far(half):
        def part(tile):
            here = columns(tile)
            groups = states // GROUP // 2
            backward_far(
                width,
                lanes_g,
                lanes_x,
                lanes_sums,
                lanes_held,
                coef.at[:, here],
                lanes_back,
                small.at[0:states, here],
                small.at[states : 2 * states, here],
                decay,
                hop,
                lanes_after,
                range(half * groups, (half + 1) * groups),
            )

        return part

    def second_end(tile):
        here = columns(tile)
        row = 2 * states + tap_count
        small[row : row + 1, here] = jnp.sum(lanes_g[...] * lanes_x[...], axis=0, keepdims=True)
        small[states : 2 * states, here] = -coef[:, here] * small[states : 2 * states, here]
        grad_keys_mixed[0:row_count, here] = lanes_back[...] * lanes_other[0:row_count, :]
        fetch((given["keys_mixed"].at[:, here], lanes_x))
        values_low[:, here] = (lanes_back[...] * lanes_x[...]).astype(jnp.bfloat16)

    def send_edge():
        edge_out[...] = jnp.zeros(edge_out.shape, jnp.float32)
        for place in range(halo):
            edge_out[place : place + 1, :] = grad_keys_mixed[place * CHUNKS : place * CHUNKS + 1, :]
        pl.when(me > 0)(edge(me - 1).start)

        @pl.when(me == size - 1)
        def at_end():
            edge_in[...] = jnp.zeros(edge_in.shape, jnp.float32)

    def edge(device):
        return pltpu.make_async_remote_copy(
            src_ref=edge_out,
            dst_ref=edge_in,
            send_sem=swap_send.at[levels],
            recv_sem=swap_recv.at[levels],
            device_id=(device, z),
            device_id_type=MESH,
        )

    def keys_tile(tile):
        here = columns(tile)
        fetch((given["key_rows"].at[:, here], lanes_other))
        for place in range(halo):
            rows = grad_keys_mixed[place * CHUNKS : (place + 1) * CHUNKS, here]
            start = row_count + place * CHUNKS
            grad_keys_mixed[start : start + CHUNKS, here] = jnp.concatenate(
                [rows[1:], edge_in[place : place + 1, here]], axis=0
            )
        tap = given["taps"]
        total = tap[0:1, here] * grad_keys_mixed[0:row_count, here]
        for offset in range(1, tap_count):
            start = offset * CHUNKS
            total = total + tap[offset : offset + 1, here] * (
                grad_keys_mixed[start : start + row_count, here]
            )
        keys_low[:, here] = total.astype(jnp.bfloat16)
        grads = grad_keys_mixed[0:row_count, here]
        for offset in range(tap_count):
            start = (halo - offset) * CHUNKS
            row = 2 * states + offset
            small[row : row + 1, here] = jnp.sum(
                grads * lanes_other[start : start + row_count, :], axis=0, keepdims=True
            )

    back = grad_keys_mixed

    def back_sum(index, grads):
        def body(i):
            rows = pl.ds(pl.multiple_of(i * 128, 128), 128)
            term = lax.dot_general(
                grads[rows, :],
                weight[...],
                (((1,), (1,)), ((), ())),
                preferred_element_type=jnp.float32,
            )
            back[rows, :] = term if index == 0 else back[rows, :] + term

        return Loop(row_count // 128, body)

    def norm_rows(i):
        rows = pl.ds(pl.multiple_of(i * ROWS_AT_ONCE, ROWS_AT_ONCE), ROWS_AT_ONCE)
        fetch(
            (given["standard"].at[rows, :], block_a),
            (given["grad_middle"].at[rows, :], block_b),
            (given["factor"].at[rows, :], block_f),
        )
        grads, standard = back[rows, :], block_a[...]
        block_c[...] = block_b[...] + norm_back(grads, given["gain"][...], standard, block_f[:, 0:1])
        fetch((block_c, results[7].at[rows, :]))
        row = 2 * states + tap_count + 1
        small[row : row + 1, :] += jnp.sum(grads * standard, axis=0, keepdims=True)
        small[row + 1 : row + 2, :] += jnp.sum(grads, axis=0, keepdims=True)

    def begin():
        small[...] = given["small"][...]

    work = [begin, Loop(tiles, first_tile), exchange(0).start]
    work.append(weight_sum(grad_query, given["grad_queries"]))
    for level in range(levels):
        work.append(functools.partial(arrive, level))
    parts = (second_fetch, second_near, second_far(0), second_far(1), second_end)
    work.append(Loop(tiles, *parts))
    work.append(send_edge)
    work.append(weight_sum(grad_value, values_low))
    work.append(lambda: pl.when(me < size - 1)(edge(me + 1).wait_recv))
    work.append(Loop(tiles, keys_tile))
    work.append(weight_sum(grad_key, keys_low))
    chain = (
        (given["query_weight"], given["grad_queries"]),
        (given["key_weight"], keys_low),
        (given["value_weight"], values_low),
    )
    for index, (source, grads) in enumerate(chain):
        work.append(functools.partial(fetch, (source, weight)))
        work.append(back_sum(index, grads))
    work.append(Loop(row_count // ROWS_AT_ONCE, norm_rows))

    sources = [given["down"], given["up"], given["out"], grad_query, grad_value, grad_key, small]
    pending = [exchange(level).wait_send for level in range(levels)]
    pending.append(lambda: pl.when(me > 0)(edge(me - 1).wait_send))
    programs = []
    start = 0
    for lane in lanes:
        programs.append(
            lane_steps(
                lane,
                line,
                sources[lane.array],
                results[lane.array],
                take(len(lane.buffers(line))),
                send_sems,
                recv_sems,
                start,
                pending,
            )
        )
        start += lane.copies(line)
    run_programs(programs, work, order)
    for wait in pending:
        wait()


def backward(row_count, arrays, resident, plan, order):
    size, line = lax.axis_size("seq"), lax.axis_size("batch")
    bits = [1 << place for place in range(size.bit_length() - 1)]
    channels = arrays["down"].shape[1]
    states = resident["rate"].shape[0]
    cells = states * CHUNKS
    small_rows = resident["small"].shape[0]
    square = (channels, channels)
    shapes = [arrays["down"].shape, arrays["up"].shape] + [square] * 4 + [(small_rows, channels)]
    lanes = []
    for index, shape in enumerate(shapes):
        rows = shape[0] // len(plan[index])
        for piece, (flipped, line_first) in enumerate(plan[index]):
            if rows % (8 * size * line):
                line_first = False
            path = bits[:0:-1] if flipped else bits[1:]
            lanes.append(Lane(index, piece * rows, rows, shape[1], path, line_first, index > 2))
    key_rows = arrays["key_rows"].shape[0]
    width = row_count // CHUNKS
    full, low = jnp.float32, jnp.bfloat16
    scratch = [(square, full)] * 3 + [((small_rows, channels), full)]
    scratch += [((row_count, LANES), full)] * 4 + [((key_rows, LANES), full)]
    scratch += [((cells, LANES), full)] * 3
    scratch += [((states, LANES), full)] * 2 + [((width, LANES), full), ((states, LANES), full)]
    scratch += [((key_rows, channels), full), ((row_count, channels), low)]
    scratch += [((row_count, channels), low), (square, low), ((states, channels), full)]
    scratch += [((ROWS_AT_ONCE, channels), full)] * 3 + [((ROWS_AT_ONCE, LANES), full)]
    scratch += [((8, channels), full)] * 2
    scratch += [((states, channels), full)] * (2 * len(bits))
    scratch = [pltpu.VMEM(shape, kind) for shape, kind in scratch]
    scratch += [buffer for lane in lanes for buffer in lane.buffers(line)]
    copies = sum(lane.copies(line) for lane in lanes)
    scratch += [pltpu.SemaphoreType.DMA((count,)) for count in (copies, copies, 8)]
    scratch += [pltpu.SemaphoreType.DMA((len(bits) + 1,))] * 2
    shapes.append((row_count, channels))
    return pl.pallas_call(
        functools.partial(backward_body, row_count, size, line, bits, lanes, order),
        out_shape=[jax.ShapeDtypeStruct(shape, full) for shape in shapes],
        in_specs=[pl.BlockSpec(memory_space=pltpu.HBM)] * len(NAMES)
        + [pl.BlockSpec(memory_space=pltpu.VMEM)] * len(RESIDENT),
        out_specs=[pl.BlockSpec(memory_space=pltpu.HBM)] * len(shapes),
        scratch_shapes=scratch,
        compiler_params=pltpu.CompilerParams(
            collective_id=0, has_side_effects=True, vmem_limit_bytes=VMEM_LIMIT
        ),
    )(*[arrays[name] for name in NAMES], *[resident[name] for name in RESIDENT])


VMEM_LIMIT = 64 * 2**20


PLAN = [
    [(False, False), (True, False), (False, False), (False, False)],
    [(True, False), (True, True), (False, True)],
    [(False, False)],
    [(False, False)],
    [(True, True)],
    [(True, False)],
    [(True, False)],
]
ORDER = [
    0, 4, 5, 1, 3, 7, 6, 2, 12, 0, 12, 4, 12, 5, 1, 12, 3, 7, 12, 0, 6, 2, 12, 12, 12, 12, 4,
    12, 12, 8, 12, 5, 3, 8, 1, 5, 7, 0, 5, 3, 6, 2, 7, 6, 5, 4, 2, 12, 0, 6, 12, 12, 0, 3, 12,
    12, 8, 7, 12, 12, 12, 0, 3, 1, 12, 5, 8, 4, 12, 12, 7, 12, 6, 12, 0, 5, 3, 2, 12, 6, 12, 4,
    12, 5, 7, 12, 1, 12, 12, 2, 12, 8, 3, 12, 0, 4, 6, 12, 12, 12, 12, 7, 12, 5, 12, 12, 1, 3,
    12, 2, 12, 12, 8, 12, 12, 12, 12, 12, 4, 9, 2, 12, 12, 12, 12, 9, 5, 6, 12, 12, 12, 12, 1,
    12, 12, 10, 12, 12, 12, 12, 10, 12, 8, 12, 12, 12, 7, 12, 12, 4, 9, 12, 12, 12, 12, 12, 5,
    12, 12, 9, 12, 12, 2, 12, 10, 12, 6, 12, 12, 11, 8, 1, 9, 11, 10, 6, 10, 1, 6, 9, 8, 10, 9,
    11, 9, 11, 11, 9, 10, 11, 10, 9, 11, 11, 9, 10, 9, 11,
]


def on_device(
    tokens,
    norm1_gain,
    norm1_bias,
    query_weight,
    key_weight,
    value_weight,
    shift_taps,
    ssm_coef,
    ssm_rate,
    ssm_skip,
    out_weight,
    norm2_gain,
    norm2_bias,
    up_weight,
    down_weight,
    out_grad,
):
    unused, row_count, channels = tokens.shape
    width = row_count // CHUNKS
    states = ssm_rate.shape[0]
    tap_count = shift_taps.shape[0]
    halo = tap_count - 1

    def mixed_order(values):
        return values.reshape(CHUNKS, width, channels).swapaxes(0, 1).reshape(row_count, channels)

    def token_order(values):
        return values.reshape(width, CHUNKS, channels).swapaxes(0, 1).reshape(1, row_count, channels)

    low = jnp.bfloat16
    inputs = mixed_order(tokens).astype(jnp.float32)
    out_grad = mixed_order(out_grad)
    standard_one, factor_one = standardize(inputs)
    normed_low = (standard_one * norm1_gain + norm1_bias).astype(low)
    key_rows = project(normed_low, key_weight)
    key_blocks = key_rows.reshape(width, CHUNKS, channels)
    before = passed_along(key_blocks[width - halo :, CHUNKS - 1], "seq", 1)
    value_rows = project(normed_low, value_weight)
    queries = project(normed_low, query_weight)
    head = jnp.concatenate([before[:, None], key_blocks[width - halo :, : CHUNKS - 1]], axis=1)
    extended = jnp.concatenate([head.reshape(halo * CHUNKS, channels), key_rows], 0)

    def delayed(offset):
        start = (halo - offset) * CHUNKS
        return extended[start : start + row_count]

    keys_mixed = sum(shift_taps[offset] * delayed(offset) for offset in range(tap_count))
    product = keys_mixed * value_rows
    skip_row = ssm_skip[None]
    mixed_rows, held, kernel = forward_mixing(row_count, product, ssm_rate, ssm_coef, skip_row)
    gated_rows = (queries * mixed_rows).astype(low)
    middle = inputs + project(gated_rows, out_weight)
    standard_two, factor_two = standardize(middle)
    normed_two_low = (standard_two * norm2_gain + norm2_bias).astype(low)
    hidden_pre = project(normed_two_low, up_weight)
    activated, gelu_pull = jax.vjp(jax.nn.gelu, hidden_pre)
    activated_low = activated.astype(low)
    mixed_out = (middle + project(activated_low, down_weight)).astype(low)
    grad_down = weight_grad(activated_low, out_grad)
    grad_hidden = gelu_pull(project_back(out_grad, down_weight))[0].astype(low)
    grad_up = weight_grad(normed_two_low, grad_hidden)
    grad_normed_two = project_back(grad_hidden, up_weight)
    grad_gain_two = jnp.sum(grad_normed_two * standard_two, axis=0)
    grad_bias_two = jnp.sum(grad_normed_two, axis=0)
    grad_middle = out_grad.astype(jnp.float32) + norm_back(
        grad_normed_two, norm2_gain, standard_two, factor_two
    )
    grad_attended = grad_middle.astype(low)
    grad_out_weight = weight_grad(gated_rows, grad_attended)
    grad_gated = project_back(grad_attended, out_weight)
    grad_queries = (grad_gated * mixed_rows).astype(low)
    grad_mixed = grad_gated * queries
    misc = 2 * states
    last_rows = jnp.stack(
        [
            jnp.sum(grad_normed_two * standard_two, axis=0),
            jnp.sum(grad_normed_two, axis=0),
        ]
    )
    lead = misc + tap_count + 3
    unit = 8 * lax.axis_size("seq")
    small = jnp.pad(last_rows, ((lead, -(lead + 2) % unit), (0, 0)))
    (
        grad_down,
        grad_up,
        grad_out_weight,
        grad_query_weight,
        grad_value_weight,
        grad_key_weight,
        small,
        grad_inputs,
    ) = backward(
        row_count,
        dict(
            down=grad_down,
            up=grad_up,
            out=grad_out_weight,
            grad_mixed=grad_mixed,
            product=product,
            held=held,
            values=value_rows,
            keys_mixed=keys_mixed,
            key_rows=extended,
            standard=standard_one,
            factor=jnp.broadcast_to(factor_one, (row_count, LANES)),
            grad_middle=grad_middle,
            query_weight=query_weight,
            key_weight=key_weight,
            value_weight=value_weight,
        ),
        dict(
            rate=ssm_rate,
            coef=ssm_coef,
            skip=skip_row,
            taps=shift_taps,
            kernel=kernel,
            gain=norm1_gain[None],
            normed_turned=normed_low.T,
            grad_queries=grad_queries,
            small=small,
        ),
        PLAN,
        ORDER,
    )
    return (
        token_order(mixed_out),
        token_order(grad_inputs),
        small[lead - 2],
        small[lead - 1],
        grad_query_weight,
        grad_key_weight,
        grad_value_weight,
        small[misc : misc + tap_count],
        small[:states],
        small[states:misc],
        small[misc + tap_count],
        grad_out_weight,
        small[lead],
        small[lead + 1],
        grad_up,
        grad_down,
    )


def solution(mesh):
    placed = (P("batch", "seq", None),) + (P(),) * 14 + (P("batch", "seq", None),)
    return jax.shard_map(
        on_device,
        mesh=mesh,
        in_specs=placed,
        out_specs=(P("batch", "seq", None),) * 2 + (P(),) * 14,
        check_vma=False,
    )
```

```python
import functools
import math
from types import SimpleNamespace
from typing import Any, NamedTuple

import jax
import jax.numpy as jnp
from jax import lax
from jax.experimental import pallas as pl
from jax.experimental.pallas import tpu as pltpu
from jax.sharding import PartitionSpec as P

epsilon = 1e-05
CHUNKS = 16
GROUP = 8
LANES = 128

VMEM_LIMIT = 64 * 2**20
ROWS_AT_ONCE = 64


def standardize(values):
    row_mean = jnp.mean(values, axis=-1, keepdims=True)
    centered = values - row_mean
    spread = jnp.mean(centered * centered, axis=-1, keepdims=True)
    factor = lax.rsqrt(spread + epsilon)
    return centered * factor, factor


def norm_back(grads, gain, standard, factor):
    scaled = grads * gain
    return factor * (
        scaled
        - jnp.mean(scaled, axis=-1, keepdims=True)
        - standard * jnp.mean(scaled * standard, axis=-1, keepdims=True)
    )


def project_back(grads_low, weight):
    return lax.dot_general(
        grads_low, weight, (((1,), (1,)), ((), ())), preferred_element_type=jnp.float32
    )


def weight_grad(rows_low, grads_low):
    return lax.dot_general(
        rows_low, grads_low, (((0,), (0,)), ((), ())), preferred_element_type=jnp.float32
    )


def block(ref, place):
    return ref[place * CHUNKS : (place + 1) * CHUNKS, :]


def chunk_rows(chunk, states):
    return pl.ds(chunk, states, stride=CHUNKS)


def state_sums(width, rows_ref, decay_ref, out_ref, group, places, weight, lead):
    decay = decay_ref[pl.ds(group * GROUP, GROUP), :][:, None, :]
    running = jnp.zeros((GROUP, CHUNKS, LANES), jnp.float32)
    for place in places:
        rows = block(rows_ref, place)
        if weight is not None:
            rows = rows * weight(place)
        running = decay * (running + rows[None]) if lead else decay * running + rows[None]
    return running


def forward_states(width, rows_ref, rate_ref, sums_ref, last_ref, decay_ref):
    states = rate_ref.shape[0]
    decay_ref[...] = jnp.exp(-rate_ref[...])

    def body(group, unused):
        running = state_sums(width, rows_ref, decay_ref, None, group, range(width), None, False)
        sums_ref[pl.ds(group * GROUP * CHUNKS, GROUP * CHUNKS), :] = running.reshape(-1, LANES)
        return unused

    lax.fori_loop(0, states // GROUP, body, 0)
    hop = jnp.exp(-width * rate_ref[...])
    held = jnp.zeros((states, LANES), jnp.float32)
    for chunk in range(CHUNKS):
        held = hop * held + sums_ref[chunk_rows(chunk, states), :]
    last_ref[...] = held


def forward_near(
    width, rows_ref, rate_ref, coef_ref, skip_ref, mixed_ref, kernel_ref, taps_ref
):
    states = rate_ref.shape[0]
    lags = lax.broadcasted_iota(jnp.int32, (8, LANES), 0).astype(jnp.float32)

    def add_states(group, totals):
        members = pl.ds(pl.multiple_of(group * GROUP, GROUP), GROUP)
        rates, coefs = rate_ref[members, :], coef_ref[members, :]
        steps = jnp.exp(-8.0 * rates)
        totals = list(totals)
        for i in range(GROUP):
            term = coefs[i : i + 1] * jnp.exp(-rates[i : i + 1] * lags)
            for place in range(width // 8):
                totals[place] = totals[place] + term
                term = term * steps[i : i + 1]
        return tuple(totals)

    zero = jnp.zeros((8, LANES), jnp.float32)
    totals = lax.fori_loop(0, states // GROUP, add_states, (zero,) * (width // 8))
    kernel_ref[...] = jnp.concatenate(totals, axis=0)
    for lag in range(width):
        taps_ref[lag * CHUNKS : (lag + 1) * CHUNKS, :] = jnp.broadcast_to(
            kernel_ref[lag : lag + 1, :], (CHUNKS, LANES)
        )
    for start in range(0, width, 4):
        sums = [skip_ref[...] * block(rows_ref, start + i) for i in range(4)]
        for place in range(start + 4):
            rows = block(rows_ref, place)
            for i in range(4):
                if start + i >= place:
                    sums[i] = sums[i] + block(taps_ref, start + i - place) * rows
        for i in range(4):
            mixed_ref[(start + i) * CHUNKS : (start + i + 1) * CHUNKS, :] = sums[i]


def forward_far(
    width, sums_ref, entering_ref, rate_ref, coef_ref, mixed_ref, held_ref, decay_ref
):
    states = rate_ref.shape[0]
    decay_ref[...] = jnp.exp(-rate_ref[...])
    hop = jnp.exp(-width * rate_ref[...])
    held = entering_ref[...]
    for chunk in range(CHUNKS):
        held_ref[chunk_rows(chunk, states), :] = held
        held = hop * held + sums_ref[chunk_rows(chunk, states), :]

    def body(group, unused):
        decay = decay_ref[pl.ds(group * GROUP, GROUP), :][:, None, :]
        coef = coef_ref[pl.ds(group * GROUP, GROUP), :][:, None, :]
        term = held_ref[pl.ds(group * GROUP * CHUNKS, GROUP * CHUNKS), :].reshape(
            GROUP, CHUNKS, LANES
        )
        term = term * (coef * decay)
        for place in range(width):
            mixed_ref[place * CHUNKS : (place + 1) * CHUNKS, :] += jnp.sum(term, axis=0)
            if place < width - 1:
                term = term * decay
        return unused

    lax.fori_loop(0, states // GROUP, body, 0)


def backward_states(width, grads_ref, rate_ref, sums_ref, first_ref, decay_ref):
    states = rate_ref.shape[0]
    decay_ref[...] = jnp.exp(-rate_ref[...])

    def body(group, unused):
        running = state_sums(
            width, grads_ref, decay_ref, None, group, range(width - 1, -1, -1), None, True
        )
        sums_ref[pl.ds(group * GROUP * CHUNKS, GROUP * CHUNKS), :] = running.reshape(-1, LANES)
        return unused

    lax.fori_loop(0, states // GROUP, body, 0)
    hop = jnp.exp(-width * rate_ref[...])
    held = jnp.zeros((states, LANES), jnp.float32)
    for chunk in range(CHUNKS - 1, -1, -1):
        held = hop * held + sums_ref[chunk_rows(chunk, states), :]
    first_ref[...] = held


def backward_near(
    width,
    grads_ref,
    rows_ref,
    sums_ref,
    entering_ref,
    rate_ref,
    skip_ref,
    kernel_ref,
    back_ref,
    coef_grad_ref,
    rate_grad_ref,
    decay_ref,
    hop_ref,
    taps_ref,
    after_ref,
    lag_ref,
):
    states = rate_ref.shape[0]
    hop = jnp.exp(-width * rate_ref[...])
    hop_ref[...] = hop
    held = entering_ref[...]
    for chunk in range(CHUNKS - 1, -1, -1):
        after_ref[chunk_rows(chunk, states), :] = held
        held = hop * held + sums_ref[chunk_rows(chunk, states), :]
    for lag in range(width):
        taps_ref[lag * CHUNKS : (lag + 1) * CHUNKS, :] = jnp.broadcast_to(
            kernel_ref[lag : lag + 1, :], (CHUNKS, LANES)
        )
    for start in range(0, width, 4):
        sums = [skip_ref[...] * block(grads_ref, start + i) for i in range(4)]
        for place in range(start, width):
            grads = block(grads_ref, place)
            for i in range(4):
                if place >= start + i:
                    sums[i] = sums[i] + block(taps_ref, place - start - i) * grads
        for i in range(4):
            back_ref[(start + i) * CHUNKS : (start + i + 1) * CHUNKS, :] = sums[i]
    for start in range(0, width, 4):
        sums = [jnp.zeros((CHUNKS, LANES), jnp.float32) for i in range(4)]
        for place in range(start, width):
            grads = block(grads_ref, place)
            for i in range(4):
                if place >= start + i:
                    sums[i] = sums[i] + block(rows_ref, place - start - i) * grads
        for i in range(4):
            lag_ref[start + i : start + i + 1, :] = jnp.sum(sums[i], axis=0, keepdims=True)
    decay_all = decay_ref[...]
    near_coef = jnp.zeros((states, LANES), jnp.float32)
    near_rate = jnp.zeros((states, LANES), jnp.float32)
    for lag in range(width - 1, -1, -1):
        near_coef = near_coef * decay_all + lag_ref[lag : lag + 1, :]
        near_rate = near_rate * decay_all + float(lag) * lag_ref[lag : lag + 1, :]
    coef_grad_ref[...] = near_coef
    rate_grad_ref[...] = near_rate


def backward_far(
    width,
    grads_ref,
    rows_ref,
    sums_ref,
    held_ref,
    coef_ref,
    back_ref,
    coef_grad_ref,
    rate_grad_ref,
    decay_ref,
    hop_ref,
    after_ref,
    groups,
):
    def body(group, unused):
        members = pl.ds(group * GROUP, GROUP)
        cells = pl.ds(group * GROUP * CHUNKS, GROUP * CHUNKS)
        cube = (GROUP, CHUNKS, LANES)
        decay = decay_ref[members, :][:, None, :]
        coef = coef_ref[members, :][:, None, :]
        after = after_ref[cells, :].reshape(cube)
        term = after * coef
        for place in range(width - 1, -1, -1):
            back_ref[place * CHUNKS : (place + 1) * CHUNKS, :] += jnp.sum(term, axis=0)
            if place > 0:
                term = term * decay
        held = held_ref[cells, :].reshape(cube)
        coef_grad_ref[members, :] += jnp.sum(held * sums_ref[cells, :].reshape(cube), axis=1)
        slope = state_sums(
            width,
            rows_ref,
            decay_ref,
            None,
            group,
            range(width),
            lambda place: float(width - 1 - place),
            False,
        )
        total = after * (float(width) * hop_ref[members, :][:, None, :] * held + slope)
        slope = state_sums(
            width,
            grads_ref,
            decay_ref,
            None,
            group,
            range(width - 1, -1, -1),
            lambda place: float(place + 1),
            True,
        )
        total = total + held * slope
        rate_grad_ref[members, :] += jnp.sum(total, axis=1)
        return unused

    lax.fori_loop(groups.start, groups.stop, body, 0)


MESH = pl.DeviceIdType.MESH


def add_rows(out_ref, out_start, a_ref, a_start, b_ref, b_start, rows):
    columns = out_ref.shape[1]
    size = 8
    for option in (16, 24, 32, 48, 64):
        if rows % option == 0 and option * columns <= 64 * 1024:
            size = option

    def body(i, unused):
        at = i * size
        out_ref[pl.ds(pl.multiple_of(out_start + at, 8), size), :] = (
            a_ref[pl.ds(pl.multiple_of(a_start + at, 8), size), :]
            + b_ref[pl.ds(pl.multiple_of(b_start + at, 8), size), :]
        )
        return unused

    lax.fori_loop(0, rows // size, body, 0)


class Lane:
    def __init__(self, rows, columns, bits, line_first, in_place):
        self.rows, self.columns = rows, columns
        self.bits, self.line_first, self.in_place = bits, line_first, in_place

    def buffers(self, line):
        half = self.rows // 2
        unit = half // line if self.line_first else half >> len(self.bits)
        counts = [half]
        size = half // line if self.line_first else half
        for unused in self.bits:
            size //= 2
            counts.append(size)
        counts.append(unit * (line + 1 if self.line_first else max(1, line // 2)))
        return [pltpu.VMEM((count, self.columns), jnp.float32) for count in counts]

    def copies(self, line):
        chain = 4 * line + 3 if self.line_first else line
        return 4 + 2 * len(self.bits) + chain


def lane_steps(
    lane, line, source, target, buffers, stage, load_sem, semaphores, first_sem, pending
):
    send_sems, recv_sems, free_sems = semaphores
    first, chain = buffers[0], buffers[-1]
    landing = buffers[1:-1]
    acc = source if lane.in_place else first
    me = lax.axis_index("seq")
    z = lax.axis_index("batch")
    half = lane.rows // 2
    core = me % 2
    counter = [first_sem]

    def fresh():
        counter[0] += 1
        return counter[0] - 1

    def remote(src, dst, index, device):
        return pltpu.make_async_remote_copy(
            src_ref=src,
            dst_ref=dst,
            send_sem=send_sems.at[index],
            recv_sem=recv_sems.at[index],
            device_id=device,
            device_id_type=MESH,
        )

    def rows_of(ref, start, count):
        if not isinstance(start, int):
            start = pl.multiple_of(start, 8)
        return ref.at[pl.ds(start, count), :]

    def side(bit):
        return (me // bit) % 2

    def partner(bit):
        return (me + bit * (1 - 2 * side(bit)), z)

    def free(index, device):
        pl.semaphore_signal(
            free_sems.at[index], inc=1, device_id=device, device_id_type=MESH
        )

    def wait_free(index):
        pl.semaphore_wait(free_sems.at[index], 1)

    mine, other = core * half, (1 - core) * half
    base_row = mine if lane.in_place else 0
    swap = remote(rows_of(source, other, half), first, fresh(), partner(1))

    def add_swap():
        if lane.in_place:
            swap.wait_recv()
            add_rows(acc, mine, acc, mine, first, 0, half)
        else:
            load = pltpu.make_async_copy(rows_of(source, mine, half), stage, load_sem)
            load.start()
            swap.wait_recv()
            load.wait()
            add_rows(acc, 0, acc, 0, stage, 0, half)

    pending.append(swap.wait_send)
    steps = [[swap.start], [add_swap]]

    def join(function):
        steps[-1].append(function)

    def step(function):
        steps.append([function])

    def neighbours_sum(base, size):
        starts, indices = [base], []
        for place, bit in enumerate(lane.bits):
            size //= 2
            start, index = starts[-1], fresh()
            copy = remote(
                rows_of(acc, base_row + start + (1 - side(bit)) * size, size),
                landing[place],
                index,
                partner(bit),
            )
            own = start + side(bit) * size
            join(copy.start)

            def receive(copy=copy, own=own, size=size, place=place, bit=bit, index=index):
                copy.wait()
                free(index, partner(bit))
                add_rows(acc, base_row + own, acc, base_row + own, landing[place], 0, size)

            step(receive)
            starts.append(own)
            indices.append(index)
        return starts, size, indices

    def neighbours_spread(starts, size, indices):
        for place in range(len(lane.bits) - 1, -1, -1):
            rows = rows_of(acc, base_row + starts[place + 1], size)
            copy = remote(rows, rows, fresh(), partner(lane.bits[place]))
            join(functools.partial(wait_free, indices[place]))
            join(copy.start)
            pending.append(copy.wait_send)
            step(copy.wait_recv)
            size *= 2

    if not lane.line_first:
        starts, size, indices = neighbours_sum(0, half)
        at = starts[-1]
        depth = jnp.minimum(z, line - 1 - z)
        lower = z < line // 2
        inward = (me, jnp.where(lower, z + 1, z - 1))
        outward = (me, jnp.where(lower, z - 1, z + 1))
        across = (me, line - 1 - z)
        middle = line // 2 - 1

        def on(level, function):
            def guarded():
                pl.when(depth == level)(function)

            return guarded

        passed = []
        for level in range(middle):
            rows = rows_of(acc, base_row + at, size)
            passed.append(fresh())
            copy = remote(rows, rows_of(chain, level * size, size), passed[-1], inward)
            join(on(level, copy.start))

            def receive(copy=copy, level=level):
                copy.wait_recv()
                add_rows(acc, base_row + at, acc, base_row + at, chain, level * size, size)

            def release(copy=copy, index=passed[-1]):
                copy.wait_send()
                free(index, inward)

            step(on(level + 1, receive))
            join(on(level, release))
        rows = rows_of(acc, base_row + at, size)
        copy = remote(rows, rows_of(chain, middle * size, size), fresh(), across)
        join(on(middle, copy.start))

        def receive_across(copy=copy):
            copy.wait()
            add_rows(acc, base_row + at, acc, base_row + at, chain, middle * size, size)

        step(on(middle, receive_across))
        for level in range(middle - 1, -1, -1):
            rows = rows_of(acc, base_row + at, size)
            copy = remote(rows, rows, fresh(), outward)
            join(on(level + 1, functools.partial(wait_free, passed[level])))
            join(on(level + 1, copy.start))
            pending.append(on(level + 1, copy.wait_send))
            step(on(level, copy.wait_recv))
        neighbours_spread(starts, size, indices)
    else:
        unit = half // line
        slots = [fresh() for unused in range(line + 1)]
        outs = [[fresh() for unused in range(2)] for unused in range(line)]
        spreads = [fresh() for unused in range(line)]

        def on(place, function):
            def guarded():
                pl.when(z == place)(function)

            return guarded

        def beside(place):
            return (me, place - 1 if place > 0 else place + 1)

        def hop(place, member, step_to):
            slot = line if step_to < 0 and member == place - 1 else member
            return remote(
                rows_of(acc, base_row + member * unit, unit),
                rows_of(chain, slot * unit, unit),
                slots[slot],
                (me, place + step_to),
            )

        def arrived(place, slot, member):
            remote(
                rows_of(acc, base_row + member * unit, unit),
                rows_of(chain, slot * unit, unit),
                slots[slot],
                beside(place),
            ).wait_recv()
            row = base_row + member * unit
            add_rows(acc, row, acc, row, chain, slot * unit, unit)

        for turn in range(line - 1):

            def rightward(place=turn):
                for member in range(line - 1, place, -1):
                    if place > 0:
                        arrived(place, member, member)
                    hop(place, member, 1).start()

            def leftward(place=line - 1 - turn):
                for member in range(place):
                    if place < line - 1:
                        arrived(place, member, member)
                    hop(place, member, -1).start()

            if turn > 0:
                step(on(turn, rightward))
            else:
                join(on(turn, rightward))
            join(on(line - 1 - turn, leftward))

        to_right, to_left = fresh(), fresh()

        def collect(place):
            if place > 0:
                arrived(place, place, place)
            if place < line - 1:
                arrived(place, line, place)
            for member in range(line - 1, place, -1):
                hop(place, member, 1).wait_send()
            if place < line - 1:
                free(to_right, (me, place + 1))
            for member in range(place):
                hop(place, member, -1).wait_send()
            if place > 0:
                free(to_left, (me, place - 1))

        def collect_all():
            for place in range(line):
                on(place, functools.partial(collect, place))()

        step(collect_all)

        base = z * unit
        starts, size, indices = neighbours_sum(base, unit)
        neighbours_spread(starts, size, indices)

        def spread_at(place, distance, receive, send):
            members = {place - distance, place + distance}
            for member in sorted(members):
                if not 0 <= member < line:
                    continue
                if receive and distance > 0:
                    remote(
                        rows_of(acc, base_row + member * unit, unit),
                        rows_of(acc, base_row + member * unit, unit),
                        spreads[member],
                        beside(place),
                    ).wait_recv()
                if not send:
                    continue
                for step_to in (1, -1):
                    going = member <= place if step_to > 0 else member >= place
                    if going and 0 <= place + step_to < line:
                        yield member, step_to

        def pass_on(place, member, step_to):
            return pltpu.make_async_remote_copy(
                src_ref=rows_of(acc, base_row + member * unit, unit),
                dst_ref=rows_of(acc, base_row + member * unit, unit),
                send_sem=send_sems.at[outs[member][0 if step_to > 0 else 1]],
                recv_sem=recv_sems.at[spreads[member]],
                device_id=(me, place + step_to),
                device_id_type=MESH,
            )

        for distance in range(line):

            def forward(place, distance):
                if distance == 0 and place > 0:
                    wait_free(to_right)
                if distance == 0 and place < line - 1:
                    wait_free(to_left)
                for member, step_to in spread_at(place, distance, True, True):
                    pass_on(place, member, step_to).start()

            def forward_all(distance=distance):
                for place in range(line):
                    on(place, functools.partial(forward, place, distance))()

            if distance == 0:
                join(forward_all)
            else:
                step(forward_all)

        def gone(place):
            for distance in range(line):
                for member, step_to in spread_at(place, distance, False, True):
                    pass_on(place, member, step_to).wait_send()

        for place in range(line):
            pending.append(on(place, functools.partial(gone, place)))

    keep_index, give_index = fresh(), fresh()
    done = rows_of(acc, base_row, half)
    keep = pltpu.make_async_copy(done, rows_of(target, mine, half), recv_sems.at[keep_index])
    give = remote(done, rows_of(target, mine, half), give_index, partner(1))
    join(keep.start)
    join(give.start)
    pending.append(keep.wait)
    pending.append(give.wait)
    assert counter[0] - first_sem <= lane.copies(line)
    return steps


def turn_order(lengths, order):
    if [order.count(place) for place in range(len(lengths))] == lengths:
        return order
    last = len(lengths) - 1
    turns = range(max(lengths[:-1], default=0))
    lanes = [place for turn in turns for place in range(last) if turn < lengths[place]]
    return [last] * lengths[last] + lanes


class Loop:
    def __init__(self, count, *parts):
        self.count, self.parts = count, parts

    def steps(self):
        return self.count * len(self.parts)


def call_all(functions):
    for function in functions:
        function()


def run_loop(loop, between):
    parts = len(loop.parts)

    def body(i, unused):
        for place, part in enumerate(loop.parts):
            part(i)
            for turn in range(loop.count):
                functions = between[turn * parts + place]
                if functions:
                    pl.when(i == turn)(functools.partial(call_all, functions))
        return unused

    lax.fori_loop(0, loop.count, body, 0)


class Runner:
    def __init__(self, programs, count, order):
        lengths = [len(program) for program in programs] + [count]
        self.programs = [list(program) for program in programs]
        self.order = turn_order(lengths, order)
        self.work_place = len(programs)
        self.at = 0

    def lanes(self):
        functions = []
        while self.at < len(self.order) and self.order[self.at] != self.work_place:
            functions += self.programs[self.order[self.at]].pop(0)
            self.at += 1
        return functions

    def run(self, work):
        for item in work:
            call_all(self.lanes())
            self.at += 1
            if not isinstance(item, Loop):
                item()
                continue
            between = []
            for unused in range(item.steps() - 1):
                between.append(self.lanes())
                self.at += 1
            run_loop(item, between + [[]])


def steps_in(work):
    return sum(item.steps() if isinstance(item, Loop) else 1 for item in work)


def state_exchange(bits, row_count, rate, totals, arrivals, entering, sends, receives, forward):
    me, z = lax.axis_index("seq"), lax.axis_index("batch")

    def copy(level):
        bit = bits[level]
        return pltpu.make_async_remote_copy(
            src_ref=totals[level],
            dst_ref=arrivals[level],
            send_sem=sends.at[level],
            recv_sem=receives.at[level],
            device_id=(me + bit * (1 - 2 * ((me // bit) % 2)), z),
            device_id_type=MESH,
        )

    def arrive(level):
        bit = bits[level]
        copy(level).wait_recv()
        place = me % bit
        after = (me // bit) % 2 == (1 if forward else 0)
        hops = (row_count * (place if forward else bit - 1 - place)).astype(jnp.float32)
        term = jnp.exp(-rate[...] * hops) * arrivals[level][...]
        term = jnp.where(after, term, 0.0)
        entering[...] = term if level == 0 else entering[...] + term
        if level + 1 < len(bits):
            far = jnp.exp(-float(row_count * bit) * rate[...])
            ours, theirs = totals[level][...], arrivals[level][...]
            totals[level + 1][...] = jnp.where(after, ours + far * theirs, theirs + far * ours)
            copy(level + 1).start()

    return copy, arrive


def lane_columns(tile):
    return pl.ds(pl.multiple_of(tile * LANES, LANES), LANES)


def row_block(i, count):
    return pl.ds(pl.multiple_of(i * count, count), count)


SKIP, GAIN_ONE, BIAS_ONE, GAIN_TWO, BIAS_TWO = range(5)


def vector(ref, place):
    return ref[place : place + 1, :]


class ForwardIn(NamedTuple):
    tokens: Any
    token_grads: Any
    vectors: Any
    query_weight: Any
    key_weight: Any
    value_weight: Any
    out_weight: Any
    taps: Any
    rate: Any
    coef: Any


class ForwardOut(NamedTuple):
    product: Any
    held: Any
    kernel: Any
    values: Any
    keys_mixed: Any
    key_rows: Any
    queries: Any
    mixed: Any
    gated: Any
    middle: Any
    normed_two: Any
    standard_two: Any
    factor_two: Any
    normed_one: Any
    standard_one: Any
    factor_one: Any
    out_grad: Any


def forward_body(row_count, size, bits, *refs):
    width = row_count // CHUNKS
    levels = len(bits)
    taken, outs = len(ForwardIn._fields), len(ForwardOut._fields)
    given = ForwardIn(*refs[:taken])
    results = ForwardOut(*refs[taken : taken + outs])
    own = ForwardOut(*refs[taken + outs : taken + 2 * outs])
    refs = refs[taken + 2 * outs :]
    sums, taps, decay, entering, edge_out, edge_in = refs[:6]
    totals, arrivals = refs[6 : 6 + levels], refs[6 + levels : 6 + 2 * levels]
    sends, receives, keeps = refs[-3:]
    rate, coef, skip = given.rate, given.coef, given.vectors.at[0:1]
    vectors = given.vectors
    channels = rate.shape[1]
    tiles = channels // LANES
    tap_count = given.taps.shape[0]
    halo = tap_count - 1
    low = jnp.bfloat16
    me, z = lax.axis_index("seq"), lax.axis_index("batch")
    barrier = pltpu.get_barrier_semaphore()

    def greet(device):
        pl.semaphore_signal(barrier, inc=1, device_id=device, device_id_type=MESH)

    for bit in bits:
        greet((me + bit * (1 - 2 * ((me // bit) % 2)), z))
    pl.when(me > 0)(lambda: greet((me - 1, z)))
    pl.when(me < size - 1)(lambda: greet((me + 1, z)))

    kept = ForwardOut(
        *[
            pltpu.make_async_copy(own[i], results[i], keeps.at[i])
            for i in range(len(ForwardOut._fields))
        ]
    )

    copy, arrive = state_exchange(
        bits, row_count, rate, totals, arrivals, entering, sends, receives, True
    )

    def edge(device):
        return pltpu.make_async_remote_copy(
            src_ref=edge_out,
            dst_ref=edge_in,
            send_sem=sends.at[levels],
            recv_sem=receives.at[levels],
            device_id=(device, z),
            device_id_type=MESH,
        )

    def reordered(rows, i):
        shape = (128, row_count)
        row = i * 128 + lax.broadcasted_iota(jnp.int32, shape, 0)
        token = lax.rem(row, CHUNKS) * width + lax.div(row, CHUNKS)
        chosen = lax.broadcasted_iota(jnp.int32, shape, 1) == token
        picks = jnp.where(chosen, 1.0, 0.0).astype(low)
        return jnp.dot(picks, rows[...], preferred_element_type=jnp.float32)

    def norm_rows(i):
        rows = row_block(i, 128)
        inputs = reordered(given.tokens, i)
        own.middle[rows, :] = inputs
        standard, factor = standardize(inputs)
        own.standard_one[rows, :] = standard
        own.factor_one[rows, :] = jnp.broadcast_to(factor, (128, LANES))
        own.normed_one[rows, :] = (
            standard * vector(vectors, GAIN_ONE) + vector(vectors, BIAS_ONE)
        ).astype(low)

    def grad_rows(i):
        own.out_grad[row_block(i, 128), :] = reordered(given.token_grads, i).astype(low)

    def project_to(target, weight, lead):
        def body(i):
            cols = row_block(i, 256)
            target[lead : lead + row_count, cols] = jnp.dot(
                own.normed_one[...], weight[:, cols], preferred_element_type=jnp.float32
            )

        return Loop(channels // 256, body)

    lead = halo * CHUNKS

    def send_edge():
        edge_out[...] = jnp.zeros(edge_out.shape, jnp.float32)
        for i in range(halo):
            row = lead + (width - halo + i) * CHUNKS + CHUNKS - 1
            edge_out[i : i + 1, :] = own.key_rows[row : row + 1, :]
        pl.semaphore_wait(
            barrier, levels + jnp.where(me > 0, 1, 0) + jnp.where(me < size - 1, 1, 0)
        )
        pl.when(me < size - 1)(edge(me + 1).start)

        @pl.when(me == 0)
        def at_start():
            edge_in[...] = jnp.zeros(edge_in.shape, jnp.float32)

    def take_edge():
        pl.when(me > 0)(edge(me - 1).wait_recv)

    def states_tile(tile):
        here = lane_columns(tile)
        keys, tap = own.key_rows, given.taps
        for i in range(halo):
            row = lead + (width - halo + i) * CHUNKS
            rows = keys[row : row + CHUNKS, here]
            keys[i * CHUNKS : (i + 1) * CHUNKS, here] = jnp.concatenate(
                [edge_in[i : i + 1, here], rows[: CHUNKS - 1]], axis=0
            )
        total = tap[0:1, here] * keys[lead : lead + row_count, here]
        for offset in range(1, tap_count):
            start = lead - offset * CHUNKS
            total = total + tap[offset : offset + 1, here] * keys[start : start + row_count, here]
        own.keys_mixed[:, here] = total
        own.product[:, here] = total * own.values[:, here]
        forward_states(
            width,
            own.product.at[:, here],
            rate.at[:, here],
            sums.at[tile],
            totals[0].at[:, here],
            decay,
        )

    def near_tile(tile):
        here = lane_columns(tile)
        forward_near(
            width,
            own.product.at[:, here],
            rate.at[:, here],
            coef.at[:, here],
            skip.at[:, here],
            own.mixed.at[:, here],
            own.kernel.at[:, here],
            taps,
        )

    def far_tile(tile):
        here = lane_columns(tile)
        forward_far(
            width,
            sums.at[tile],
            entering.at[:, here],
            rate.at[:, here],
            coef.at[:, here],
            own.mixed.at[:, here],
            own.held.at[tile],
            decay,
        )

    def out_rows(i):
        rows = row_block(i, 128)
        gated = (own.queries[rows, :] * own.mixed[rows, :]).astype(low)
        own.gated[rows, :] = gated
        middle = own.middle[rows, :] + jnp.dot(
            gated, given.out_weight[...], preferred_element_type=jnp.float32
        )
        own.middle[rows, :] = middle
        standard, factor = standardize(middle)
        own.standard_two[rows, :] = standard
        own.factor_two[rows, :] = jnp.broadcast_to(factor, (128, LANES))
        own.normed_two[rows, :] = (
            standard * vector(vectors, GAIN_TWO) + vector(vectors, BIAS_TWO)
        ).astype(low)

    def loop(item, between=()):
        between = list(between)
        run_loop(item, between + [[]] * (item.steps() - len(between)))

    def keep_all(*copies):
        for one in copies:
            one.start()

    loop(Loop(row_count // 128, norm_rows))
    keep_all(kept.standard_one, kept.factor_one, kept.normed_one)
    loop(project_to(own.key_rows, given.key_weight, lead))
    send_edge()
    loop(project_to(own.values, given.value_weight, 0))
    keep_all(kept.values)
    take_edge()
    loop(Loop(tiles, states_tile))
    copy(0).start()
    keep_all(kept.key_rows, kept.keys_mixed, kept.product)
    loop(project_to(own.queries, given.query_weight, 0))
    keep_all(kept.queries)
    loop(Loop(row_count // 128, grad_rows))
    keep_all(kept.out_grad)
    between = [[] for unused in range(tiles)]
    for level in range(levels):
        between[level * tiles // levels].append(functools.partial(arrive, level))
    loop(Loop(tiles, near_tile), between)
    keep_all(kept.kernel)
    loop(Loop(tiles, far_tile))
    keep_all(kept.mixed, kept.held)
    loop(Loop(row_count // 128, out_rows))
    keep_all(kept.gated, kept.middle, kept.normed_two, kept.standard_two, kept.factor_two)
    for level in range(levels):
        copy(level).wait_send()
    pl.when(me < size - 1)(edge(me + 1).wait_send)
    for one in kept:
        one.wait()


def forward(row_count, arrays):
    size = lax.axis_size("seq")
    bits = [1 << place for place in range(size.bit_length() - 1)]
    states, channels = arrays.rate.shape
    tiles, width = channels // LANES, row_count // CHUNKS
    halo = arrays.taps.shape[0] - 1
    full, low = jnp.float32, jnp.bfloat16
    square = ((row_count, channels), full)
    low_square = ((row_count, channels), low)
    thin = ((row_count, LANES), full)
    held = ((tiles, states * CHUNKS, LANES), full)
    outs = ForwardOut(
        product=square,
        held=held,
        kernel=((width, channels), full),
        values=square,
        keys_mixed=square,
        key_rows=((row_count + halo * CHUNKS, channels), full),
        queries=square,
        mixed=square,
        gated=low_square,
        middle=square,
        normed_two=low_square,
        standard_two=square,
        factor_two=thin,
        normed_one=low_square,
        standard_one=square,
        factor_one=thin,
        out_grad=low_square,
    )
    scratch = list(outs) + [held, thin, ((states, LANES), full), ((states, channels), full)]
    scratch += [((8, channels), full)] * 2 + [((states, channels), full)] * (2 * len(bits))
    counts = [len(bits) + 1, len(bits) + 1, len(outs)]
    found = pl.pallas_call(
        functools.partial(forward_body, row_count, size, bits),
        out_shape=[jax.ShapeDtypeStruct(*out) for out in outs],
        in_specs=[pl.BlockSpec(memory_space=pltpu.VMEM)] * len(ForwardIn._fields),
        out_specs=[pl.BlockSpec(memory_space=pltpu.HBM)] * len(outs),
        scratch_shapes=[pltpu.VMEM(*shape) for shape in scratch]
        + [pltpu.SemaphoreType.DMA((count,)) for count in counts],
        compiler_params=pltpu.CompilerParams(
            collective_id=1, has_side_effects=True, vmem_limit_bytes=VMEM_LIMIT
        ),
    )(*[getattr(arrays, name) for name in ForwardIn._fields])
    return ForwardOut(*found)


class BackwardIn(NamedTuple):
    up_weight: Any
    down_weight: Any
    out_weight: Any
    query_weight: Any
    key_weight: Any
    value_weight: Any
    product: Any
    held: Any
    values: Any
    keys_mixed: Any
    key_rows: Any
    queries: Any
    mixed: Any
    gated: Any
    middle: Any
    standard_two: Any
    factor_two: Any
    standard_one: Any
    factor_one: Any
    rate: Any
    coef: Any
    vectors: Any
    taps: Any
    kernel: Any
    out_grad: Any
    normed_one: Any
    normed_two: Any


FAR = 19


class Results(NamedTuple):
    down: Any
    up: Any
    out: Any
    query: Any
    value: Any
    key: Any
    small: Any
    tokens: Any
    mixed_out: Any
    own_down: Any
    own_up: Any
    own_out: Any


HIDDEN_AT_ONCE = 256


def gelu_pair(values):
    slope = math.sqrt(2.0 / math.pi)
    squared = values * values
    bent = jnp.tanh(slope * (values + 0.044715 * (values * squared)))
    half = 0.5 * (1.0 + bent)
    steep = 0.5 * values * (1.0 - bent * bent) * (slope * (1.0 + 3.0 * 0.044715 * squared))
    return values * half, half + steep


def backward_body(row_count, size, line, bits, lanes, order, *refs):
    width = row_count // CHUNKS
    given = BackwardIn(*refs[: len(BackwardIn._fields)])
    rest = list(refs[len(given) :])

    def take(count):
        taken = rest[:count]
        del rest[:count]
        return taken

    results = Results(*take(len(Results._fields)))
    semaphores = rest[-6:-3]
    load_sems, swap_send, swap_recv = rest[-3:]
    del rest[-6:]
    (grad_query, grad_value, grad_key, small) = take(4)
    (shifted, total, grad_middle) = take(3)
    (grad_queries, values_low, keys_low, weight) = take(4)
    (entering, edge_out, edge_in, stage) = take(4)
    levels = len(bits)
    totals, arrivals = take(levels), take(levels)

    me = lax.axis_index("seq")
    z = lax.axis_index("batch")
    channels = small.shape[1]
    tiles = channels // LANES
    rate, coef = given.rate, given.coef
    states = rate.shape[0]
    tap_count = given.taps.shape[0]
    halo = tap_count - 1
    hidden = given.up_weight.shape[1]
    low, full = jnp.bfloat16, jnp.float32
    misc = 2 * states

    barrier = pltpu.get_barrier_semaphore()

    def greet(device):
        pl.semaphore_signal(barrier, inc=1, device_id=device, device_id_type=MESH)

    for bit in bits:
        greet((me + bit * (1 - 2 * ((me // bit) % 2)), z))
    pl.when(z > 0)(lambda: greet((me, z - 1)))
    pl.when(z < line - 1)(lambda: greet((me, z + 1)))
    pl.when(me > 0)(lambda: greet((me - 1, z)))
    pl.when(me < size - 1)(lambda: greet((me + 1, z)))
    pl.semaphore_wait(
        barrier,
        len(bits)
        + jnp.where(z > 0, 1, 0)
        + jnp.where(z < line - 1, 1, 0)
        + jnp.where(me > 0, 1, 0)
        + jnp.where(me < size - 1, 1, 0),
    )

    def local(source, target, place):
        return pltpu.make_async_copy(source, target, load_sems.at[place])

    def fetch(*triples):
        copies = [local(*triple) for triple in triples]
        for copy in copies:
            copy.start()
        for copy in copies:
            copy.wait()

    def add_small(row, value):
        small[row : row + 1, :] += jnp.sum(value, axis=0, keepdims=True)

    exchange, arrive = state_exchange(
        bits, row_count, rate, totals, arrivals, entering, swap_send, swap_recv, False
    )

    def edge(device):
        return pltpu.make_async_remote_copy(
            src_ref=edge_out,
            dst_ref=edge_in,
            send_sem=swap_send.at[levels],
            recv_sem=swap_recv.at[levels],
            device_id=(device, z),
            device_id_type=MESH,
        )

    steps = hidden // HIDDEN_AT_ONCE
    per_block = channels // HIDDEN_AT_ONCE
    held_weight = local(given.out_weight, weight, 7)
    held_standard = local(given.standard_two, shifted.at[:row_count], 8)
    held_gated = local(given.gated, values_low, 9)
    held_middle = local(given.middle, total, 10)
    out_rows = local(keys_low, results.mixed_out, 10)

    def feed_forward(
        up_tile, down_tile, active, grad_low, slope, down_sum, up_sum, block_a, block_b, thin
    ):
        def weights(step):
            here = row_block(step, HIDDEN_AT_ONCE)
            slot = step % 2
            return (
                local(given.up_weight.at[:, here], up_tile.at[slot], slot),
                local(given.down_weight.at[here, :], down_tile.at[slot], 2 + slot),
            )

        def sums(step):
            part = step // per_block
            here = row_block(step % per_block, HIDDEN_AT_ONCE)
            return (
                local(down_sum, results.own_down.at[part, here, :], 4),
                local(up_sum, results.own_up.at[part, :, here], 5),
            )

        def start():
            for copy in weights(0):
                copy.start()
            for copy in (held_middle, held_weight, held_standard, held_gated):
                copy.start()
            small[...] = jnp.zeros(small.shape, full)
            grad_middle[...] = jnp.zeros(grad_middle.shape, full)
            held_middle.wait()

        def part_one(step):
            slot = step % 2
            for copy in weights(step):
                copy.wait()

            @pl.when(step + 1 < steps)
            def following():
                for copy in weights(step + 1):
                    copy.start()

            before = jnp.dot(
                given.normed_two[...], up_tile[slot], preferred_element_type=full
            )
            after, steep = gelu_pair(before)
            active[...] = after.astype(low)
            slope[...] = steep

        def part_two(step):
            slot = step % 2
            total[...] += jnp.dot(active[...], down_tile[slot], preferred_element_type=full)
            grads = project_back(given.out_grad[...], down_tile[slot])
            grad_low[...] = (grads * slope[...]).astype(low)

        def part_three(step):
            @pl.when(step > 0)
            def previous():
                for copy in sums(step - 1):
                    copy.wait()

            down_sum[...] = weight_grad(active[...], given.out_grad[...])
            up_sum[...] = weight_grad(given.normed_two[...], grad_low[...])
            for copy in sums(step):
                copy.start()

        def part_four(step):
            grad_middle[...] += project_back(grad_low[...], up_tile[step % 2])

        def finish():
            for copy in sums(steps - 1):
                copy.wait()
            keys_low[...] = total[...].astype(low)
            out_rows.start()
            held_standard.wait()
            held_weight.wait()
            held_gated.wait()
            out_rows.wait()

        def norm_two(i):
            rows = row_block(i, 128)
            fetch((given.factor_two.at[rows, :], thin, 11))
            grads, standard = grad_middle[rows, :], shifted[rows, :]
            add_small(misc + tap_count + 3, grads * standard)
            add_small(misc + tap_count + 4, grads)
            back = given.out_grad[rows, :].astype(full) + norm_back(
                grads, vector(given.vectors, GAIN_TWO), standard, thin[:, 0:1]
            )
            grad_middle[rows, :] = back
            keys_low[rows, :] = back.astype(low)

        def out_sum(i):
            here = row_block(i, 256)
            down_sum[...] = weight_grad(values_low[:, here], keys_low[...])
            fetch((down_sum, results.own_out.at[0, here, :], 4))

        def gate(i):
            rows = row_block(i, 128)
            fetch(
                (given.mixed.at[rows, :], block_a, 11),
                (given.queries.at[rows, :], block_b, 12),
            )
            grads = project_back(keys_low[rows, :], weight[...])
            grad_queries[rows, :] = (grads * block_a[...]).astype(low)
            total[rows, :] = grads * block_b[...]

        return [
            start,
            Loop(steps, part_one, part_two, part_three, part_four),
            finish,
            Loop(row_count // 128, norm_two),
            Loop(channels // 256, out_sum),
            Loop(row_count // 128, gate),
        ]

    def weight_sum(target, grads):
        def body(i):
            rows = row_block(i, 256)
            target[rows, :] = weight_grad(given.normed_one[:, rows], grads[...])

        return Loop(channels // 256, body)

    back = shifted

    def mixer(
        rows_tile, keys_tile, other, held_tile, back_tile, taps, sums, after, decay, hop, lag
    ):
        def tile_loads(tile):
            here, slot = lane_columns(tile), tile % 2
            return (
                local(given.product.at[:, here], rows_tile.at[slot], 10 + slot),
                local(given.held.at[tile], held_tile.at[slot], 12 + slot),
                local(given.values.at[:, here], other.at[slot, pl.ds(0, row_count)], 14 + slot),
                local(given.keys_mixed.at[:, here], keys_tile.at[slot], 16 + slot),
            )

        def key_loads(tile):
            slot = tile % 2
            return local(given.key_rows.at[:, lane_columns(tile)], other.at[slot], 14 + slot)

        def first_tile(tile):
            here = lane_columns(tile)
            backward_states(
                width,
                total.at[:, here],
                rate.at[:, here],
                sums.at[tile],
                totals[0].at[:, here],
                decay,
            )

        def start_tiles():
            for copy in tile_loads(0):
                copy.start()
            exchange(0).start()

        def near(tile):
            here, slot = lane_columns(tile), tile % 2
            for copy in tile_loads(tile):
                copy.wait()

            @pl.when(tile + 1 < tiles)
            def following():
                for copy in tile_loads(tile + 1):
                    copy.start()

            decay[...] = jnp.exp(-rate[:, here])
            backward_near(
                width,
                total.at[:, here],
                rows_tile.at[slot],
                sums.at[tile],
                entering.at[:, here],
                rate.at[:, here],
                given.vectors.at[0:1, here],
                given.kernel.at[:, here],
                back_tile,
                small.at[0:states, here],
                small.at[states:misc, here],
                decay,
                hop,
                taps,
                after,
                lag,
            )

        def far(half):
            def part(tile):
                here, slot = lane_columns(tile), tile % 2
                groups = states // GROUP // 2
                backward_far(
                    width,
                    total.at[:, here],
                    rows_tile.at[slot],
                    sums.at[tile],
                    held_tile.at[slot],
                    coef.at[:, here],
                    back_tile,
                    small.at[0:states, here],
                    small.at[states:misc, here],
                    decay,
                    hop,
                    after,
                    range(half * groups, (half + 1) * groups),
                )

            return part

        def end(tile):
            here, slot = lane_columns(tile), tile % 2
            row = misc + tap_count
            small[row : row + 1, here] = jnp.sum(
                total[:, here] * rows_tile[slot], axis=0, keepdims=True
            )
            small[states:misc, here] = -coef[:, here] * small[states:misc, here]
            shifted[0:row_count, here] = back_tile[...] * other[slot, 0:row_count, :]
            values_low[:, here] = (back_tile[...] * keys_tile[slot]).astype(low)

        held_ones = local(given.standard_one, total, 7)
        held_factor = local(given.factor_one, back_tile, 8)

        def send_edge():
            key_loads(0).start()
            held_ones.start()
            held_factor.start()
            edge_out[...] = jnp.zeros(edge_out.shape, full)
            for place in range(halo):
                row = place * CHUNKS
                edge_out[place : place + 1, :] = shifted[row : row + 1, :]
            pl.when(me > 0)(edge(me - 1).start)

            @pl.when(me == size - 1)
            def at_end():
                edge_in[...] = jnp.zeros(edge_in.shape, full)

        def take_edge():
            pl.when(me < size - 1)(edge(me + 1).wait_recv)

        def keys_part(tile):
            here, slot = lane_columns(tile), tile % 2
            key_loads(tile).wait()

            @pl.when(tile + 1 < tiles)
            def following():
                key_loads(tile + 1).start()

            for place in range(halo):
                rows = shifted[place * CHUNKS : (place + 1) * CHUNKS, here]
                start = row_count + place * CHUNKS
                shifted[start : start + CHUNKS, here] = jnp.concatenate(
                    [rows[1:], edge_in[place : place + 1, here]], axis=0
                )
            tap = given.taps
            sum_rows = tap[0:1, here] * shifted[0:row_count, here]
            for offset in range(1, tap_count):
                start = offset * CHUNKS
                sum_rows = sum_rows + tap[offset : offset + 1, here] * (
                    shifted[start : start + row_count, here]
                )
            keys_low[:, here] = sum_rows.astype(low)
            grads = shifted[0:row_count, here]
            for offset in range(tap_count):
                start = (halo - offset) * CHUNKS
                small[misc + offset : misc + offset + 1, here] = jnp.sum(
                    grads * other[slot, start : start + row_count, :], axis=0, keepdims=True
                )

        def back_sum(index, grads):
            def body(i):
                rows = row_block(i, 128)
                term = project_back(grads[rows, :], weight[...])
                back[rows, :] = term if index == 0 else back[rows, :] + term

            return Loop(row_count // 128, body)

        def before_norm():
            held_ones.wait()
            held_factor.wait()

        def norm_one(i):
            rows = row_block(i, ROWS_AT_ONCE)
            grads, standard = back[rows, :], total[rows, :]
            add_small(misc + tap_count + 1, grads * standard)
            add_small(misc + tap_count + 2, grads)
            grad_middle[rows, :] += norm_back(
                grads, vector(given.vectors, GAIN_ONE), standard, back_tile[rows, 0:1]
            )

        tokens_out = local(grad_middle, results.tokens, 9)
        work = [Loop(tiles, first_tile), start_tiles]
        work.append(weight_sum(grad_query, grad_queries))
        for level in range(levels):
            work.append(functools.partial(arrive, level))
        work.append(Loop(tiles, near, far(0), far(1), end))
        work.append(send_edge)
        work.append(weight_sum(grad_value, values_low))
        work.append(take_edge)
        work.append(Loop(tiles, keys_part))
        work.append(weight_sum(grad_key, keys_low))
        chain = (
            (given.query_weight, grad_queries),
            (given.key_weight, keys_low),
            (given.value_weight, values_low),
        )
        for index, (source, grads) in enumerate(chain):
            work.append(functools.partial(fetch, (source, weight, 0)))
            work.append(back_sum(index, grads))
        work.append(before_norm)
        work.append(Loop(row_count // ROWS_AT_ONCE, norm_one))
        work.append(tokens_out.start)
        work.append(tokens_out.wait)
        return work

    def block_of(lane):
        cols = pl.ds(lane.column, lane.columns)
        if lane.array == 0:
            target = results.down.at[pl.ds(lane.part * channels, channels), cols]
            return results.own_down.at[lane.part, :, cols], target
        if lane.array == 1:
            target = results.up.at[:, pl.ds(lane.part * channels + lane.column, lane.columns)]
            return results.own_up.at[lane.part, :, cols], target
        if lane.array == 2:
            return results.own_out.at[0, :, cols], results.out.at[:, cols]
        source = (grad_query, grad_value, grad_key, small)[lane.array - 3]
        return source.at[:, cols], results[lane.array].at[:, cols]

    pending = [exchange(level).wait_send for level in range(levels)]
    pending.append(lambda: pl.when(me > 0)(edge(me - 1).wait_send))
    programs = []
    start = 0
    for lane in lanes:
        source, target = block_of(lane)
        programs.append(
            lane_steps(
                lane,
                line,
                source,
                target,
                take(len(lane.buffers(line))),
                stage,
                load_sems.at[6],
                semaphores,
                start,
                pending,
            )
        )
        start += lane.copies(line)

    def vmem(*shape, kind=full):
        return pltpu.VMEM(shape, kind)

    count = work_steps(row_count, channels, hidden, levels)
    runner = Runner(programs, count, order)
    done = [0]

    def run(make):
        def scoped(*refs):
            work = make(*refs)
            done[0] += steps_in(work)
            runner.run(work)

        return scoped

    pl.run_scoped(
        run(feed_forward),
        vmem(2, channels, HIDDEN_AT_ONCE, kind=low),
        vmem(2, HIDDEN_AT_ONCE, channels, kind=low),
        vmem(row_count, HIDDEN_AT_ONCE, kind=low),
        vmem(row_count, HIDDEN_AT_ONCE, kind=low),
        vmem(row_count, HIDDEN_AT_ONCE),
        vmem(HIDDEN_AT_ONCE, channels),
        vmem(channels, HIDDEN_AT_ONCE),
        vmem(128, channels),
        vmem(128, channels),
        vmem(128, LANES),
    )
    cells = states * CHUNKS
    pl.run_scoped(
        run(mixer),
        vmem(2, row_count, LANES),
        vmem(2, row_count, LANES),
        vmem(2, row_count + halo * CHUNKS, LANES),
        vmem(2, cells, LANES),
        vmem(row_count, LANES),
        vmem(row_count, LANES),
        vmem(tiles, cells, LANES),
        vmem(cells, LANES),
        vmem(states, LANES),
        vmem(states, LANES),
        vmem(width, LANES),
    )
    assert done[0] == count
    call_all(runner.lanes())
    call_all(pending)


def work_steps(row_count, channels, hidden, levels):
    tiles, weights = channels // LANES, channels // 256
    first = 2 + 4 * (hidden // HIDDEN_AT_ONCE) + 2 * (row_count // 128) + weights
    second = 6 * tiles + 3 * weights + levels + 6 + 3 * (row_count // 128)
    return first + second + row_count // ROWS_AT_ONCE + 3


def backward(row_count, arrays, plan, order):
    size, line = lax.axis_size("seq"), lax.axis_size("batch")
    bits = [1 << place for place in range(size.bit_length() - 1)]
    channels, hidden = arrays.up_weight.shape
    states = arrays.rate.shape[0]
    tap_count = arrays.taps.shape[0]
    misc_rows = 2 * states + tap_count + 5
    small_rows = misc_rows + -misc_rows % (8 * size)
    full, low = jnp.float32, jnp.bfloat16
    parts = hidden // channels
    lanes = []
    for index, pieces in enumerate(plan):
        columns = channels if index == 6 else channels // 2
        for piece, (flipped, line_first) in enumerate(pieces):
            rows = small_rows if index == 6 else channels
            if rows % (8 * size * line):
                line_first = False
            path = bits[:0:-1] if flipped else bits[1:]
            lane = Lane(rows, columns, path, line_first, index > 2)
            lane.array, lane.part, lane.column = index, piece // 2, piece % 2 * columns
            lanes.append(lane)
    square = ((channels, channels), full)
    wide = ((row_count, channels), full)
    low_wide = ((row_count, channels), low)
    small = ((small_rows, channels), full)
    key_rows = arrays.key_rows.shape[0]
    one = ((states, channels), full)
    scratch = [square] * 3 + [small, ((key_rows, channels), full), wide, wide]
    scratch += [low_wide] * 3 + [((channels, channels), low)]
    scratch += [one] + [((8, channels), full)] * 2 + [((channels // 2, channels // 2), full)]
    scratch += [one] * (2 * len(bits))
    scratch = [pltpu.VMEM(*shape) for shape in scratch]
    scratch += [buffer for lane in lanes for buffer in lane.buffers(line)]
    copies = sum(lane.copies(line) for lane in lanes)
    counts = [20, len(bits) + 1, len(bits) + 1]
    outs = [((hidden, channels), full), ((channels, hidden), full)] + [square] * 4
    outs += [small, wide, low_wide]
    outs += [((parts, channels, channels), full)] * 2 + [((1, channels, channels), full)]
    found = pl.pallas_call(
        functools.partial(backward_body, row_count, size, line, bits, lanes, order),
        out_shape=[jax.ShapeDtypeStruct(*out) for out in outs],
        in_specs=[pl.BlockSpec(memory_space=pltpu.HBM)] * FAR
        + [pl.BlockSpec(memory_space=pltpu.VMEM)] * (len(BackwardIn._fields) - FAR),
        out_specs=[pl.BlockSpec(memory_space=pltpu.HBM)] * len(outs),
        scratch_shapes=scratch
        + [pltpu.SemaphoreType.DMA((copies,)), pltpu.SemaphoreType.DMA((copies,))]
        + [pltpu.SemaphoreType.REGULAR((copies,))]
        + [pltpu.SemaphoreType.DMA((count,)) for count in counts],
        compiler_params=pltpu.CompilerParams(
            collective_id=0, has_side_effects=True, vmem_limit_bytes=VMEM_LIMIT
        ),
    )(*[getattr(arrays, name) for name in BackwardIn._fields])
    return Results(*found)


PLAN = [
    [(True, False), (False, False), (False, True), (True, True), (True, False), (True, False), (False, True), (False, False)],
    [(False, False), (True, True), (False, False), (True, False), (False, False), (False, True), (False, False), (True, True)],
    [(True, False), (True, False)],
    [(True, False), (False, False)],
    [(True, False), (True, False)],
    [(False, True), (False, False)],
    [(False, False)],
]
ORDER = [
    25, 25, 25, 25, 25, 25, 25, 25, 25, 25, 25, 25, 8, 25, 25, 25, 25, 0, 9, 1, 8, 25, 25, 25,
    0, 25, 9, 25, 1, 25, 25, 25, 10, 25, 25, 8, 25, 10, 25, 11, 3, 2, 25, 0, 25, 9, 25, 11, 25,
    3, 8, 25, 1, 2, 25, 9, 25, 25, 12, 25, 25, 25, 25, 12, 4, 5, 13, 25, 11, 9, 3, 10, 25, 4,
    25, 1, 5, 0, 25, 13, 9, 25, 3, 25, 25, 25, 8, 14, 25, 10, 25, 6, 12, 3, 15, 7, 14, 25, 6,
    11, 15, 9, 2, 4, 7, 8, 25, 25, 2, 25, 1, 5, 8, 14, 9, 25, 25, 0, 12, 2, 4, 25, 3, 16, 1, 17,
    25, 25, 0, 16, 13, 1, 17, 7, 8, 25, 14, 25, 0, 9, 5, 13, 25, 3, 2, 10, 25, 25, 16, 13, 6,
    25, 1, 8, 10, 25, 0, 3, 25, 6, 11, 17, 10, 25, 25, 16, 25, 25, 18, 13, 19, 25, 7, 2, 6, 18,
    11, 19, 15, 1, 11, 15, 0, 17, 3, 12, 15, 10, 4, 25, 13, 2, 6, 14, 12, 9, 4, 18, 19, 12, 15,
    5, 14, 11, 16, 25, 9, 25, 6, 4, 13, 7, 25, 5, 10, 14, 25, 17, 19, 2, 25, 16, 25, 12, 9, 3,
    25, 18, 15, 7, 25, 5, 19, 25, 25, 6, 4, 11, 13, 17, 25, 2, 25, 18, 16, 25, 14, 25, 3, 25,
    12, 15, 25, 7, 19, 25, 25, 4, 15, 5, 25, 6, 13, 25, 7, 25, 16, 17, 25, 18, 25, 2, 25, 25, 5,
    25, 25, 14, 25, 3, 25, 21, 20, 19, 21, 20, 16, 7, 25, 25, 15, 25, 25, 25, 25, 6, 17, 19, 25,
    25, 25, 25, 23, 22, 25, 13, 25, 25, 23, 25, 22, 21, 18, 25, 25, 19, 25, 25, 25, 2, 25, 25,
    25, 25, 25, 20, 15, 25, 25, 25, 22, 25, 23, 25, 25, 6, 25, 25, 25, 21, 25, 22, 24, 25, 25,
    13, 17, 24, 18, 21, 23, 15, 20, 6, 21, 23, 24, 18, 22, 20, 24, 23, 22, 21, 24, 22, 20, 23,
    22, 24, 21, 22, 20, 23, 24, 20, 22, 21, 22, 24, 23, 22, 24, 20,
]


def on_device(
    tokens,
    norm1_gain,
    norm1_bias,
    query_weight,
    key_weight,
    value_weight,
    shift_taps,
    ssm_coef,
    ssm_rate,
    ssm_skip,
    out_weight,
    norm2_gain,
    norm2_bias,
    up_weight,
    down_weight,
    out_grad,
):
    unused, row_count, channels = tokens.shape
    width = row_count // CHUNKS
    states = ssm_rate.shape[0]
    tap_count = shift_taps.shape[0]

    def token_order(values):
        return values.reshape(width, CHUNKS, channels).swapaxes(0, 1).reshape(1, row_count, channels)

    vectors = jnp.stack([ssm_skip, norm1_gain, norm1_bias, norm2_gain, norm2_bias])
    arrays = SimpleNamespace(
        tokens=tokens[0],
        token_grads=out_grad[0],
        vectors=jnp.concatenate([vectors, jnp.zeros_like(vectors[:3])], axis=0),
        query_weight=query_weight,
        key_weight=key_weight,
        value_weight=value_weight,
        out_weight=out_weight,
        up_weight=up_weight,
        down_weight=down_weight,
        taps=shift_taps,
        rate=ssm_rate,
        coef=ssm_coef,
    )
    vars(arrays).update(forward(row_count, arrays)._asdict())
    found = backward(row_count, arrays, PLAN, ORDER)
    small = found.small
    misc = 2 * states
    first = misc + tap_count
    return (
        token_order(found.mixed_out),
        token_order(found.tokens),
        small[first + 1],
        small[first + 2],
        found.query,
        found.key,
        found.value,
        small[misc:first],
        small[:states],
        small[states:misc],
        small[first],
        found.out,
        small[first + 3],
        small[first + 4],
        found.up,
        found.down,
    )


def solution(mesh):
    placed = (P("batch", "seq", None),) + (P(),) * 14 + (P("batch", "seq", None),)
    return jax.shard_map(
        on_device,
        mesh=mesh,
        in_specs=placed,
        out_specs=(P("batch", "seq", None),) * 2 + (P(),) * 14,
        check_vma=False,
    )
```

```python
import functools
import math
from types import SimpleNamespace
from typing import Any, NamedTuple

import jax
import jax.numpy as jnp
from jax import lax
from jax.experimental import pallas as pl
from jax.experimental.pallas import tpu as pltpu
from jax.sharding import PartitionSpec as P

epsilon = 1e-05
CHUNKS = 16
GROUP = 8
LANES = 128

VMEM_LIMIT = 64 * 2**20
ROWS_AT_ONCE = 64


def standardize(values):
    row_mean = jnp.mean(values, axis=-1, keepdims=True)
    centered = values - row_mean
    spread = jnp.mean(centered * centered, axis=-1, keepdims=True)
    factor = lax.rsqrt(spread + epsilon)
    return centered * factor, factor


def norm_back(grads, gain, standard, factor):
    scaled = grads * gain
    return factor * (
        scaled
        - jnp.mean(scaled, axis=-1, keepdims=True)
        - standard * jnp.mean(scaled * standard, axis=-1, keepdims=True)
    )


def project_back(grads_low, weight):
    return lax.dot_general(
        grads_low, weight, (((1,), (1,)), ((), ())), preferred_element_type=jnp.float32
    )


def weight_grad(rows_low, grads_low):
    return lax.dot_general(
        rows_low, grads_low, (((0,), (0,)), ((), ())), preferred_element_type=jnp.float32
    )


def block(ref, place):
    return ref[place * CHUNKS : (place + 1) * CHUNKS, :]


def chunk_rows(chunk, states):
    return pl.ds(chunk, states, stride=CHUNKS)


def state_sums(width, rows_ref, decay_ref, out_ref, group, places, weight, lead):
    decay = decay_ref[pl.ds(group * GROUP, GROUP), :][:, None, :]
    running = jnp.zeros((GROUP, CHUNKS, LANES), jnp.float32)
    for place in places:
        rows = block(rows_ref, place)
        if weight is not None:
            rows = rows * weight(place)
        running = decay * (running + rows[None]) if lead else decay * running + rows[None]
    return running


def forward_states(width, rows_ref, rate_ref, sums_ref, last_ref, decay_ref):
    states = rate_ref.shape[0]
    decay_ref[...] = jnp.exp(-rate_ref[...])

    def body(group, unused):
        running = state_sums(width, rows_ref, decay_ref, None, group, range(width), None, False)
        sums_ref[pl.ds(group * GROUP * CHUNKS, GROUP * CHUNKS), :] = running.reshape(-1, LANES)
        return unused

    lax.fori_loop(0, states // GROUP, body, 0)
    hop = jnp.exp(-width * rate_ref[...])
    held = jnp.zeros((states, LANES), jnp.float32)
    for chunk in range(CHUNKS):
        held = hop * held + sums_ref[chunk_rows(chunk, states), :]
    last_ref[...] = held


def forward_near(
    width, rows_ref, rate_ref, coef_ref, skip_ref, mixed_ref, kernel_ref, taps_ref
):
    states = rate_ref.shape[0]
    lags = lax.broadcasted_iota(jnp.int32, (8, LANES), 0).astype(jnp.float32)

    def add_states(group, totals):
        members = pl.ds(pl.multiple_of(group * GROUP, GROUP), GROUP)
        rates, coefs = rate_ref[members, :], coef_ref[members, :]
        steps = jnp.exp(-8.0 * rates)
        totals = list(totals)
        for i in range(GROUP):
            term = coefs[i : i + 1] * jnp.exp(-rates[i : i + 1] * lags)
            for place in range(width // 8):
                totals[place] = totals[place] + term
                term = term * steps[i : i + 1]
        return tuple(totals)

    zero = jnp.zeros((8, LANES), jnp.float32)
    totals = lax.fori_loop(0, states // GROUP, add_states, (zero,) * (width // 8))
    kernel_ref[...] = jnp.concatenate(totals, axis=0)
    for lag in range(width):
        taps_ref[lag * CHUNKS : (lag + 1) * CHUNKS, :] = jnp.broadcast_to(
            kernel_ref[lag : lag + 1, :], (CHUNKS, LANES)
        )
    for start in range(0, width, 4):
        sums = [skip_ref[...] * block(rows_ref, start + i) for i in range(4)]
        for place in range(start + 4):
            rows = block(rows_ref, place)
            for i in range(4):
                if start + i >= place:
                    sums[i] = sums[i] + block(taps_ref, start + i - place) * rows
        for i in range(4):
            mixed_ref[(start + i) * CHUNKS : (start + i + 1) * CHUNKS, :] = sums[i]


def forward_far(
    width, sums_ref, entering_ref, rate_ref, coef_ref, mixed_ref, held_ref, decay_ref
):
    states = rate_ref.shape[0]
    decay_ref[...] = jnp.exp(-rate_ref[...])
    hop = jnp.exp(-width * rate_ref[...])
    held = entering_ref[...]
    for chunk in range(CHUNKS):
        held_ref[chunk_rows(chunk, states), :] = held
        held = hop * held + sums_ref[chunk_rows(chunk, states), :]

    def body(group, unused):
        decay = decay_ref[pl.ds(group * GROUP, GROUP), :][:, None, :]
        coef = coef_ref[pl.ds(group * GROUP, GROUP), :][:, None, :]
        term = held_ref[pl.ds(group * GROUP * CHUNKS, GROUP * CHUNKS), :].reshape(
            GROUP, CHUNKS, LANES
        )
        term = term * (coef * decay)
        for place in range(width):
            mixed_ref[place * CHUNKS : (place + 1) * CHUNKS, :] += jnp.sum(term, axis=0)
            if place < width - 1:
                term = term * decay
        return unused

    lax.fori_loop(0, states // GROUP, body, 0)


def backward_states(width, grads_ref, rate_ref, sums_ref, first_ref, decay_ref):
    states = rate_ref.shape[0]
    decay_ref[...] = jnp.exp(-rate_ref[...])

    def body(group, unused):
        running = state_sums(
            width, grads_ref, decay_ref, None, group, range(width - 1, -1, -1), None, True
        )
        sums_ref[pl.ds(group * GROUP * CHUNKS, GROUP * CHUNKS), :] = running.reshape(-1, LANES)
        return unused

    lax.fori_loop(0, states // GROUP, body, 0)
    hop = jnp.exp(-width * rate_ref[...])
    held = jnp.zeros((states, LANES), jnp.float32)
    for chunk in range(CHUNKS - 1, -1, -1):
        held = hop * held + sums_ref[chunk_rows(chunk, states), :]
    first_ref[...] = held


def backward_near(
    width,
    grads_ref,
    rows_ref,
    sums_ref,
    entering_ref,
    rate_ref,
    skip_ref,
    kernel_ref,
    back_ref,
    coef_grad_ref,
    rate_grad_ref,
    decay_ref,
    hop_ref,
    taps_ref,
    after_ref,
    lag_ref,
):
    states = rate_ref.shape[0]
    hop = jnp.exp(-width * rate_ref[...])
    hop_ref[...] = hop
    held = entering_ref[...]
    for chunk in range(CHUNKS - 1, -1, -1):
        after_ref[chunk_rows(chunk, states), :] = held
        held = hop * held + sums_ref[chunk_rows(chunk, states), :]
    for lag in range(width):
        taps_ref[lag * CHUNKS : (lag + 1) * CHUNKS, :] = jnp.broadcast_to(
            kernel_ref[lag : lag + 1, :], (CHUNKS, LANES)
        )
    for start in range(0, width, 4):
        sums = [skip_ref[...] * block(grads_ref, start + i) for i in range(4)]
        for place in range(start, width):
            grads = block(grads_ref, place)
            for i in range(4):
                if place >= start + i:
                    sums[i] = sums[i] + block(taps_ref, place - start - i) * grads
        for i in range(4):
            back_ref[(start + i) * CHUNKS : (start + i + 1) * CHUNKS, :] = sums[i]
    for start in range(0, width, 4):
        sums = [jnp.zeros((CHUNKS, LANES), jnp.float32) for i in range(4)]
        for place in range(start, width):
            grads = block(grads_ref, place)
            for i in range(4):
                if place >= start + i:
                    sums[i] = sums[i] + block(rows_ref, place - start - i) * grads
        for i in range(4):
            lag_ref[start + i : start + i + 1, :] = jnp.sum(sums[i], axis=0, keepdims=True)
    decay_all = decay_ref[...]
    near_coef = jnp.zeros((states, LANES), jnp.float32)
    near_rate = jnp.zeros((states, LANES), jnp.float32)
    for lag in range(width - 1, -1, -1):
        near_coef = near_coef * decay_all + lag_ref[lag : lag + 1, :]
        near_rate = near_rate * decay_all + float(lag) * lag_ref[lag : lag + 1, :]
    coef_grad_ref[...] = near_coef
    rate_grad_ref[...] = near_rate


def backward_far(
    width,
    grads_ref,
    rows_ref,
    sums_ref,
    held_ref,
    coef_ref,
    back_ref,
    coef_grad_ref,
    rate_grad_ref,
    decay_ref,
    hop_ref,
    after_ref,
    groups,
):
    def body(group, unused):
        members = pl.ds(group * GROUP, GROUP)
        cells = pl.ds(group * GROUP * CHUNKS, GROUP * CHUNKS)
        cube = (GROUP, CHUNKS, LANES)
        decay = decay_ref[members, :][:, None, :]
        coef = coef_ref[members, :][:, None, :]
        after = after_ref[cells, :].reshape(cube)
        term = after * coef
        for place in range(width - 1, -1, -1):
            back_ref[place * CHUNKS : (place + 1) * CHUNKS, :] += jnp.sum(term, axis=0)
            if place > 0:
                term = term * decay
        held = held_ref[cells, :].reshape(cube)
        coef_grad_ref[members, :] += jnp.sum(held * sums_ref[cells, :].reshape(cube), axis=1)
        slope = state_sums(
            width,
            rows_ref,
            decay_ref,
            None,
            group,
            range(width),
            lambda place: float(width - 1 - place),
            False,
        )
        total = after * (float(width) * hop_ref[members, :][:, None, :] * held + slope)
        slope = state_sums(
            width,
            grads_ref,
            decay_ref,
            None,
            group,
            range(width - 1, -1, -1),
            lambda place: float(place + 1),
            True,
        )
        total = total + held * slope
        rate_grad_ref[members, :] += jnp.sum(total, axis=1)
        return unused

    lax.fori_loop(groups.start, groups.stop, body, 0)


MESH = pl.DeviceIdType.MESH


def add_rows(out_ref, out_start, a_ref, a_start, b_ref, b_start, rows):
    columns = out_ref.shape[1]
    size = 8
    for option in (16, 24, 32, 48, 64):
        if rows % option == 0 and option * columns <= 64 * 1024:
            size = option

    def body(i, unused):
        at = i * size
        out_ref[pl.ds(pl.multiple_of(out_start + at, 8), size), :] = (
            a_ref[pl.ds(pl.multiple_of(a_start + at, 8), size), :]
            + b_ref[pl.ds(pl.multiple_of(b_start + at, 8), size), :]
        )
        return unused

    lax.fori_loop(0, rows // size, body, 0)


class Lane:
    def __init__(self, rows, columns, bits, line_first, in_place):
        self.rows, self.columns = rows, columns
        self.bits, self.line_first, self.in_place = bits, line_first, in_place

    def buffers(self, line):
        half = self.rows // 2
        unit = half // line if self.line_first else half >> len(self.bits)
        counts = [half]
        size = half // line if self.line_first else half
        for unused in self.bits:
            size //= 2
            counts.append(size)
        counts.append(unit * (line + 1 if self.line_first else max(1, line // 2)))
        return [pltpu.VMEM((count, self.columns), jnp.float32) for count in counts]

    def copies(self, line):
        chain = 4 * line + 3 if self.line_first else line
        return 4 + 2 * len(self.bits) + chain


def lane_steps(
    lane, line, source, target, buffers, stages, semaphores, first_sem, pending
):
    send_sems, recv_sems, free_sems = semaphores
    first, chain = buffers[0], buffers[-1]
    landing = buffers[1:-1]
    acc = source if lane.in_place else first
    me = lax.axis_index("seq")
    z = lax.axis_index("batch")
    half = lane.rows // 2
    core = me % 2
    counter = [first_sem]

    def fresh():
        counter[0] += 1
        return counter[0] - 1

    def remote(src, dst, index, device):
        return pltpu.make_async_remote_copy(
            src_ref=src,
            dst_ref=dst,
            send_sem=send_sems.at[index],
            recv_sem=recv_sems.at[index],
            device_id=device,
            device_id_type=MESH,
        )

    def rows_of(ref, start, count):
        if not isinstance(start, int):
            start = pl.multiple_of(start, 8)
        return ref.at[pl.ds(start, count), :]

    def side(bit):
        return (me // bit) % 2

    def partner(bit):
        return (me + bit * (1 - 2 * side(bit)), z)

    def free(index, device):
        pl.semaphore_signal(
            free_sems.at[index], inc=1, device_id=device, device_id_type=MESH
        )

    def wait_free(index):
        pl.semaphore_wait(free_sems.at[index], 1)

    mine, other = core * half, (1 - core) * half
    base_row = mine if lane.in_place else 0
    swap = remote(rows_of(source, other, half), first, fresh(), partner(1))

    def load():
        place = len(stages) - 1 if lane.stage is None else lane.stage
        return pltpu.make_async_copy(rows_of(source, mine, half), *stages[place])

    def begin():
        swap.start()
        if not lane.in_place and lane.stage is not None:
            load().start()

    def add_swap():
        if lane.in_place:
            swap.wait_recv()
            add_rows(acc, mine, acc, mine, first, 0, half)
        else:
            if lane.stage is None:
                load().start()
            swap.wait_recv()
            load().wait()
            add_rows(acc, 0, acc, 0, stages[-1 if lane.stage is None else lane.stage][0], 0, half)

    pending.append(swap.wait_send)
    steps = [[begin], [add_swap]]

    def join(function):
        steps[-1].append(function)

    def step(function):
        steps.append([function])

    def neighbours_sum(base, size):
        starts, indices = [base], []
        for place, bit in enumerate(lane.bits):
            size //= 2
            start, index = starts[-1], fresh()
            copy = remote(
                rows_of(acc, base_row + start + (1 - side(bit)) * size, size),
                landing[place],
                index,
                partner(bit),
            )
            own = start + side(bit) * size
            join(copy.start)

            def receive(copy=copy, own=own, size=size, place=place, bit=bit, index=index):
                copy.wait()
                free(index, partner(bit))
                add_rows(acc, base_row + own, acc, base_row + own, landing[place], 0, size)

            step(receive)
            starts.append(own)
            indices.append(index)
        return starts, size, indices

    def neighbours_spread(starts, size, indices):
        for place in range(len(lane.bits) - 1, -1, -1):
            rows = rows_of(acc, base_row + starts[place + 1], size)
            copy = remote(rows, rows, fresh(), partner(lane.bits[place]))
            join(functools.partial(wait_free, indices[place]))
            join(copy.start)
            pending.append(copy.wait_send)
            step(copy.wait_recv)
            size *= 2

    if not lane.line_first:
        starts, size, indices = neighbours_sum(0, half)
        at = starts[-1]
        depth = jnp.minimum(z, line - 1 - z)
        lower = z < line // 2
        inward = (me, jnp.where(lower, z + 1, z - 1))
        outward = (me, jnp.where(lower, z - 1, z + 1))
        across = (me, line - 1 - z)
        middle = line // 2 - 1

        def on(level, function):
            def guarded():
                pl.when(depth == level)(function)

            return guarded

        passed = []
        for level in range(middle):
            rows = rows_of(acc, base_row + at, size)
            passed.append(fresh())
            copy = remote(rows, rows_of(chain, level * size, size), passed[-1], inward)
            join(on(level, copy.start))

            def receive(copy=copy, level=level):
                copy.wait_recv()
                add_rows(acc, base_row + at, acc, base_row + at, chain, level * size, size)

            def release(copy=copy, index=passed[-1]):
                copy.wait_send()
                free(index, inward)

            step(on(level + 1, receive))
            join(on(level, release))
        rows = rows_of(acc, base_row + at, size)
        copy = remote(rows, rows_of(chain, middle * size, size), fresh(), across)
        join(on(middle, copy.start))

        def receive_across(copy=copy):
            copy.wait()
            add_rows(acc, base_row + at, acc, base_row + at, chain, middle * size, size)

        step(on(middle, receive_across))
        for level in range(middle - 1, -1, -1):
            rows = rows_of(acc, base_row + at, size)
            copy = remote(rows, rows, fresh(), outward)
            join(on(level + 1, functools.partial(wait_free, passed[level])))
            join(on(level + 1, copy.start))
            pending.append(on(level + 1, copy.wait_send))
            step(on(level, copy.wait_recv))
        neighbours_spread(starts, size, indices)
    else:
        unit = half // line
        slots = [fresh() for unused in range(line + 1)]
        outs = [[fresh() for unused in range(2)] for unused in range(line)]
        spreads = [fresh() for unused in range(line)]

        def on(place, function):
            def guarded():
                pl.when(z == place)(function)

            return guarded

        def beside(place):
            return (me, place - 1 if place > 0 else place + 1)

        def hop(place, member, step_to):
            slot = line if step_to < 0 and member == place - 1 else member
            return remote(
                rows_of(acc, base_row + member * unit, unit),
                rows_of(chain, slot * unit, unit),
                slots[slot],
                (me, place + step_to),
            )

        def arrived(place, slot, member):
            remote(
                rows_of(acc, base_row + member * unit, unit),
                rows_of(chain, slot * unit, unit),
                slots[slot],
                beside(place),
            ).wait_recv()
            row = base_row + member * unit
            add_rows(acc, row, acc, row, chain, slot * unit, unit)

        for turn in range(line - 1):

            def rightward(place=turn):
                for member in range(line - 1, place, -1):
                    if place > 0:
                        arrived(place, member, member)
                    hop(place, member, 1).start()

            def leftward(place=line - 1 - turn):
                for member in range(place):
                    if place < line - 1:
                        arrived(place, member, member)
                    hop(place, member, -1).start()

            if turn > 0:
                step(on(turn, rightward))
            else:
                join(on(turn, rightward))
            join(on(line - 1 - turn, leftward))

        to_right, to_left = fresh(), fresh()

        def collect(place):
            if place > 0:
                arrived(place, place, place)
            if place < line - 1:
                arrived(place, line, place)
            for member in range(line - 1, place, -1):
                hop(place, member, 1).wait_send()
            if place < line - 1:
                free(to_right, (me, place + 1))
            for member in range(place):
                hop(place, member, -1).wait_send()
            if place > 0:
                free(to_left, (me, place - 1))

        def collect_all():
            for place in range(line):
                on(place, functools.partial(collect, place))()

        step(collect_all)

        base = z * unit
        starts, size, indices = neighbours_sum(base, unit)
        neighbours_spread(starts, size, indices)

        def spread_at(place, distance, receive, send):
            members = {place - distance, place + distance}
            for member in sorted(members):
                if not 0 <= member < line:
                    continue
                if receive and distance > 0:
                    remote(
                        rows_of(acc, base_row + member * unit, unit),
                        rows_of(acc, base_row + member * unit, unit),
                        spreads[member],
                        beside(place),
                    ).wait_recv()
                if not send:
                    continue
                for step_to in (1, -1):
                    going = member <= place if step_to > 0 else member >= place
                    if going and 0 <= place + step_to < line:
                        yield member, step_to

        def pass_on(place, member, step_to):
            return pltpu.make_async_remote_copy(
                src_ref=rows_of(acc, base_row + member * unit, unit),
                dst_ref=rows_of(acc, base_row + member * unit, unit),
                send_sem=send_sems.at[outs[member][0 if step_to > 0 else 1]],
                recv_sem=recv_sems.at[spreads[member]],
                device_id=(me, place + step_to),
                device_id_type=MESH,
            )

        for distance in range(line):

            def forward(place, distance):
                if distance == 0 and place > 0:
                    wait_free(to_right)
                if distance == 0 and place < line - 1:
                    wait_free(to_left)
                for member, step_to in spread_at(place, distance, True, True):
                    pass_on(place, member, step_to).start()

            def forward_all(distance=distance):
                for place in range(line):
                    on(place, functools.partial(forward, place, distance))()

            if distance == 0:
                join(forward_all)
            else:
                step(forward_all)

        def gone(place):
            for distance in range(line):
                for member, step_to in spread_at(place, distance, False, True):
                    pass_on(place, member, step_to).wait_send()

        for place in range(line):
            pending.append(on(place, functools.partial(gone, place)))

    keep_index, give_index = fresh(), fresh()
    done = rows_of(acc, base_row, half)
    keep = pltpu.make_async_copy(done, rows_of(target, mine, half), recv_sems.at[keep_index])
    give = remote(done, rows_of(target, mine, half), give_index, partner(1))
    join(keep.start)
    join(give.start)
    pending.append(keep.wait)
    pending.append(give.wait)
    assert counter[0] - first_sem <= lane.copies(line)
    return steps


def turn_order(lengths, order):
    if [order.count(place) for place in range(len(lengths))] == lengths:
        return order
    last = len(lengths) - 1
    turns = range(max(lengths[:-1], default=0))
    lanes = [place for turn in turns for place in range(last) if turn < lengths[place]]
    return [last] * lengths[last] + lanes


class Loop:
    def __init__(self, count, *parts):
        self.count, self.parts = count, parts

    def steps(self):
        return self.count * len(self.parts)


def call_all(functions):
    for function in functions:
        function()


def run_loop(loop, between):
    parts = len(loop.parts)

    def body(i, unused):
        for place, part in enumerate(loop.parts):
            part(i)
            for turn in range(loop.count):
                functions = between[turn * parts + place]
                if functions:
                    pl.when(i == turn)(functools.partial(call_all, functions))
        return unused

    lax.fori_loop(0, loop.count, body, 0)


def give_stages(lanes, order, count):
    free, seen = list(range(count)), [0] * len(lanes)
    for place in order:
        if place == len(lanes) or lanes[place].in_place:
            continue
        seen[place] += 1
        lane = lanes[place]
        if seen[place] == 1:
            lane.stage = free.pop() if free else None
        elif seen[place] == 2 and lane.stage is not None:
            free.append(lane.stage)


class Runner:
    def __init__(self, lanes, programs, count, order):
        lengths = [len(program) for program in programs] + [count]
        self.programs = [list(program) for program in programs]
        self.order = turn_order(lengths, order)
        give_stages(lanes, self.order, STAGES)
        self.work_place = len(programs)
        self.at = 0

    def lanes(self):
        functions = []
        while self.at < len(self.order) and self.order[self.at] != self.work_place:
            functions += self.programs[self.order[self.at]].pop(0)
            self.at += 1
        return functions

    def run(self, work):
        for item in work:
            call_all(self.lanes())
            self.at += 1
            if not isinstance(item, Loop):
                item()
                continue
            between = []
            for unused in range(item.steps() - 1):
                between.append(self.lanes())
                self.at += 1
            run_loop(item, between + [[]])


def steps_in(work):
    return sum(item.steps() if isinstance(item, Loop) else 1 for item in work)


def state_exchange(bits, row_count, rate, totals, arrivals, entering, sends, receives, forward):
    me, z = lax.axis_index("seq"), lax.axis_index("batch")

    def copy(level):
        bit = bits[level]
        return pltpu.make_async_remote_copy(
            src_ref=totals[level],
            dst_ref=arrivals[level],
            send_sem=sends.at[level],
            recv_sem=receives.at[level],
            device_id=(me + bit * (1 - 2 * ((me // bit) % 2)), z),
            device_id_type=MESH,
        )

    def arrive(level):
        bit = bits[level]
        copy(level).wait_recv()
        place = me % bit
        after = (me // bit) % 2 == (1 if forward else 0)
        hops = (row_count * (place if forward else bit - 1 - place)).astype(jnp.float32)
        term = jnp.exp(-rate[...] * hops) * arrivals[level][...]
        term = jnp.where(after, term, 0.0)
        entering[...] = term if level == 0 else entering[...] + term
        if level + 1 < len(bits):
            far = jnp.exp(-float(row_count * bit) * rate[...])
            ours, theirs = totals[level][...], arrivals[level][...]
            totals[level + 1][...] = jnp.where(after, ours + far * theirs, theirs + far * ours)
            copy(level + 1).start()

    return copy, arrive


def lane_columns(tile):
    return pl.ds(pl.multiple_of(tile * LANES, LANES), LANES)


def row_block(i, count):
    return pl.ds(pl.multiple_of(i * count, count), count)


SKIP, GAIN_ONE, BIAS_ONE, GAIN_TWO, BIAS_TWO = range(5)


def vector(ref, place):
    return ref[place : place + 1, :]


class ForwardIn(NamedTuple):
    tokens: Any
    token_grads: Any
    skip: Any
    gain_one: Any
    bias_one: Any
    gain_two: Any
    bias_two: Any
    query_weight: Any
    key_weight: Any
    value_weight: Any
    out_weight: Any
    taps: Any
    rate: Any
    coef: Any


class ForwardOut(NamedTuple):
    product: Any
    held: Any
    kernel: Any
    values: Any
    keys_mixed: Any
    key_rows: Any
    queries: Any
    mixed: Any
    gated: Any
    middle: Any
    normed_two: Any
    standard_two: Any
    factor_two: Any
    normed_one: Any
    standard_one: Any
    factor_one: Any
    out_grad: Any
    vectors: Any


def forward_body(row_count, size, bits, *refs):
    width = row_count // CHUNKS
    levels = len(bits)
    taken, outs = len(ForwardIn._fields), len(ForwardOut._fields)
    given = ForwardIn(*refs[:taken])
    results = ForwardOut(*refs[taken : taken + outs])
    own = ForwardOut(*refs[taken + outs : taken + 2 * outs])
    refs = refs[taken + 2 * outs :]
    sums, taps, decay, entering, edge_out, edge_in = refs[:6]
    totals, arrivals = refs[6 : 6 + levels], refs[6 + levels : 6 + 2 * levels]
    sends, receives, keeps = refs[-3:]
    vectors = own.vectors
    rate, coef, skip = given.rate, given.coef, vectors.at[0:1]
    channels = rate.shape[1]
    tiles = channels // LANES
    tap_count = given.taps.shape[0]
    halo = tap_count - 1
    low = jnp.bfloat16
    me, z = lax.axis_index("seq"), lax.axis_index("batch")
    barrier = pltpu.get_barrier_semaphore()

    def greet(device):
        pl.semaphore_signal(barrier, inc=1, device_id=device, device_id_type=MESH)

    for bit in bits:
        greet((me + bit * (1 - 2 * ((me // bit) % 2)), z))
    pl.when(me > 0)(lambda: greet((me - 1, z)))
    pl.when(me < size - 1)(lambda: greet((me + 1, z)))

    kept = ForwardOut(
        *[
            pltpu.make_async_copy(own[i], results[i], keeps.at[i])
            for i in range(len(ForwardOut._fields))
        ]
    )

    copy, arrive = state_exchange(
        bits, row_count, rate, totals, arrivals, entering, sends, receives, True
    )

    def edge(device):
        return pltpu.make_async_remote_copy(
            src_ref=edge_out,
            dst_ref=edge_in,
            send_sem=sends.at[levels],
            recv_sem=receives.at[levels],
            device_id=(device, z),
            device_id_type=MESH,
        )

    def reordered(rows, i):
        shape = (128, row_count)
        row = i * 128 + lax.broadcasted_iota(jnp.int32, shape, 0)
        token = lax.rem(row, CHUNKS) * width + lax.div(row, CHUNKS)
        chosen = lax.broadcasted_iota(jnp.int32, shape, 1) == token
        picks = jnp.where(chosen, 1.0, 0.0).astype(low)
        return jnp.dot(picks, rows[...], preferred_element_type=jnp.float32)

    def norm_rows(i):
        rows = row_block(i, 128)
        inputs = reordered(given.tokens, i)
        own.middle[rows, :] = inputs
        standard, factor = standardize(inputs)
        own.standard_one[rows, :] = standard
        own.factor_one[rows, :] = jnp.broadcast_to(factor, (128, LANES))
        own.normed_one[rows, :] = (
            standard * vector(vectors, GAIN_ONE) + vector(vectors, BIAS_ONE)
        ).astype(low)

    def grad_rows(i):
        own.out_grad[row_block(i, 128), :] = reordered(given.token_grads, i).astype(low)

    def project_to(target, weight, lead):
        def body(i):
            cols = row_block(i, 256)
            target[lead : lead + row_count, cols] = jnp.dot(
                own.normed_one[...], weight[:, cols], preferred_element_type=jnp.float32
            )

        return Loop(channels // 256, body)

    lead = halo * CHUNKS

    def send_edge():
        edge_out[...] = jnp.zeros(edge_out.shape, jnp.float32)
        for i in range(halo):
            row = lead + (width - halo + i) * CHUNKS + CHUNKS - 1
            edge_out[i : i + 1, :] = own.key_rows[row : row + 1, :]
        pl.semaphore_wait(
            barrier, levels + jnp.where(me > 0, 1, 0) + jnp.where(me < size - 1, 1, 0)
        )
        pl.when(me < size - 1)(edge(me + 1).start)

        @pl.when(me == 0)
        def at_start():
            edge_in[...] = jnp.zeros(edge_in.shape, jnp.float32)

    def take_edge():
        pl.when(me > 0)(edge(me - 1).wait_recv)

    def states_tile(tile):
        here = lane_columns(tile)
        keys, tap = own.key_rows, given.taps
        for i in range(halo):
            row = lead + (width - halo + i) * CHUNKS
            rows = keys[row : row + CHUNKS, here]
            keys[i * CHUNKS : (i + 1) * CHUNKS, here] = jnp.concatenate(
                [edge_in[i : i + 1, here], rows[: CHUNKS - 1]], axis=0
            )
        total = tap[0:1, here] * keys[lead : lead + row_count, here]
        for offset in range(1, tap_count):
            start = lead - offset * CHUNKS
            total = total + tap[offset : offset + 1, here] * keys[start : start + row_count, here]
        own.keys_mixed[:, here] = total
        own.product[:, here] = total * own.values[:, here]
        forward_states(
            width,
            own.product.at[:, here],
            rate.at[:, here],
            sums.at[tile],
            totals[0].at[:, here],
            decay,
        )

    def near_tile(tile):
        here = lane_columns(tile)
        forward_near(
            width,
            own.product.at[:, here],
            rate.at[:, here],
            coef.at[:, here],
            skip.at[:, here],
            own.mixed.at[:, here],
            own.kernel.at[:, here],
            taps,
        )

    def far_tile(tile):
        here = lane_columns(tile)
        forward_far(
            width,
            sums.at[tile],
            entering.at[:, here],
            rate.at[:, here],
            coef.at[:, here],
            own.mixed.at[:, here],
            own.held.at[tile],
            decay,
        )

    def out_rows(i):
        rows = row_block(i, 128)
        gated = (own.queries[rows, :] * own.mixed[rows, :]).astype(low)
        own.gated[rows, :] = gated
        middle = own.middle[rows, :] + jnp.dot(
            gated, given.out_weight[...], preferred_element_type=jnp.float32
        )
        own.middle[rows, :] = middle
        standard, factor = standardize(middle)
        own.standard_two[rows, :] = standard
        own.factor_two[rows, :] = jnp.broadcast_to(factor, (128, LANES))
        own.normed_two[rows, :] = (
            standard * vector(vectors, GAIN_TWO) + vector(vectors, BIAS_TWO)
        ).astype(low)

    def loop(item, between=()):
        between = list(between)
        run_loop(item, between + [[]] * (item.steps() - len(between)))

    def keep_all(*copies):
        for one in copies:
            one.start()

    vectors[...] = jnp.zeros(vectors.shape, jnp.float32)
    singles = (given.skip, given.gain_one, given.bias_one, given.gain_two, given.bias_two)
    for place, single in enumerate(singles):
        vectors[place : place + 1, :] = single[...][None]
    keep_all(kept.vectors)
    loop(Loop(row_count // 128, norm_rows))
    keep_all(kept.standard_one, kept.factor_one, kept.normed_one)
    loop(project_to(own.key_rows, given.key_weight, lead))
    send_edge()
    loop(project_to(own.values, given.value_weight, 0))
    keep_all(kept.values)
    take_edge()
    loop(Loop(tiles, states_tile))
    copy(0).start()
    keep_all(kept.key_rows, kept.keys_mixed, kept.product)
    loop(project_to(own.queries, given.query_weight, 0))
    keep_all(kept.queries)
    loop(Loop(row_count // 128, grad_rows))
    keep_all(kept.out_grad)
    between = [[] for unused in range(tiles)]
    for level in range(levels):
        between[level * tiles // levels].append(functools.partial(arrive, level))
    loop(Loop(tiles, near_tile), between)
    keep_all(kept.kernel)
    loop(Loop(tiles, far_tile))
    keep_all(kept.mixed, kept.held)
    loop(Loop(row_count // 128, out_rows))
    keep_all(kept.gated, kept.middle, kept.normed_two, kept.standard_two, kept.factor_two)
    for level in range(levels):
        copy(level).wait_send()
    pl.when(me < size - 1)(edge(me + 1).wait_send)
    for one in kept:
        one.wait()


def forward(row_count, arrays):
    size = lax.axis_size("seq")
    bits = [1 << place for place in range(size.bit_length() - 1)]
    states, channels = arrays.rate.shape
    tiles, width = channels // LANES, row_count // CHUNKS
    halo = arrays.taps.shape[0] - 1
    full, low = jnp.float32, jnp.bfloat16
    square = ((row_count, channels), full)
    low_square = ((row_count, channels), low)
    thin = ((row_count, LANES), full)
    held = ((tiles, states * CHUNKS, LANES), full)
    outs = ForwardOut(
        product=square,
        held=held,
        kernel=((width, channels), full),
        values=square,
        keys_mixed=square,
        key_rows=((row_count + halo * CHUNKS, channels), full),
        queries=square,
        mixed=square,
        gated=low_square,
        middle=square,
        normed_two=low_square,
        standard_two=square,
        factor_two=thin,
        normed_one=low_square,
        standard_one=square,
        factor_one=thin,
        out_grad=low_square,
        vectors=((8, channels), full),
    )
    scratch = list(outs) + [held, thin, ((states, LANES), full), ((states, channels), full)]
    scratch += [((8, channels), full)] * 2 + [((states, channels), full)] * (2 * len(bits))
    counts = [len(bits) + 1, len(bits) + 1, len(outs)]
    found = pl.pallas_call(
        functools.partial(forward_body, row_count, size, bits),
        out_shape=[jax.ShapeDtypeStruct(*out) for out in outs],
        in_specs=[pl.BlockSpec(memory_space=pltpu.VMEM)] * len(ForwardIn._fields),
        out_specs=[pl.BlockSpec(memory_space=pltpu.HBM)] * len(outs),
        scratch_shapes=[pltpu.VMEM(*shape) for shape in scratch]
        + [pltpu.SemaphoreType.DMA((count,)) for count in counts],
        compiler_params=pltpu.CompilerParams(
            collective_id=1, has_side_effects=True, vmem_limit_bytes=VMEM_LIMIT
        ),
    )(*[getattr(arrays, name) for name in ForwardIn._fields])
    return ForwardOut(*found)


class BackwardIn(NamedTuple):
    up_weight: Any
    down_weight: Any
    out_weight: Any
    query_weight: Any
    key_weight: Any
    value_weight: Any
    product: Any
    held: Any
    values: Any
    keys_mixed: Any
    key_rows: Any
    queries: Any
    mixed: Any
    gated: Any
    middle: Any
    standard_two: Any
    factor_two: Any
    standard_one: Any
    factor_one: Any
    rate: Any
    coef: Any
    vectors: Any
    taps: Any
    kernel: Any
    out_grad: Any
    normed_one: Any
    normed_two: Any


FAR = 19


class Results(NamedTuple):
    down: Any
    up: Any
    out: Any
    query: Any
    value: Any
    key: Any
    small: Any
    tokens: Any
    mixed_out: Any
    own_down: Any
    own_up: Any
    own_out: Any


HIDDEN_AT_ONCE = 256
STAGES = 3


def gelu_pair(values):
    slope = math.sqrt(2.0 / math.pi)
    squared = values * values
    bent = jnp.tanh(slope * (values + 0.044715 * (values * squared)))
    half = 0.5 * (1.0 + bent)
    steep = 0.5 * values * (1.0 - bent * bent) * (slope * (1.0 + 3.0 * 0.044715 * squared))
    return values * half, half + steep


def backward_body(row_count, size, line, bits, lanes, order, *refs):
    width = row_count // CHUNKS
    given = BackwardIn(*refs[: len(BackwardIn._fields)])
    rest = list(refs[len(given) :])

    def take(count):
        taken = rest[:count]
        del rest[:count]
        return taken

    results = Results(*take(len(Results._fields)))
    semaphores = rest[-6:-3]
    load_sems, swap_send, swap_recv = rest[-3:]
    del rest[-6:]
    (grad_query, grad_value, grad_key, small) = take(4)
    (shifted, total, grad_middle) = take(3)
    (grad_queries, values_low, keys_low, weight) = take(4)
    (entering, edge_out, edge_in) = take(3)
    stages = [(ref, load_sems.at[20 + i]) for i, ref in enumerate(take(STAGES + 1))]
    levels = len(bits)
    totals, arrivals = take(levels), take(levels)

    me = lax.axis_index("seq")
    z = lax.axis_index("batch")
    channels = small.shape[1]
    tiles = channels // LANES
    rate, coef = given.rate, given.coef
    states = rate.shape[0]
    tap_count = given.taps.shape[0]
    halo = tap_count - 1
    hidden = given.up_weight.shape[1]
    low, full = jnp.bfloat16, jnp.float32
    misc = 2 * states

    barrier = pltpu.get_barrier_semaphore()

    def greet(device):
        pl.semaphore_signal(barrier, inc=1, device_id=device, device_id_type=MESH)

    for bit in bits:
        greet((me + bit * (1 - 2 * ((me // bit) % 2)), z))
    pl.when(z > 0)(lambda: greet((me, z - 1)))
    pl.when(z < line - 1)(lambda: greet((me, z + 1)))
    pl.when(me > 0)(lambda: greet((me - 1, z)))
    pl.when(me < size - 1)(lambda: greet((me + 1, z)))
    pl.semaphore_wait(
        barrier,
        len(bits)
        + jnp.where(z > 0, 1, 0)
        + jnp.where(z < line - 1, 1, 0)
        + jnp.where(me > 0, 1, 0)
        + jnp.where(me < size - 1, 1, 0),
    )

    def local(source, target, place):
        return pltpu.make_async_copy(source, target, load_sems.at[place])

    def fetch(*triples):
        copies = [local(*triple) for triple in triples]
        for copy in copies:
            copy.start()
        for copy in copies:
            copy.wait()

    def add_small(row, value):
        small[row : row + 1, :] += jnp.sum(value, axis=0, keepdims=True)

    exchange, arrive = state_exchange(
        bits, row_count, rate, totals, arrivals, entering, swap_send, swap_recv, False
    )

    def edge(device):
        return pltpu.make_async_remote_copy(
            src_ref=edge_out,
            dst_ref=edge_in,
            send_sem=swap_send.at[levels],
            recv_sem=swap_recv.at[levels],
            device_id=(device, z),
            device_id_type=MESH,
        )

    steps = hidden // HIDDEN_AT_ONCE
    per_block = channels // HIDDEN_AT_ONCE
    held_weight = local(given.out_weight, weight, 7)
    held_standard = local(given.standard_two, shifted.at[:row_count], 8)
    held_gated = local(given.gated, values_low, 9)
    held_middle = local(given.middle, total, 10)
    out_rows = local(keys_low, results.mixed_out, 10)

    def feed_forward(
        up_tile, down_tile, active, grad_low, slope, down_sum, up_sum, block_a, block_b, thin
    ):
        def weights(step):
            here = row_block(step, HIDDEN_AT_ONCE)
            slot = step % 2
            return (
                local(given.up_weight.at[:, here], up_tile.at[slot], slot),
                local(given.down_weight.at[here, :], down_tile.at[slot], 2 + slot),
            )

        def sums(step):
            part = step // per_block
            here = row_block(step % per_block, HIDDEN_AT_ONCE)
            return (
                local(down_sum, results.own_down.at[part, here, :], 4),
                local(up_sum, results.own_up.at[part, :, here], 5),
            )

        def start():
            for copy in weights(0):
                copy.start()
            for copy in (held_middle, held_weight, held_standard, held_gated):
                copy.start()
            small[...] = jnp.zeros(small.shape, full)
            grad_middle[...] = jnp.zeros(grad_middle.shape, full)
            held_middle.wait()

        def part_one(step):
            slot = step % 2
            for copy in weights(step):
                copy.wait()

            @pl.when(step + 1 < steps)
            def following():
                for copy in weights(step + 1):
                    copy.start()

            before = jnp.dot(
                given.normed_two[...], up_tile[slot], preferred_element_type=full
            )
            after, steep = gelu_pair(before)
            active[...] = after.astype(low)
            slope[...] = steep

        def part_two(step):
            slot = step % 2
            total[...] += jnp.dot(active[...], down_tile[slot], preferred_element_type=full)
            grads = project_back(given.out_grad[...], down_tile[slot])
            grad_low[...] = (grads * slope[...]).astype(low)

        def part_three(step):
            @pl.when(step > 0)
            def previous():
                for copy in sums(step - 1):
                    copy.wait()

            down_sum[...] = weight_grad(active[...], given.out_grad[...])
            up_sum[...] = weight_grad(given.normed_two[...], grad_low[...])
            for copy in sums(step):
                copy.start()

        def part_four(step):
            grad_middle[...] += project_back(grad_low[...], up_tile[step % 2])

        def finish():
            for copy in sums(steps - 1):
                copy.wait()
            keys_low[...] = total[...].astype(low)
            out_rows.start()
            held_standard.wait()
            held_weight.wait()
            held_gated.wait()
            out_rows.wait()

        def norm_two(i):
            rows = row_block(i, 128)
            fetch((given.factor_two.at[rows, :], thin, 11))
            grads, standard = grad_middle[rows, :], shifted[rows, :]
            add_small(misc + tap_count + 3, grads * standard)
            add_small(misc + tap_count + 4, grads)
            back = given.out_grad[rows, :].astype(full) + norm_back(
                grads, vector(given.vectors, GAIN_TWO), standard, thin[:, 0:1]
            )
            grad_middle[rows, :] = back
            keys_low[rows, :] = back.astype(low)

        def out_sum(i):
            here = row_block(i, 256)
            down_sum[...] = weight_grad(values_low[:, here], keys_low[...])
            fetch((down_sum, results.own_out.at[0, here, :], 4))

        def gate(i):
            rows = row_block(i, 128)
            fetch(
                (given.mixed.at[rows, :], block_a, 11),
                (given.queries.at[rows, :], block_b, 12),
            )
            grads = project_back(keys_low[rows, :], weight[...])
            grad_queries[rows, :] = (grads * block_a[...]).astype(low)
            total[rows, :] = grads * block_b[...]

        return [
            start,
            Loop(steps, part_one, part_two, part_three, part_four),
            finish,
            Loop(row_count // 128, norm_two),
            Loop(channels // 256, out_sum),
            Loop(row_count // 128, gate),
        ]

    def weight_sum(target, grads):
        def body(i):
            rows = row_block(i, 256)
            target[rows, :] = weight_grad(given.normed_one[:, rows], grads[...])

        return Loop(channels // 256, body)

    back = shifted

    def mixer(
        rows_tile, keys_tile, other, held_tile, back_tile, taps, sums, after, decay, hop, lag
    ):
        def tile_loads(tile):
            here, slot = lane_columns(tile), tile % 2
            return (
                local(given.product.at[:, here], rows_tile.at[slot], 10 + slot),
                local(given.held.at[tile], held_tile.at[slot], 12 + slot),
                local(given.values.at[:, here], other.at[slot, pl.ds(0, row_count)], 14 + slot),
                local(given.keys_mixed.at[:, here], keys_tile.at[slot], 16 + slot),
            )

        def key_loads(tile):
            slot = tile % 2
            return local(given.key_rows.at[:, lane_columns(tile)], other.at[slot], 14 + slot)

        def first_tile(tile):
            here = lane_columns(tile)
            backward_states(
                width,
                total.at[:, here],
                rate.at[:, here],
                sums.at[tile],
                totals[0].at[:, here],
                decay,
            )

        def start_tiles():
            for copy in tile_loads(0):
                copy.start()
            exchange(0).start()

        def near(tile):
            here, slot = lane_columns(tile), tile % 2
            for copy in tile_loads(tile):
                copy.wait()

            @pl.when(tile + 1 < tiles)
            def following():
                for copy in tile_loads(tile + 1):
                    copy.start()

            decay[...] = jnp.exp(-rate[:, here])
            backward_near(
                width,
                total.at[:, here],
                rows_tile.at[slot],
                sums.at[tile],
                entering.at[:, here],
                rate.at[:, here],
                given.vectors.at[0:1, here],
                given.kernel.at[:, here],
                back_tile,
                small.at[0:states, here],
                small.at[states:misc, here],
                decay,
                hop,
                taps,
                after,
                lag,
            )

        def far(half):
            def part(tile):
                here, slot = lane_columns(tile), tile % 2
                groups = states // GROUP // 2
                backward_far(
                    width,
                    total.at[:, here],
                    rows_tile.at[slot],
                    sums.at[tile],
                    held_tile.at[slot],
                    coef.at[:, here],
                    back_tile,
                    small.at[0:states, here],
                    small.at[states:misc, here],
                    decay,
                    hop,
                    after,
                    range(half * groups, (half + 1) * groups),
                )

            return part

        def end(tile):
            here, slot = lane_columns(tile), tile % 2
            row = misc + tap_count
            small[row : row + 1, here] = jnp.sum(
                total[:, here] * rows_tile[slot], axis=0, keepdims=True
            )
            small[states:misc, here] = -coef[:, here] * small[states:misc, here]
            shifted[0:row_count, here] = back_tile[...] * other[slot, 0:row_count, :]
            values_low[:, here] = (back_tile[...] * keys_tile[slot]).astype(low)

        held_ones = local(given.standard_one, total, 7)
        held_factor = local(given.factor_one, back_tile, 8)

        def send_edge():
            key_loads(0).start()
            held_ones.start()
            held_factor.start()
            edge_out[...] = jnp.zeros(edge_out.shape, full)
            for place in range(halo):
                row = place * CHUNKS
                edge_out[place : place + 1, :] = shifted[row : row + 1, :]
            pl.when(me > 0)(edge(me - 1).start)

            @pl.when(me == size - 1)
            def at_end():
                edge_in[...] = jnp.zeros(edge_in.shape, full)

        def take_edge():
            pl.when(me < size - 1)(edge(me + 1).wait_recv)

        def keys_part(tile):
            here, slot = lane_columns(tile), tile % 2
            key_loads(tile).wait()

            @pl.when(tile + 1 < tiles)
            def following():
                key_loads(tile + 1).start()

            for place in range(halo):
                rows = shifted[place * CHUNKS : (place + 1) * CHUNKS, here]
                start = row_count + place * CHUNKS
                shifted[start : start + CHUNKS, here] = jnp.concatenate(
                    [rows[1:], edge_in[place : place + 1, here]], axis=0
                )
            tap = given.taps
            sum_rows = tap[0:1, here] * shifted[0:row_count, here]
            for offset in range(1, tap_count):
                start = offset * CHUNKS
                sum_rows = sum_rows + tap[offset : offset + 1, here] * (
                    shifted[start : start + row_count, here]
                )
            keys_low[:, here] = sum_rows.astype(low)
            grads = shifted[0:row_count, here]
            for offset in range(tap_count):
                start = (halo - offset) * CHUNKS
                small[misc + offset : misc + offset + 1, here] = jnp.sum(
                    grads * other[slot, start : start + row_count, :], axis=0, keepdims=True
                )

        def back_sum(index, grads):
            def body(i):
                rows = row_block(i, 128)
                term = project_back(grads[rows, :], weight[...])
                back[rows, :] = term if index == 0 else back[rows, :] + term

            return Loop(row_count // 128, body)

        def before_norm():
            held_ones.wait()
            held_factor.wait()

        def norm_one(i):
            rows = row_block(i, ROWS_AT_ONCE)
            grads, standard = back[rows, :], total[rows, :]
            add_small(misc + tap_count + 1, grads * standard)
            add_small(misc + tap_count + 2, grads)
            grad_middle[rows, :] += norm_back(
                grads, vector(given.vectors, GAIN_ONE), standard, back_tile[rows, 0:1]
            )

        tokens_out = local(grad_middle, results.tokens, 9)
        work = [Loop(tiles, first_tile), start_tiles]
        work.append(weight_sum(grad_query, grad_queries))
        for level in range(levels):
            work.append(functools.partial(arrive, level))
        work.append(Loop(tiles, near, far(0), far(1), end))
        work.append(send_edge)
        work.append(weight_sum(grad_value, values_low))
        work.append(take_edge)
        work.append(Loop(tiles, keys_part))
        work.append(weight_sum(grad_key, keys_low))
        chain = (
            (given.query_weight, grad_queries),
            (given.key_weight, keys_low),
            (given.value_weight, values_low),
        )
        for index, (source, grads) in enumerate(chain):
            work.append(functools.partial(fetch, (source, weight, 0)))
            work.append(back_sum(index, grads))
        work.append(before_norm)
        work.append(Loop(row_count // ROWS_AT_ONCE, norm_one))
        work.append(tokens_out.start)
        work.append(tokens_out.wait)
        return work

    def block_of(lane):
        cols = pl.ds(lane.column, lane.columns)
        if lane.array == 0:
            target = results.down.at[pl.ds(lane.part * channels, channels), cols]
            return results.own_down.at[lane.part, :, cols], target
        if lane.array == 1:
            target = results.up.at[:, pl.ds(lane.part * channels + lane.column, lane.columns)]
            return results.own_up.at[lane.part, :, cols], target
        if lane.array == 2:
            return results.own_out.at[0, :, cols], results.out.at[:, cols]
        source = (grad_query, grad_value, grad_key, small)[lane.array - 3]
        return source.at[:, cols], results[lane.array].at[:, cols]

    pending = [exchange(level).wait_send for level in range(levels)]
    pending.append(lambda: pl.when(me > 0)(edge(me - 1).wait_send))
    programs = []
    start = 0
    for lane in lanes:
        source, target = block_of(lane)
        programs.append(
            lane_steps(
                lane,
                line,
                source,
                target,
                take(len(lane.buffers(line))),
                stages,
                semaphores,
                start,
                pending,
            )
        )
        start += lane.copies(line)

    def vmem(*shape, kind=full):
        return pltpu.VMEM(shape, kind)

    count = work_steps(row_count, channels, hidden, levels)
    runner = Runner(lanes, programs, count, order)
    done = [0]

    def run(make):
        def scoped(*refs):
            work = make(*refs)
            done[0] += steps_in(work)
            runner.run(work)

        return scoped

    pl.run_scoped(
        run(feed_forward),
        vmem(2, channels, HIDDEN_AT_ONCE, kind=low),
        vmem(2, HIDDEN_AT_ONCE, channels, kind=low),
        vmem(row_count, HIDDEN_AT_ONCE, kind=low),
        vmem(row_count, HIDDEN_AT_ONCE, kind=low),
        vmem(row_count, HIDDEN_AT_ONCE),
        vmem(HIDDEN_AT_ONCE, channels),
        vmem(channels, HIDDEN_AT_ONCE),
        vmem(128, channels),
        vmem(128, channels),
        vmem(128, LANES),
    )
    cells = states * CHUNKS
    pl.run_scoped(
        run(mixer),
        vmem(2, row_count, LANES),
        vmem(2, row_count, LANES),
        vmem(2, row_count + halo * CHUNKS, LANES),
        vmem(2, cells, LANES),
        vmem(row_count, LANES),
        vmem(row_count, LANES),
        vmem(tiles, cells, LANES),
        vmem(cells, LANES),
        vmem(states, LANES),
        vmem(states, LANES),
        vmem(width, LANES),
    )
    assert done[0] == count
    call_all(runner.lanes())
    call_all(pending)


def work_steps(row_count, channels, hidden, levels):
    tiles, weights = channels // LANES, channels // 256
    first = 2 + 4 * (hidden // HIDDEN_AT_ONCE) + 2 * (row_count // 128) + weights
    second = 6 * tiles + 3 * weights + levels + 6 + 3 * (row_count // 128)
    return first + second + row_count // ROWS_AT_ONCE + 3


def backward(row_count, arrays, plan, order):
    size, line = lax.axis_size("seq"), lax.axis_size("batch")
    bits = [1 << place for place in range(size.bit_length() - 1)]
    channels, hidden = arrays.up_weight.shape
    states = arrays.rate.shape[0]
    tap_count = arrays.taps.shape[0]
    misc_rows = 2 * states + tap_count + 5
    small_rows = misc_rows + -misc_rows % (8 * size)
    full, low = jnp.float32, jnp.bfloat16
    parts = hidden // channels
    lanes = []
    for index, pieces in enumerate(plan):
        columns = channels if index == 6 else channels // 2
        for piece, (flipped, line_first) in enumerate(pieces):
            rows = small_rows if index == 6 else channels
            if rows % (8 * size * line):
                line_first = False
            path = bits[:0:-1] if flipped else bits[1:]
            lane = Lane(rows, columns, path, line_first, index > 2)
            lane.array, lane.part, lane.column = index, piece // 2, piece % 2 * columns
            lanes.append(lane)
    square = ((channels, channels), full)
    wide = ((row_count, channels), full)
    low_wide = ((row_count, channels), low)
    small = ((small_rows, channels), full)
    key_rows = arrays.key_rows.shape[0]
    one = ((states, channels), full)
    scratch = [square] * 3 + [small, ((key_rows, channels), full), wide, wide]
    scratch += [low_wide] * 3 + [((channels, channels), low)]
    scratch += [one] + [((8, channels), full)] * 2 + [((channels // 2, channels // 2), full)] * (STAGES + 1)
    scratch += [one] * (2 * len(bits))
    scratch = [pltpu.VMEM(*shape) for shape in scratch]
    scratch += [buffer for lane in lanes for buffer in lane.buffers(line)]
    copies = sum(lane.copies(line) for lane in lanes)
    counts = [21 + STAGES, len(bits) + 1, len(bits) + 1]
    outs = [((hidden, channels), full), ((channels, hidden), full)] + [square] * 4
    outs += [small, wide, low_wide]
    outs += [((parts, channels, channels), full)] * 2 + [((1, channels, channels), full)]
    found = pl.pallas_call(
        functools.partial(backward_body, row_count, size, line, bits, lanes, order),
        out_shape=[jax.ShapeDtypeStruct(*out) for out in outs],
        in_specs=[pl.BlockSpec(memory_space=pltpu.HBM)] * FAR
        + [pl.BlockSpec(memory_space=pltpu.VMEM)] * (len(BackwardIn._fields) - FAR),
        out_specs=[pl.BlockSpec(memory_space=pltpu.HBM)] * len(outs),
        scratch_shapes=scratch
        + [pltpu.SemaphoreType.DMA((copies,)), pltpu.SemaphoreType.DMA((copies,))]
        + [pltpu.SemaphoreType.REGULAR((copies,))]
        + [pltpu.SemaphoreType.DMA((count,)) for count in counts],
        compiler_params=pltpu.CompilerParams(
            collective_id=0, has_side_effects=True, vmem_limit_bytes=VMEM_LIMIT
        ),
    )(*[getattr(arrays, name) for name in BackwardIn._fields])
    return Results(*found)


def finish_body(row_count, states, tap_count, *refs):
    width = row_count // CHUNKS
    count = 9
    sources, targets = Results(*refs[:count], None, None, None), refs[count:]
    large, (mixed_out, tokens) = targets[:6], targets[6:8]
    (taps, coef, rate, skip, gain_one, bias_one, gain_two, bias_two) = targets[8:16]
    held_small, held_mixed, held_tokens, load_sems, store_sems = targets[16:21]
    passing = targets[21:]
    tiles = held_tokens.shape[0]
    pairs = [(sources.small, held_small), (sources.mixed_out, held_mixed)]
    for tile in range(tiles):
        pairs.append((sources.tokens.at[:, pl.ds(tile * LANES, LANES)], held_tokens.at[tile]))
    loads, stores = [], []
    for source, held, target in zip(sources[:6], passing, large):
        size = PASSING_SIZE // target.shape[1]
        for start in range(0, target.shape[0], size):
            rows = pl.ds(start, size)
            stores.append((held.at[rows, :], target.at[rows, :]))
            loads.append((source.at[rows, :], held.at[rows, :]))
    stores = [pltpu.make_async_copy(*pair, store_sems.at[i]) for i, pair in enumerate(stores)]
    copies = [pltpu.make_async_copy(*pair, load_sems.at[i]) for i, pair in enumerate(pairs + loads)]
    first_large = len(pairs)
    for copy in copies[first_large:] + copies[:first_large]:
        copy.start()
    moves = list(zip(copies[first_large:], stores))

    def move(some):
        for load, store in some:
            load.wait()
            store.start()

    move(moves[: len(moves) // 2])
    copies[0].wait()
    misc = 2 * states
    first = misc + tap_count
    coef[...] = held_small[0:states, :]
    rate[...] = held_small[states:misc, :]
    taps[...] = held_small[misc:first, :]
    for row, target in enumerate((skip, gain_one, bias_one, gain_two, bias_two)):
        target[...] = held_small[first + row, :]
    for copy in copies[1:first_large]:
        copy.wait()

    def body(chunk, unused):
        rows = row_block(chunk, width)
        for tile in range(tiles):
            tokens[rows, tile * LANES : (tile + 1) * LANES] = held_tokens.at[tile][
                pl.ds(chunk, width, stride=CHUNKS), :
            ]
        return unused

    lax.fori_loop(0, CHUNKS, body, 0)
    token = lax.broadcasted_iota(jnp.int32, (128, row_count), 0)
    row = lax.broadcasted_iota(jnp.int32, (128, row_count), 1)
    for i in range(row_count // 128):
        at = token + i * 128
        chosen = row == lax.rem(at, width) * CHUNKS + lax.div(at, width)
        picks = jnp.where(chosen, 1.0, 0.0).astype(jnp.bfloat16)
        mixed_out[i * 128 : (i + 1) * 128, :] = jnp.dot(
            picks, held_mixed[...], preferred_element_type=jnp.float32
        ).astype(jnp.bfloat16)
    move(moves[len(moves) // 2 :])
    for store in stores:
        store.wait()


PASSING_SIZE = 384 * 768


def finish(row_count, states, tap_count, found):
    channels = found.small.shape[1]
    full = jnp.float32
    wide = (row_count, channels)
    shapes = [(array.shape, full) for array in found[:6]]
    shapes += [(wide, jnp.bfloat16), (wide, full), ((tap_count, channels), full)]
    shapes += [((states, channels), full)] * 2 + [((channels,), full)] * 5
    tiles = channels // LANES
    scratch = [(found.small.shape, full), (wide, jnp.bfloat16), ((tiles, row_count, LANES), full)]
    pieces = sum(array.size // PASSING_SIZE for array in found[:6])
    counts = [2 + tiles + pieces, pieces]
    memory = [pltpu.HBM] * 6 + [pltpu.VMEM] * 10
    return pl.pallas_call(
        functools.partial(finish_body, row_count, states, tap_count),
        out_shape=[jax.ShapeDtypeStruct(*shape) for shape in shapes],
        in_specs=[pl.BlockSpec(memory_space=pltpu.HBM)] * 9,
        out_specs=[pl.BlockSpec(memory_space=space) for space in memory],
        scratch_shapes=[pltpu.VMEM(*shape) for shape in scratch]
        + [pltpu.SemaphoreType.DMA((count,)) for count in counts]
        + [pltpu.VMEM(array.shape, full) for array in found[:6]],
        compiler_params=pltpu.CompilerParams(vmem_limit_bytes=VMEM_LIMIT),
    )(*found[:9])


PLAN = [
    [(True, False), (True, True), (True, True), (True, False), (True, False), (False, True), (True, False), (False, False)],
    [(True, False), (True, True), (False, False), (False, False), (False, True), (True, True), (True, False), (False, False)],
    [(False, True), (False, False)],
    [(True, False), (False, False)],
    [(True, False), (True, False)],
    [(False, True), (False, False)],
    [(False, False)],
]
ORDER = [
    25, 25, 25, 25, 25, 25, 25, 25, 25, 25, 25, 25, 8, 25, 25, 25, 25, 0, 9, 1, 25, 25, 8, 25,
    25, 25, 0, 25, 9, 1, 25, 25, 10, 25, 25, 25, 25, 3, 11, 25, 25, 8, 10, 25, 25, 3, 25, 25, 9,
    11, 25, 25, 8, 12, 25, 0, 25, 25, 25, 4, 13, 5, 25, 12, 9, 25, 25, 25, 4, 10, 25, 1, 13, 3,
    5, 25, 9, 25, 25, 14, 25, 25, 7, 1, 15, 11, 8, 6, 25, 4, 14, 0, 7, 25, 1, 8, 10, 3, 15, 9,
    12, 6, 25, 4, 25, 8, 11, 25, 12, 25, 25, 16, 7, 25, 13, 1, 14, 12, 25, 16, 25, 15, 25, 9,
    13, 6, 25, 8, 1, 5, 7, 25, 13, 25, 12, 15, 0, 9, 14, 5, 25, 25, 8, 1, 10, 6, 25, 0, 12, 13,
    3, 5, 25, 25, 9, 25, 25, 18, 4, 19, 2, 17, 1, 10, 25, 12, 13, 5, 11, 0, 18, 3, 19, 2, 5, 17,
    25, 12, 16, 13, 4, 18, 10, 5, 0, 7, 3, 11, 25, 25, 13, 15, 19, 25, 10, 25, 16, 4, 14, 25,
    25, 11, 6, 25, 25, 0, 9, 7, 18, 25, 25, 16, 1, 19, 5, 25, 3, 25, 15, 11, 25, 25, 7, 25, 14,
    25, 10, 25, 6, 25, 12, 4, 3, 25, 9, 16, 7, 25, 25, 13, 15, 25, 1, 25, 18, 14, 11, 25, 4, 25,
    16, 25, 19, 6, 25, 25, 25, 21, 20, 2, 17, 15, 5, 12, 16, 7, 25, 25, 21, 25, 20, 9, 25, 18,
    14, 25, 25, 25, 13, 25, 19, 6, 25, 25, 22, 23, 25, 1, 25, 25, 21, 25, 25, 22, 25, 23, 15,
    25, 25, 25, 16, 25, 25, 12, 5, 20, 25, 25, 25, 21, 25, 25, 18, 25, 25, 22, 25, 25, 25, 25,
    13, 25, 14, 25, 25, 25, 23, 22, 19, 24, 2, 17, 20, 24, 16, 6, 21, 18, 5, 23, 17, 24, 22, 19,
    20, 21, 2, 22, 23, 17, 16, 18, 20, 24, 21, 19, 2, 22, 23, 24, 17, 22, 21, 2, 24, 16, 22, 17,
    2, 20, 23, 24, 21, 2, 17, 22, 23, 20, 24, 2, 22, 2, 23, 20, 22, 24, 2,
]


def on_device(
    tokens,
    norm1_gain,
    norm1_bias,
    query_weight,
    key_weight,
    value_weight,
    shift_taps,
    ssm_coef,
    ssm_rate,
    ssm_skip,
    out_weight,
    norm2_gain,
    norm2_bias,
    up_weight,
    down_weight,
    out_grad,
):
    unused, row_count, channels = tokens.shape
    states = ssm_rate.shape[0]
    tap_count = shift_taps.shape[0]

    arrays = SimpleNamespace(
        tokens=tokens[0],
        token_grads=out_grad[0],
        skip=ssm_skip,
        gain_one=norm1_gain,
        bias_one=norm1_bias,
        gain_two=norm2_gain,
        bias_two=norm2_bias,
        query_weight=query_weight,
        key_weight=key_weight,
        value_weight=value_weight,
        out_weight=out_weight,
        up_weight=up_weight,
        down_weight=down_weight,
        taps=shift_taps,
        rate=ssm_rate,
        coef=ssm_coef,
    )
    vars(arrays).update(forward(row_count, arrays)._asdict())
    found = backward(row_count, arrays, PLAN, ORDER)
    (down, up, out, query, value, key, mixed_out, grad_tokens, *rest) = finish(
        row_count, states, tap_count, found
    )
    (taps, coef, rate, skip, gain_one, bias_one, gain_two, bias_two) = rest
    return (
        mixed_out[None],
        grad_tokens[None],
        gain_one,
        bias_one,
        query,
        key,
        value,
        taps,
        coef,
        rate,
        skip,
        out,
        gain_two,
        bias_two,
        up,
        down,
    )


def solution(mesh):
    placed = (P("batch", "seq", None),) + (P(),) * 14 + (P("batch", "seq", None),)
    return jax.shard_map(
        on_device,
        mesh=mesh,
        in_specs=placed,
        out_specs=(P("batch", "seq", None),) * 2 + (P(),) * 14,
        check_vma=False,
    )
```

```python
import functools
import math
from types import SimpleNamespace
from typing import Any, NamedTuple

import jax
import jax.numpy as jnp
from jax import lax
from jax.experimental import pallas as pl
from jax.experimental.pallas import tpu as pltpu
from jax.sharding import PartitionSpec as P

epsilon = 1e-05
CHUNKS = 16
GROUP = 8
LANES = 128

VMEM_LIMIT = 64 * 2**20
ROWS_AT_ONCE = 64


def standardize(values):
    row_mean = jnp.mean(values, axis=-1, keepdims=True)
    centered = values - row_mean
    spread = jnp.mean(centered * centered, axis=-1, keepdims=True)
    factor = lax.rsqrt(spread + epsilon)
    return centered * factor, factor


def norm_back(grads, gain, standard, factor):
    scaled = grads * gain
    return factor * (
        scaled
        - jnp.mean(scaled, axis=-1, keepdims=True)
        - standard * jnp.mean(scaled * standard, axis=-1, keepdims=True)
    )


def project_back(grads_low, weight):
    return lax.dot_general(
        grads_low, weight, (((1,), (1,)), ((), ())), preferred_element_type=jnp.float32
    )


def weight_grad(rows_low, grads_low):
    return lax.dot_general(
        rows_low, grads_low, (((0,), (0,)), ((), ())), preferred_element_type=jnp.float32
    )


def block(ref, place):
    return ref[place * CHUNKS : (place + 1) * CHUNKS, :]


def chunk_rows(chunk, states):
    return pl.ds(chunk, states, stride=CHUNKS)


def state_sums(width, rows_ref, decay_ref, out_ref, group, places, weight, lead):
    decay = decay_ref[pl.ds(group * GROUP, GROUP), :][:, None, :]
    running = jnp.zeros((GROUP, CHUNKS, LANES), jnp.float32)
    for place in places:
        rows = block(rows_ref, place)
        if weight is not None:
            rows = rows * weight(place)
        running = decay * (running + rows[None]) if lead else decay * running + rows[None]
    return running


def forward_states(width, rows_ref, rate_ref, sums_ref, last_ref, decay_ref):
    states = rate_ref.shape[0]
    decay_ref[...] = jnp.exp(-rate_ref[...])

    def body(group, unused):
        running = state_sums(width, rows_ref, decay_ref, None, group, range(width), None, False)
        sums_ref[pl.ds(group * GROUP * CHUNKS, GROUP * CHUNKS), :] = running.reshape(-1, LANES)
        return unused

    lax.fori_loop(0, states // GROUP, body, 0)
    hop = jnp.exp(-width * rate_ref[...])
    held = jnp.zeros((states, LANES), jnp.float32)
    for chunk in range(CHUNKS):
        held = hop * held + sums_ref[chunk_rows(chunk, states), :]
    last_ref[...] = held


def forward_near(
    width, rows_ref, rate_ref, coef_ref, skip_ref, mixed_ref, kernel_ref, taps_ref
):
    states = rate_ref.shape[0]
    lags = lax.broadcasted_iota(jnp.int32, (8, LANES), 0).astype(jnp.float32)

    def add_states(group, totals):
        members = pl.ds(pl.multiple_of(group * GROUP, GROUP), GROUP)
        rates, coefs = rate_ref[members, :], coef_ref[members, :]
        steps = jnp.exp(-8.0 * rates)
        totals = list(totals)
        for i in range(GROUP):
            term = coefs[i : i + 1] * jnp.exp(-rates[i : i + 1] * lags)
            for place in range(width // 8):
                totals[place] = totals[place] + term
                term = term * steps[i : i + 1]
        return tuple(totals)

    zero = jnp.zeros((8, LANES), jnp.float32)
    totals = lax.fori_loop(0, states // GROUP, add_states, (zero,) * (width // 8))
    kernel_ref[...] = jnp.concatenate(totals, axis=0)
    for lag in range(width):
        taps_ref[lag * CHUNKS : (lag + 1) * CHUNKS, :] = jnp.broadcast_to(
            kernel_ref[lag : lag + 1, :], (CHUNKS, LANES)
        )
    for start in range(0, width, 4):
        sums = [skip_ref[...] * block(rows_ref, start + i) for i in range(4)]
        for place in range(start + 4):
            rows = block(rows_ref, place)
            for i in range(4):
                if start + i >= place:
                    sums[i] = sums[i] + block(taps_ref, start + i - place) * rows
        for i in range(4):
            mixed_ref[(start + i) * CHUNKS : (start + i + 1) * CHUNKS, :] = sums[i]


def forward_far(
    width, sums_ref, entering_ref, rate_ref, coef_ref, mixed_ref, held_ref, decay_ref
):
    states = rate_ref.shape[0]
    decay_ref[...] = jnp.exp(-rate_ref[...])
    hop = jnp.exp(-width * rate_ref[...])
    held = entering_ref[...]
    for chunk in range(CHUNKS):
        held_ref[chunk_rows(chunk, states), :] = held
        held = hop * held + sums_ref[chunk_rows(chunk, states), :]

    def body(group, unused):
        decay = decay_ref[pl.ds(group * GROUP, GROUP), :][:, None, :]
        coef = coef_ref[pl.ds(group * GROUP, GROUP), :][:, None, :]
        term = held_ref[pl.ds(group * GROUP * CHUNKS, GROUP * CHUNKS), :].reshape(
            GROUP, CHUNKS, LANES
        )
        term = term * (coef * decay)
        for place in range(width):
            mixed_ref[place * CHUNKS : (place + 1) * CHUNKS, :] += jnp.sum(term, axis=0)
            if place < width - 1:
                term = term * decay
        return unused

    lax.fori_loop(0, states // GROUP, body, 0)


def backward_states(width, grads_ref, rate_ref, sums_ref, first_ref, decay_ref):
    states = rate_ref.shape[0]
    decay_ref[...] = jnp.exp(-rate_ref[...])

    def body(group, unused):
        running = state_sums(
            width, grads_ref, decay_ref, None, group, range(width - 1, -1, -1), None, True
        )
        sums_ref[pl.ds(group * GROUP * CHUNKS, GROUP * CHUNKS), :] = running.reshape(-1, LANES)
        return unused

    lax.fori_loop(0, states // GROUP, body, 0)
    hop = jnp.exp(-width * rate_ref[...])
    held = jnp.zeros((states, LANES), jnp.float32)
    for chunk in range(CHUNKS - 1, -1, -1):
        held = hop * held + sums_ref[chunk_rows(chunk, states), :]
    first_ref[...] = held


def backward_near(
    width,
    grads_ref,
    rows_ref,
    sums_ref,
    entering_ref,
    rate_ref,
    skip_ref,
    kernel_ref,
    back_ref,
    coef_grad_ref,
    rate_grad_ref,
    decay_ref,
    hop_ref,
    taps_ref,
    after_ref,
    lag_ref,
):
    states = rate_ref.shape[0]
    hop = jnp.exp(-width * rate_ref[...])
    hop_ref[...] = hop
    held = entering_ref[...]
    for chunk in range(CHUNKS - 1, -1, -1):
        after_ref[chunk_rows(chunk, states), :] = held
        held = hop * held + sums_ref[chunk_rows(chunk, states), :]
    for lag in range(width):
        taps_ref[lag * CHUNKS : (lag + 1) * CHUNKS, :] = jnp.broadcast_to(
            kernel_ref[lag : lag + 1, :], (CHUNKS, LANES)
        )
    for start in range(0, width, 4):
        sums = [skip_ref[...] * block(grads_ref, start + i) for i in range(4)]
        for place in range(start, width):
            grads = block(grads_ref, place)
            for i in range(4):
                if place >= start + i:
                    sums[i] = sums[i] + block(taps_ref, place - start - i) * grads
        for i in range(4):
            back_ref[(start + i) * CHUNKS : (start + i + 1) * CHUNKS, :] = sums[i]
    for start in range(0, width, 4):
        sums = [jnp.zeros((CHUNKS, LANES), jnp.float32) for i in range(4)]
        for place in range(start, width):
            grads = block(grads_ref, place)
            for i in range(4):
                if place >= start + i:
                    sums[i] = sums[i] + block(rows_ref, place - start - i) * grads
        for i in range(4):
            lag_ref[start + i : start + i + 1, :] = jnp.sum(sums[i], axis=0, keepdims=True)
    decay_all = decay_ref[...]
    near_coef = jnp.zeros((states, LANES), jnp.float32)
    near_rate = jnp.zeros((states, LANES), jnp.float32)
    for lag in range(width - 1, -1, -1):
        near_coef = near_coef * decay_all + lag_ref[lag : lag + 1, :]
        near_rate = near_rate * decay_all + float(lag) * lag_ref[lag : lag + 1, :]
    coef_grad_ref[...] = near_coef
    rate_grad_ref[...] = near_rate


def backward_far(
    width,
    grads_ref,
    rows_ref,
    sums_ref,
    held_ref,
    coef_ref,
    back_ref,
    coef_grad_ref,
    rate_grad_ref,
    decay_ref,
    hop_ref,
    after_ref,
    groups,
):
    def body(group, unused):
        members = pl.ds(group * GROUP, GROUP)
        cells = pl.ds(group * GROUP * CHUNKS, GROUP * CHUNKS)
        cube = (GROUP, CHUNKS, LANES)
        decay = decay_ref[members, :][:, None, :]
        coef = coef_ref[members, :][:, None, :]
        after = after_ref[cells, :].reshape(cube)
        term = after * coef
        for place in range(width - 1, -1, -1):
            back_ref[place * CHUNKS : (place + 1) * CHUNKS, :] += jnp.sum(term, axis=0)
            if place > 0:
                term = term * decay
        held = held_ref[cells, :].reshape(cube)
        coef_grad_ref[members, :] += jnp.sum(held * sums_ref[cells, :].reshape(cube), axis=1)
        slope = state_sums(
            width,
            rows_ref,
            decay_ref,
            None,
            group,
            range(width),
            lambda place: float(width - 1 - place),
            False,
        )
        total = after * (float(width) * hop_ref[members, :][:, None, :] * held + slope)
        slope = state_sums(
            width,
            grads_ref,
            decay_ref,
            None,
            group,
            range(width - 1, -1, -1),
            lambda place: float(place + 1),
            True,
        )
        total = total + held * slope
        rate_grad_ref[members, :] += jnp.sum(total, axis=1)
        return unused

    lax.fori_loop(groups.start, groups.stop, body, 0)


MESH = pl.DeviceIdType.MESH


def add_rows(out_ref, out_start, a_ref, a_start, b_ref, b_start, rows):
    columns = out_ref.shape[1]
    size = 8
    for option in (16, 24, 32, 48, 64):
        if rows % option == 0 and option * columns <= 64 * 1024:
            size = option

    def body(i, unused):
        at = i * size
        out_ref[pl.ds(pl.multiple_of(out_start + at, 8), size), :] = (
            a_ref[pl.ds(pl.multiple_of(a_start + at, 8), size), :]
            + b_ref[pl.ds(pl.multiple_of(b_start + at, 8), size), :]
        )
        return unused

    lax.fori_loop(0, rows // size, body, 0)


class Lane:
    def __init__(self, rows, columns, bits, line_first, in_place):
        self.rows, self.columns = rows, columns
        self.bits, self.line_first, self.in_place = bits, line_first, in_place

    def buffers(self, line):
        half = self.rows // 2
        unit = half // line if self.line_first else half >> len(self.bits)
        counts = [half]
        size = half // line if self.line_first else half
        for unused in self.bits:
            size //= 2
            counts.append(size)
        counts.append(unit * (line + 1 if self.line_first else max(1, line // 2)))
        return [pltpu.VMEM((count, self.columns), jnp.float32) for count in counts]

    def copies(self, line):
        chain = 4 * line + 3 if self.line_first else line
        return 4 + 2 * len(self.bits) + chain


def lane_steps(
    lane, line, source, target, buffers, stages, semaphores, first_sem, pending
):
    send_sems, recv_sems, free_sems = semaphores
    first, chain = buffers[0], buffers[-1]
    landing = buffers[1:-1]
    acc = source if lane.in_place else first
    me = lax.axis_index("seq")
    z = lax.axis_index("batch")
    half = lane.rows // 2
    core = me % 2
    counter = [first_sem]

    def fresh():
        counter[0] += 1
        return counter[0] - 1

    def remote(src, dst, index, device):
        return pltpu.make_async_remote_copy(
            src_ref=src,
            dst_ref=dst,
            send_sem=send_sems.at[index],
            recv_sem=recv_sems.at[index],
            device_id=device,
            device_id_type=MESH,
        )

    def rows_of(ref, start, count):
        if not isinstance(start, int):
            start = pl.multiple_of(start, 8)
        return ref.at[pl.ds(start, count), :]

    def side(bit):
        return (me // bit) % 2

    def partner(bit):
        return (me + bit * (1 - 2 * side(bit)), z)

    def free(index, device):
        pl.semaphore_signal(
            free_sems.at[index], inc=1, device_id=device, device_id_type=MESH
        )

    def wait_free(index):
        pl.semaphore_wait(free_sems.at[index], 1)

    mine, other = core * half, (1 - core) * half
    base_row = mine if lane.in_place else 0
    swap = remote(rows_of(source, other, half), first, fresh(), partner(1))

    def load():
        place = len(stages) - 1 if lane.stage is None else lane.stage
        return pltpu.make_async_copy(rows_of(source, mine, half), *stages[place])

    def begin():
        swap.start()
        if not lane.in_place and lane.stage is not None:
            load().start()

    def add_swap():
        if lane.in_place:
            swap.wait_recv()
            add_rows(acc, mine, acc, mine, first, 0, half)
        else:
            if lane.stage is None:
                load().start()
            swap.wait_recv()
            load().wait()
            add_rows(acc, 0, acc, 0, stages[-1 if lane.stage is None else lane.stage][0], 0, half)

    pending.append(swap.wait_send)
    steps = [[begin], [add_swap]]

    def join(function):
        steps[-1].append(function)

    def step(function):
        steps.append([function])

    def neighbours_sum(base, size):
        starts, indices = [base], []
        for place, bit in enumerate(lane.bits):
            size //= 2
            start, index = starts[-1], fresh()
            copy = remote(
                rows_of(acc, base_row + start + (1 - side(bit)) * size, size),
                landing[place],
                index,
                partner(bit),
            )
            own = start + side(bit) * size
            join(copy.start)

            def receive(copy=copy, own=own, size=size, place=place, bit=bit, index=index):
                copy.wait()
                free(index, partner(bit))
                add_rows(acc, base_row + own, acc, base_row + own, landing[place], 0, size)

            step(receive)
            starts.append(own)
            indices.append(index)
        return starts, size, indices

    def neighbours_spread(starts, size, indices):
        for place in range(len(lane.bits) - 1, -1, -1):
            rows = rows_of(acc, base_row + starts[place + 1], size)
            copy = remote(rows, rows, fresh(), partner(lane.bits[place]))
            join(functools.partial(wait_free, indices[place]))
            join(copy.start)
            pending.append(copy.wait_send)
            step(copy.wait_recv)
            size *= 2

    if not lane.line_first:
        starts, size, indices = neighbours_sum(0, half)
        at = starts[-1]
        depth = jnp.minimum(z, line - 1 - z)
        lower = z < line // 2
        inward = (me, jnp.where(lower, z + 1, z - 1))
        outward = (me, jnp.where(lower, z - 1, z + 1))
        across = (me, line - 1 - z)
        middle = line // 2 - 1

        def on(level, function):
            def guarded():
                pl.when(depth == level)(function)

            return guarded

        passed = []
        for level in range(middle):
            rows = rows_of(acc, base_row + at, size)
            passed.append(fresh())
            copy = remote(rows, rows_of(chain, level * size, size), passed[-1], inward)
            join(on(level, copy.start))

            def receive(copy=copy, level=level):
                copy.wait_recv()
                add_rows(acc, base_row + at, acc, base_row + at, chain, level * size, size)

            def release(copy=copy, index=passed[-1]):
                copy.wait_send()
                free(index, inward)

            step(on(level + 1, receive))
            join(on(level, release))
        rows = rows_of(acc, base_row + at, size)
        copy = remote(rows, rows_of(chain, middle * size, size), fresh(), across)
        join(on(middle, copy.start))

        def receive_across(copy=copy):
            copy.wait()
            add_rows(acc, base_row + at, acc, base_row + at, chain, middle * size, size)

        step(on(middle, receive_across))
        for level in range(middle - 1, -1, -1):
            rows = rows_of(acc, base_row + at, size)
            copy = remote(rows, rows, fresh(), outward)
            join(on(level + 1, functools.partial(wait_free, passed[level])))
            join(on(level + 1, copy.start))
            pending.append(on(level + 1, copy.wait_send))
            step(on(level, copy.wait_recv))
        neighbours_spread(starts, size, indices)
    else:
        unit = half // line
        slots = [fresh() for unused in range(line + 1)]
        outs = [[fresh() for unused in range(2)] for unused in range(line)]
        spreads = [fresh() for unused in range(line)]

        def on(place, function):
            def guarded():
                pl.when(z == place)(function)

            return guarded

        def beside(place):
            return (me, place - 1 if place > 0 else place + 1)

        def hop(place, member, step_to):
            slot = line if step_to < 0 and member == place - 1 else member
            return remote(
                rows_of(acc, base_row + member * unit, unit),
                rows_of(chain, slot * unit, unit),
                slots[slot],
                (me, place + step_to),
            )

        def arrived(place, slot, member):
            remote(
                rows_of(acc, base_row + member * unit, unit),
                rows_of(chain, slot * unit, unit),
                slots[slot],
                beside(place),
            ).wait_recv()
            row = base_row + member * unit
            add_rows(acc, row, acc, row, chain, slot * unit, unit)

        for turn in range(line - 1):

            def rightward(place=turn):
                for member in range(line - 1, place, -1):
                    if place > 0:
                        arrived(place, member, member)
                    hop(place, member, 1).start()

            def leftward(place=line - 1 - turn):
                for member in range(place):
                    if place < line - 1:
                        arrived(place, member, member)
                    hop(place, member, -1).start()

            if turn > 0:
                step(on(turn, rightward))
            else:
                join(on(turn, rightward))
            join(on(line - 1 - turn, leftward))

        to_right, to_left = fresh(), fresh()

        def collect(place):
            if place > 0:
                arrived(place, place, place)
            if place < line - 1:
                arrived(place, line, place)
            for member in range(line - 1, place, -1):
                hop(place, member, 1).wait_send()
            if place < line - 1:
                free(to_right, (me, place + 1))
            for member in range(place):
                hop(place, member, -1).wait_send()
            if place > 0:
                free(to_left, (me, place - 1))

        def collect_all():
            for place in range(line):
                on(place, functools.partial(collect, place))()

        step(collect_all)

        base = z * unit
        starts, size, indices = neighbours_sum(base, unit)
        neighbours_spread(starts, size, indices)

        def spread_at(place, distance, receive, send):
            members = {place - distance, place + distance}
            for member in sorted(members):
                if not 0 <= member < line:
                    continue
                if receive and distance > 0:
                    remote(
                        rows_of(acc, base_row + member * unit, unit),
                        rows_of(acc, base_row + member * unit, unit),
                        spreads[member],
                        beside(place),
                    ).wait_recv()
                if not send:
                    continue
                for step_to in (1, -1):
                    going = member <= place if step_to > 0 else member >= place
                    if going and 0 <= place + step_to < line:
                        yield member, step_to

        def pass_on(place, member, step_to):
            return pltpu.make_async_remote_copy(
                src_ref=rows_of(acc, base_row + member * unit, unit),
                dst_ref=rows_of(acc, base_row + member * unit, unit),
                send_sem=send_sems.at[outs[member][0 if step_to > 0 else 1]],
                recv_sem=recv_sems.at[spreads[member]],
                device_id=(me, place + step_to),
                device_id_type=MESH,
            )

        for distance in range(line):

            def forward(place, distance):
                if distance == 0 and place > 0:
                    wait_free(to_right)
                if distance == 0 and place < line - 1:
                    wait_free(to_left)
                for member, step_to in spread_at(place, distance, True, True):
                    pass_on(place, member, step_to).start()

            def forward_all(distance=distance):
                for place in range(line):
                    on(place, functools.partial(forward, place, distance))()

            if distance == 0:
                join(forward_all)
            else:
                step(forward_all)

        def gone(place):
            for distance in range(line):
                for member, step_to in spread_at(place, distance, False, True):
                    pass_on(place, member, step_to).wait_send()

        for place in range(line):
            pending.append(on(place, functools.partial(gone, place)))

    keep_index, give_index = fresh(), fresh()
    done = rows_of(acc, base_row, half)
    keep = pltpu.make_async_copy(done, rows_of(target, mine, half), recv_sems.at[keep_index])
    give = remote(done, rows_of(target, mine, half), give_index, partner(1))
    join(keep.start)
    join(give.start)
    pending.append(keep.wait)
    pending.append(give.wait)
    assert counter[0] - first_sem <= lane.copies(line)
    return steps


def turn_order(lengths, order):
    if [order.count(place) for place in range(len(lengths))] == lengths:
        return order
    last = len(lengths) - 1
    turns = range(max(lengths[:-1], default=0))
    lanes = [place for turn in turns for place in range(last) if turn < lengths[place]]
    return [last] * lengths[last] + lanes


class Loop:
    def __init__(self, count, *parts):
        self.count, self.parts = count, parts

    def steps(self):
        return self.count * len(self.parts)


def call_all(functions):
    for function in functions:
        function()


def run_loop(loop, between):
    parts = len(loop.parts)

    def body(i, unused):
        for place, part in enumerate(loop.parts):
            part(i)
            for turn in range(loop.count):
                functions = between[turn * parts + place]
                if functions:
                    pl.when(i == turn)(functools.partial(call_all, functions))
        return unused

    lax.fori_loop(0, loop.count, body, 0)


def give_stages(lanes, order, count):
    free, seen = list(range(count)), [0] * len(lanes)
    for place in order:
        if place == len(lanes) or lanes[place].in_place:
            continue
        seen[place] += 1
        lane = lanes[place]
        if seen[place] == 1:
            lane.stage = free.pop() if free else None
        elif seen[place] == 2 and lane.stage is not None:
            free.append(lane.stage)


class Runner:
    def __init__(self, lanes, programs, count, order):
        lengths = [len(program) for program in programs] + [count]
        self.programs = [list(program) for program in programs]
        self.order = turn_order(lengths, order)
        give_stages(lanes, self.order, STAGES)
        self.work_place = len(programs)
        self.at = 0

    def lanes(self):
        functions = []
        while self.at < len(self.order) and self.order[self.at] != self.work_place:
            functions += self.programs[self.order[self.at]].pop(0)
            self.at += 1
        return functions

    def run(self, work):
        for item in work:
            call_all(self.lanes())
            self.at += 1
            if not isinstance(item, Loop):
                item()
                continue
            between = []
            for unused in range(item.steps() - 1):
                between.append(self.lanes())
                self.at += 1
            run_loop(item, between + [[]])


def steps_in(work):
    return sum(item.steps() if isinstance(item, Loop) else 1 for item in work)


def state_exchange(bits, row_count, rate, totals, arrivals, entering, sends, receives, forward):
    me, z = lax.axis_index("seq"), lax.axis_index("batch")

    def copy(level):
        bit = bits[level]
        return pltpu.make_async_remote_copy(
            src_ref=totals[level],
            dst_ref=arrivals[level],
            send_sem=sends[level],
            recv_sem=receives[level],
            device_id=(me + bit * (1 - 2 * ((me // bit) % 2)), z),
            device_id_type=MESH,
        )

    def arrive(level):
        bit = bits[level]
        copy(level).wait_recv()
        place = me % bit
        after = (me // bit) % 2 == (1 if forward else 0)
        hops = (row_count * (place if forward else bit - 1 - place)).astype(jnp.float32)
        term = jnp.exp(-rate[...] * hops) * arrivals[level][...]
        term = jnp.where(after, term, 0.0)
        entering[...] = term if level == 0 else entering[...] + term
        if level + 1 < len(bits):
            far = jnp.exp(-float(row_count * bit) * rate[...])
            ours, theirs = totals[level][...], arrivals[level][...]
            totals[level + 1][...] = jnp.where(after, ours + far * theirs, theirs + far * ours)
            copy(level + 1).start()

    return copy, arrive


def lane_columns(tile):
    return pl.ds(pl.multiple_of(tile * LANES, LANES), LANES)


def row_block(i, count):
    return pl.ds(pl.multiple_of(i * count, count), count)


SKIP, GAIN_ONE, BIAS_ONE, GAIN_TWO, BIAS_TWO = range(5)


def vector(ref, place):
    return ref[place : place + 1, :]


class ForwardIn(NamedTuple):
    tokens: Any
    token_grads: Any
    skip: Any
    gain_one: Any
    bias_one: Any
    gain_two: Any
    bias_two: Any
    query_weight: Any
    key_weight: Any
    value_weight: Any
    out_weight: Any
    taps: Any
    rate: Any
    coef: Any


class ForwardOut(NamedTuple):
    product: Any
    held: Any
    kernel: Any
    values: Any
    keys_mixed: Any
    key_rows: Any
    queries: Any
    mixed: Any
    gated: Any
    middle: Any
    normed_two: Any
    standard_two: Any
    factor_two: Any
    normed_one: Any
    standard_one: Any
    factor_one: Any
    out_grad: Any
    vectors: Any


def forward_body(row_count, size, bits, *refs):
    width = row_count // CHUNKS
    levels = len(bits)
    taken, outs = len(ForwardIn._fields), len(ForwardOut._fields)
    given = ForwardIn(*refs[:taken])
    results = ForwardOut(*refs[taken : taken + outs])
    own = ForwardOut(*refs[taken + outs : taken + 2 * outs])
    refs = refs[taken + 2 * outs :]
    brought, refs = refs[:4], refs[4:]
    sums, taps, decay, entering, edge_out, edge_in = refs[:6]
    totals, arrivals = refs[6 : 6 + levels], refs[6 + levels : 6 + 2 * levels]
    sends, receives, keeps = refs[-3:]
    vectors = own.vectors
    rate, coef, skip = given.rate, given.coef, vectors.at[0:1]
    channels = rate.shape[1]
    tiles = channels // LANES
    tap_count = given.taps.shape[0]
    halo = tap_count - 1
    low = jnp.bfloat16
    me, z = lax.axis_index("seq"), lax.axis_index("batch")
    barrier = pltpu.get_barrier_semaphore()

    def greet(device):
        pl.semaphore_signal(barrier, inc=1, device_id=device, device_id_type=MESH)

    for bit in bits:
        greet((me + bit * (1 - 2 * ((me // bit) % 2)), z))
    pl.when(me > 0)(lambda: greet((me - 1, z)))
    pl.when(me < size - 1)(lambda: greet((me + 1, z)))

    kept = ForwardOut(
        *[
            pltpu.make_async_copy(own[i], results[i], keeps.at[i])
            for i in range(len(ForwardOut._fields))
        ]
    )

    def half_exchange(part):
        size_of = channels // 2
        here = pl.ds(part * size_of, size_of)
        first = part * levels
        return state_exchange(
            bits,
            row_count,
            rate.at[:, here],
            [total.at[:, here] for total in totals],
            [arrival.at[:, here] for arrival in arrivals],
            entering.at[:, here],
            [sends.at[first + level] for level in range(levels)],
            [receives.at[first + level] for level in range(levels)],
            True,
        )

    halves = [half_exchange(0), half_exchange(1)]

    def begin_half(part):
        return halves[part][0](0).start

    def arrive_half(part, level):
        return functools.partial(halves[part][1], level)

    def edge(device):
        return pltpu.make_async_remote_copy(
            src_ref=edge_out,
            dst_ref=edge_in,
            send_sem=sends.at[2 * levels],
            recv_sem=receives.at[2 * levels],
            device_id=(device, z),
            device_id_type=MESH,
        )

    def reordered(rows, i):
        shape = (128, row_count)
        row = i * 128 + lax.broadcasted_iota(jnp.int32, shape, 0)
        token = lax.rem(row, CHUNKS) * width + lax.div(row, CHUNKS)
        chosen = lax.broadcasted_iota(jnp.int32, shape, 1) == token
        picks = jnp.where(chosen, 1.0, 0.0).astype(low)
        return jnp.dot(picks, rows[...], preferred_element_type=jnp.float32)

    far = (given.key_weight, given.value_weight, given.query_weight, given.out_weight)
    weights = [
        pltpu.make_async_copy(far[i], brought[i], keeps.at[len(ForwardOut._fields) + i])
        for i in range(4)
    ]
    for weight in weights:
        weight.start()

    def norm_rows(i):
        rows = row_block(i, 128)
        inputs = reordered(given.tokens, i)
        own.middle[rows, :] = inputs
        standard, factor = standardize(inputs)
        own.standard_one[rows, :] = standard
        own.factor_one[rows, :] = jnp.broadcast_to(factor, (128, LANES))
        own.normed_one[rows, :] = (
            standard * vector(vectors, GAIN_ONE) + vector(vectors, BIAS_ONE)
        ).astype(low)

    def grad_rows(i):
        own.out_grad[row_block(i, 128), :] = reordered(given.token_grads, i).astype(low)

    def project_to(target, weight, lead):
        def body(i):
            cols = row_block(i, 256)
            target[lead : lead + row_count, cols] = jnp.dot(
                own.normed_one[...], weight[:, cols], preferred_element_type=jnp.float32
            )

        return Loop(channels // 256, body)

    lead = halo * CHUNKS

    def send_edge():
        edge_out[...] = jnp.zeros(edge_out.shape, jnp.float32)
        for i in range(halo):
            row = lead + (width - halo + i) * CHUNKS + CHUNKS - 1
            edge_out[i : i + 1, :] = own.key_rows[row : row + 1, :]
        pl.semaphore_wait(
            barrier, levels + jnp.where(me > 0, 1, 0) + jnp.where(me < size - 1, 1, 0)
        )
        pl.when(me < size - 1)(edge(me + 1).start)

        @pl.when(me == 0)
        def at_start():
            edge_in[...] = jnp.zeros(edge_in.shape, jnp.float32)

    def take_edge():
        pl.when(me > 0)(edge(me - 1).wait_recv)

    def states_tile(tile):
        here = lane_columns(tile)
        keys, tap = own.key_rows, given.taps
        for i in range(halo):
            row = lead + (width - halo + i) * CHUNKS
            rows = keys[row : row + CHUNKS, here]
            keys[i * CHUNKS : (i + 1) * CHUNKS, here] = jnp.concatenate(
                [edge_in[i : i + 1, here], rows[: CHUNKS - 1]], axis=0
            )
        total = tap[0:1, here] * keys[lead : lead + row_count, here]
        for offset in range(1, tap_count):
            start = lead - offset * CHUNKS
            total = total + tap[offset : offset + 1, here] * keys[start : start + row_count, here]
        own.keys_mixed[:, here] = total
        own.product[:, here] = total * own.values[:, here]
        forward_states(
            width,
            own.product.at[:, here],
            rate.at[:, here],
            sums.at[tile],
            totals[0].at[:, here],
            decay,
        )

    def near_tile(tile):
        here = lane_columns(tile)
        forward_near(
            width,
            own.product.at[:, here],
            rate.at[:, here],
            coef.at[:, here],
            skip.at[:, here],
            own.mixed.at[:, here],
            own.kernel.at[:, here],
            taps,
        )

    def far_tile(tile):
        here = lane_columns(tile)
        forward_far(
            width,
            sums.at[tile],
            entering.at[:, here],
            rate.at[:, here],
            coef.at[:, here],
            own.mixed.at[:, here],
            own.held.at[tile],
            decay,
        )

    def out_rows(i):
        rows = row_block(i, 128)
        gated = (own.queries[rows, :] * own.mixed[rows, :]).astype(low)
        own.gated[rows, :] = gated
        middle = own.middle[rows, :] + jnp.dot(
            gated, brought[3][...], preferred_element_type=jnp.float32
        )
        own.middle[rows, :] = middle
        standard, factor = standardize(middle)
        own.standard_two[rows, :] = standard
        own.factor_two[rows, :] = jnp.broadcast_to(factor, (128, LANES))
        own.normed_two[rows, :] = (
            standard * vector(vectors, GAIN_TWO) + vector(vectors, BIAS_TWO)
        ).astype(low)

    def loop(item, between=()):
        between = list(between)
        run_loop(item, between + [[]] * (item.steps() - len(between)))

    def keep_all(*copies):
        for one in copies:
            one.start()

    vectors[...] = jnp.zeros(vectors.shape, jnp.float32)
    singles = (given.skip, given.gain_one, given.bias_one, given.gain_two, given.bias_two)
    for place, single in enumerate(singles):
        vectors[place : place + 1, :] = single[...][None]
    keep_all(kept.vectors)
    loop(Loop(row_count // 128, norm_rows))
    keep_all(kept.standard_one, kept.factor_one, kept.normed_one)
    weights[0].wait()
    loop(project_to(own.key_rows, brought[0], lead))
    send_edge()
    weights[1].wait()
    loop(project_to(own.values, brought[1], 0))
    keep_all(kept.values)
    take_edge()
    between = [[] for unused in range(tiles)]
    between[tiles // 2 - 1].append(begin_half(0))
    between[tiles - 2].append(arrive_half(0, 0))
    loop(Loop(tiles, states_tile), between)
    begin_half(1)()
    keep_all(kept.key_rows, kept.keys_mixed, kept.product)
    weights[2].wait()
    loop(project_to(own.queries, brought[2], 0))
    keep_all(kept.queries)
    arrive_half(1, 0)()
    if levels > 1:
        arrive_half(0, 1)()
    loop(Loop(row_count // 128, grad_rows))
    keep_all(kept.out_grad)
    between = [[] for unused in range(tiles)]
    for level in range(1, levels):
        if level + 1 < levels:
            between[max(0, level * tiles // levels - 1)].append(arrive_half(0, level + 1))
            between[max(0, level * tiles // levels - 1)].insert(0, arrive_half(1, level))
        else:
            between[tiles - 1].append(arrive_half(1, level))
    loop(Loop(tiles, near_tile), between)
    keep_all(kept.kernel)
    loop(Loop(tiles, far_tile))
    keep_all(kept.mixed, kept.held)
    weights[3].wait()
    loop(Loop(row_count // 128, out_rows))
    keep_all(kept.gated, kept.middle, kept.normed_two, kept.standard_two, kept.factor_two)
    for copy, unused in halves:
        for level in range(levels):
            copy(level).wait_send()
    pl.when(me < size - 1)(edge(me + 1).wait_send)
    for one in kept:
        one.wait()


def forward(row_count, arrays):
    size = lax.axis_size("seq")
    bits = [1 << place for place in range(size.bit_length() - 1)]
    states, channels = arrays.rate.shape
    tiles, width = channels // LANES, row_count // CHUNKS
    halo = arrays.taps.shape[0] - 1
    full, low = jnp.float32, jnp.bfloat16
    square = ((row_count, channels), full)
    low_square = ((row_count, channels), low)
    thin = ((row_count, LANES), full)
    held = ((tiles, states * CHUNKS, LANES), full)
    outs = ForwardOut(
        product=square,
        held=held,
        kernel=((width, channels), full),
        values=square,
        keys_mixed=square,
        key_rows=((row_count + halo * CHUNKS, channels), full),
        queries=square,
        mixed=square,
        gated=low_square,
        middle=square,
        normed_two=low_square,
        standard_two=square,
        factor_two=thin,
        normed_one=low_square,
        standard_one=square,
        factor_one=thin,
        out_grad=low_square,
        vectors=((8, channels), full),
    )
    square_low = (channels, channels)
    weights = [(square_low, low)] * 4
    scratch = list(outs) + weights + [held, thin, ((states, LANES), full), ((states, channels), full)]
    scratch += [((8, channels), full)] * 2 + [((states, channels), full)] * (2 * len(bits))
    counts = [2 * len(bits) + 1, 2 * len(bits) + 1, len(outs) + 4]
    found = pl.pallas_call(
        functools.partial(forward_body, row_count, size, bits),
        out_shape=[jax.ShapeDtypeStruct(*out) for out in outs],
        in_specs=[
            pl.BlockSpec(memory_space=pltpu.HBM if shape == square_low else pltpu.VMEM)
            for shape in (getattr(arrays, name).shape for name in ForwardIn._fields)
        ],
        out_specs=[pl.BlockSpec(memory_space=pltpu.HBM)] * len(outs),
        scratch_shapes=[pltpu.VMEM(*shape) for shape in scratch]
        + [pltpu.SemaphoreType.DMA((count,)) for count in counts],
        compiler_params=pltpu.CompilerParams(
            collective_id=1, has_side_effects=True, vmem_limit_bytes=VMEM_LIMIT
        ),
    )(*[getattr(arrays, name) for name in ForwardIn._fields])
    return ForwardOut(*found)


class BackwardIn(NamedTuple):
    up_weight: Any
    down_weight: Any
    out_weight: Any
    query_weight: Any
    key_weight: Any
    value_weight: Any
    product: Any
    held: Any
    values: Any
    keys_mixed: Any
    key_rows: Any
    queries: Any
    mixed: Any
    gated: Any
    middle: Any
    standard_two: Any
    factor_two: Any
    standard_one: Any
    factor_one: Any
    rate: Any
    coef: Any
    vectors: Any
    taps: Any
    kernel: Any
    out_grad: Any
    normed_one: Any
    normed_two: Any


FAR = 19


class Results(NamedTuple):
    down: Any
    up: Any
    out: Any
    query: Any
    value: Any
    key: Any
    small: Any
    tokens: Any
    mixed_out: Any
    own_down: Any
    own_up: Any
    own_out: Any


HIDDEN_AT_ONCE = 256
STAGES = 3


def gelu_pair(values):
    slope = math.sqrt(2.0 / math.pi)
    squared = values * values
    bent = jnp.tanh(slope * (values + 0.044715 * (values * squared)))
    half = 0.5 * (1.0 + bent)
    steep = 0.5 * values * (1.0 - bent * bent) * (slope * (1.0 + 3.0 * 0.044715 * squared))
    return values * half, half + steep


def backward_body(row_count, size, line, bits, lanes, order, *refs):
    width = row_count // CHUNKS
    given = BackwardIn(*refs[: len(BackwardIn._fields)])
    rest = list(refs[len(given) :])

    def take(count):
        taken = rest[:count]
        del rest[:count]
        return taken

    results = Results(*take(len(Results._fields)))
    semaphores = rest[-6:-3]
    load_sems, swap_send, swap_recv = rest[-3:]
    del rest[-6:]
    (grad_query, grad_value, grad_key, small) = take(4)
    (shifted, total, grad_middle) = take(3)
    (grad_queries, values_low, keys_low, weight) = take(4)
    (entering, edge_out, edge_in) = take(3)
    stages = [(ref, load_sems.at[20 + i]) for i, ref in enumerate(take(STAGES + 1))]
    levels = len(bits)
    totals, arrivals = take(levels), take(levels)

    me = lax.axis_index("seq")
    z = lax.axis_index("batch")
    channels = small.shape[1]
    tiles = channels // LANES
    rate, coef = given.rate, given.coef
    states = rate.shape[0]
    tap_count = given.taps.shape[0]
    halo = tap_count - 1
    hidden = given.up_weight.shape[1]
    low, full = jnp.bfloat16, jnp.float32
    misc = 2 * states

    barrier = pltpu.get_barrier_semaphore()

    def greet(device):
        pl.semaphore_signal(barrier, inc=1, device_id=device, device_id_type=MESH)

    for bit in bits:
        greet((me + bit * (1 - 2 * ((me // bit) % 2)), z))
    pl.when(z > 0)(lambda: greet((me, z - 1)))
    pl.when(z < line - 1)(lambda: greet((me, z + 1)))
    pl.when(me > 0)(lambda: greet((me - 1, z)))
    pl.when(me < size - 1)(lambda: greet((me + 1, z)))
    pl.semaphore_wait(
        barrier,
        len(bits)
        + jnp.where(z > 0, 1, 0)
        + jnp.where(z < line - 1, 1, 0)
        + jnp.where(me > 0, 1, 0)
        + jnp.where(me < size - 1, 1, 0),
    )

    def local(source, target, place):
        return pltpu.make_async_copy(source, target, load_sems.at[place])

    def fetch(*triples):
        copies = [local(*triple) for triple in triples]
        for copy in copies:
            copy.start()
        for copy in copies:
            copy.wait()

    def add_small(row, value):
        small[row : row + 1, :] += jnp.sum(value, axis=0, keepdims=True)

    exchange, arrive = state_exchange(
        bits,
        row_count,
        rate,
        totals,
        arrivals,
        entering,
        [swap_send.at[level] for level in range(levels)],
        [swap_recv.at[level] for level in range(levels)],
        False,
    )

    def edge(device):
        return pltpu.make_async_remote_copy(
            src_ref=edge_out,
            dst_ref=edge_in,
            send_sem=swap_send.at[levels],
            recv_sem=swap_recv.at[levels],
            device_id=(device, z),
            device_id_type=MESH,
        )

    steps = hidden // HIDDEN_AT_ONCE
    per_block = channels // HIDDEN_AT_ONCE
    held_weight = local(given.out_weight, weight, 7)
    held_standard = local(given.standard_two, shifted.at[:row_count], 8)
    held_gated = local(given.gated, values_low, 9)
    held_middle = local(given.middle, total, 10)
    out_rows = local(keys_low, results.mixed_out, 10)

    def feed_forward(
        up_tile, down_tile, active, grad_low, slope, down_sum, up_sum, block_a, block_b, thin
    ):
        def weights(step):
            here = row_block(step, HIDDEN_AT_ONCE)
            slot = step % 2
            return (
                local(given.up_weight.at[:, here], up_tile.at[slot], slot),
                local(given.down_weight.at[here, :], down_tile.at[slot], 2 + slot),
            )

        def sums(step):
            part = step // per_block
            here = row_block(step % per_block, HIDDEN_AT_ONCE)
            return (
                local(down_sum, results.own_down.at[part, here, :], 4),
                local(up_sum, results.own_up.at[part, :, here], 5),
            )

        def start():
            for copy in weights(0):
                copy.start()
            for copy in (held_middle, held_weight, held_standard, held_gated):
                copy.start()
            small[...] = jnp.zeros(small.shape, full)
            grad_middle[...] = jnp.zeros(grad_middle.shape, full)
            held_middle.wait()

        def part_one(step):
            slot = step % 2
            for copy in weights(step):
                copy.wait()

            @pl.when(step + 1 < steps)
            def following():
                for copy in weights(step + 1):
                    copy.start()

            before = jnp.dot(
                given.normed_two[...], up_tile[slot], preferred_element_type=full
            )
            after, steep = gelu_pair(before)
            active[...] = after.astype(low)
            slope[...] = steep

        def part_two(step):
            slot = step % 2
            total[...] += jnp.dot(active[...], down_tile[slot], preferred_element_type=full)
            grads = project_back(given.out_grad[...], down_tile[slot])
            grad_low[...] = (grads * slope[...]).astype(low)

        def part_three(step):
            @pl.when(step > 0)
            def previous():
                for copy in sums(step - 1):
                    copy.wait()

            down_sum[...] = weight_grad(active[...], given.out_grad[...])
            up_sum[...] = weight_grad(given.normed_two[...], grad_low[...])
            for copy in sums(step):
                copy.start()

        def part_four(step):
            grad_middle[...] += project_back(grad_low[...], up_tile[step % 2])

        def finish():
            for copy in sums(steps - 1):
                copy.wait()
            keys_low[...] = total[...].astype(low)
            out_rows.start()
            held_standard.wait()
            held_weight.wait()
            held_gated.wait()
            out_rows.wait()

        def norm_two(i):
            rows = row_block(i, 128)
            fetch((given.factor_two.at[rows, :], thin, 11))
            grads, standard = grad_middle[rows, :], shifted[rows, :]
            add_small(misc + tap_count + 3, grads * standard)
            add_small(misc + tap_count + 4, grads)
            back = given.out_grad[rows, :].astype(full) + norm_back(
                grads, vector(given.vectors, GAIN_TWO), standard, thin[:, 0:1]
            )
            grad_middle[rows, :] = back
            keys_low[rows, :] = back.astype(low)

        def out_sum(i):
            here = row_block(i, 256)
            down_sum[...] = weight_grad(values_low[:, here], keys_low[...])
            fetch((down_sum, results.own_out.at[0, here, :], 4))

        def gate(i):
            rows = row_block(i, 128)
            fetch(
                (given.mixed.at[rows, :], block_a, 11),
                (given.queries.at[rows, :], block_b, 12),
            )
            grads = project_back(keys_low[rows, :], weight[...])
            grad_queries[rows, :] = (grads * block_a[...]).astype(low)
            total[rows, :] = grads * block_b[...]

        return [
            start,
            Loop(steps, part_one, part_two, part_three, part_four),
            finish,
            Loop(row_count // 128, norm_two),
            Loop(channels // 256, out_sum),
            Loop(row_count // 128, gate),
        ]

    def weight_sum(target, grads):
        def body(i):
            rows = row_block(i, 256)
            target[rows, :] = weight_grad(given.normed_one[:, rows], grads[...])

        return Loop(channels // 256, body)

    back = shifted

    def mixer(
        rows_tile, keys_tile, other, held_tile, back_tile, taps, sums, after, decay, hop, lag
    ):
        def tile_loads(tile):
            here, slot = lane_columns(tile), tile % 2
            return (
                local(given.product.at[:, here], rows_tile.at[slot], 10 + slot),
                local(given.held.at[tile], held_tile.at[slot], 12 + slot),
                local(given.values.at[:, here], other.at[slot, pl.ds(0, row_count)], 14 + slot),
                local(given.keys_mixed.at[:, here], keys_tile.at[slot], 16 + slot),
            )

        def key_loads(tile):
            slot = tile % 2
            return local(given.key_rows.at[:, lane_columns(tile)], other.at[slot], 14 + slot)

        def first_tile(tile):
            here = lane_columns(tile)
            backward_states(
                width,
                total.at[:, here],
                rate.at[:, here],
                sums.at[tile],
                totals[0].at[:, here],
                decay,
            )

        def start_tiles():
            for copy in tile_loads(0):
                copy.start()
            exchange(0).start()

        def near(tile):
            here, slot = lane_columns(tile), tile % 2
            for copy in tile_loads(tile):
                copy.wait()

            @pl.when(tile + 1 < tiles)
            def following():
                for copy in tile_loads(tile + 1):
                    copy.start()

            decay[...] = jnp.exp(-rate[:, here])
            backward_near(
                width,
                total.at[:, here],
                rows_tile.at[slot],
                sums.at[tile],
                entering.at[:, here],
                rate.at[:, here],
                given.vectors.at[0:1, here],
                given.kernel.at[:, here],
                back_tile,
                small.at[0:states, here],
                small.at[states:misc, here],
                decay,
                hop,
                taps,
                after,
                lag,
            )

        def far(half):
            def part(tile):
                here, slot = lane_columns(tile), tile % 2
                groups = states // GROUP // 2
                backward_far(
                    width,
                    total.at[:, here],
                    rows_tile.at[slot],
                    sums.at[tile],
                    held_tile.at[slot],
                    coef.at[:, here],
                    back_tile,
                    small.at[0:states, here],
                    small.at[states:misc, here],
                    decay,
                    hop,
                    after,
                    range(half * groups, (half + 1) * groups),
                )

            return part

        def end(tile):
            here, slot = lane_columns(tile), tile % 2
            row = misc + tap_count
            small[row : row + 1, here] = jnp.sum(
                total[:, here] * rows_tile[slot], axis=0, keepdims=True
            )
            small[states:misc, here] = -coef[:, here] * small[states:misc, here]
            shifted[0:row_count, here] = back_tile[...] * other[slot, 0:row_count, :]
            values_low[:, here] = (back_tile[...] * keys_tile[slot]).astype(low)

        held_ones = local(given.standard_one, total, 7)
        held_factor = local(given.factor_one, back_tile, 8)

        def send_edge():
            key_loads(0).start()
            held_ones.start()
            held_factor.start()
            edge_out[...] = jnp.zeros(edge_out.shape, full)
            for place in range(halo):
                row = place * CHUNKS
                edge_out[place : place + 1, :] = shifted[row : row + 1, :]
            pl.when(me > 0)(edge(me - 1).start)

            @pl.when(me == size - 1)
            def at_end():
                edge_in[...] = jnp.zeros(edge_in.shape, full)

        def take_edge():
            pl.when(me < size - 1)(edge(me + 1).wait_recv)

        def keys_part(tile):
            here, slot = lane_columns(tile), tile % 2
            key_loads(tile).wait()

            @pl.when(tile + 1 < tiles)
            def following():
                key_loads(tile + 1).start()

            for place in range(halo):
                rows = shifted[place * CHUNKS : (place + 1) * CHUNKS, here]
                start = row_count + place * CHUNKS
                shifted[start : start + CHUNKS, here] = jnp.concatenate(
                    [rows[1:], edge_in[place : place + 1, here]], axis=0
                )
            tap = given.taps
            sum_rows = tap[0:1, here] * shifted[0:row_count, here]
            for offset in range(1, tap_count):
                start = offset * CHUNKS
                sum_rows = sum_rows + tap[offset : offset + 1, here] * (
                    shifted[start : start + row_count, here]
                )
            keys_low[:, here] = sum_rows.astype(low)
            grads = shifted[0:row_count, here]
            for offset in range(tap_count):
                start = (halo - offset) * CHUNKS
                small[misc + offset : misc + offset + 1, here] = jnp.sum(
                    grads * other[slot, start : start + row_count, :], axis=0, keepdims=True
                )

        def back_sum(index, grads):
            def body(i):
                rows = row_block(i, 128)
                term = project_back(grads[rows, :], weight[...])
                back[rows, :] = term if index == 0 else back[rows, :] + term

            return Loop(row_count // 128, body)

        def before_norm():
            held_ones.wait()
            held_factor.wait()

        def norm_one(i):
            rows = row_block(i, ROWS_AT_ONCE)
            grads, standard = back[rows, :], total[rows, :]
            add_small(misc + tap_count + 1, grads * standard)
            add_small(misc + tap_count + 2, grads)
            grad_middle[rows, :] += norm_back(
                grads, vector(given.vectors, GAIN_ONE), standard, back_tile[rows, 0:1]
            )

        tokens_out = local(grad_middle, results.tokens, 9)
        work = [Loop(tiles, first_tile), start_tiles]
        work.append(weight_sum(grad_query, grad_queries))
        for level in range(levels):
            work.append(functools.partial(arrive, level))
        work.append(Loop(tiles, near, far(0), far(1), end))
        work.append(send_edge)
        work.append(weight_sum(grad_value, values_low))
        work.append(take_edge)
        work.append(Loop(tiles, keys_part))
        work.append(weight_sum(grad_key, keys_low))
        chain = (
            (given.query_weight, grad_queries),
            (given.key_weight, keys_low),
            (given.value_weight, values_low),
        )
        for index, (source, grads) in enumerate(chain):
            work.append(functools.partial(fetch, (source, weight, 0)))
            work.append(back_sum(index, grads))
        work.append(before_norm)
        work.append(Loop(row_count // ROWS_AT_ONCE, norm_one))
        work.append(tokens_out.start)
        work.append(tokens_out.wait)
        return work

    def block_of(lane):
        cols = pl.ds(lane.column, lane.columns)
        if lane.array == 0:
            target = results.down.at[pl.ds(lane.part * channels, channels), cols]
            return results.own_down.at[lane.part, :, cols], target
        if lane.array == 1:
            target = results.up.at[:, pl.ds(lane.part * channels + lane.column, lane.columns)]
            return results.own_up.at[lane.part, :, cols], target
        if lane.array == 2:
            return results.own_out.at[0, :, cols], results.out.at[:, cols]
        source = (grad_query, grad_value, grad_key, small)[lane.array - 3]
        return source.at[:, cols], results[lane.array].at[:, cols]

    pending = [exchange(level).wait_send for level in range(levels)]
    pending.append(lambda: pl.when(me > 0)(edge(me - 1).wait_send))
    programs = []
    start = 0
    for lane in lanes:
        source, target = block_of(lane)
        programs.append(
            lane_steps(
                lane,
                line,
                source,
                target,
                take(len(lane.buffers(line))),
                stages,
                semaphores,
                start,
                pending,
            )
        )
        start += lane.copies(line)

    def vmem(*shape, kind=full):
        return pltpu.VMEM(shape, kind)

    count = work_steps(row_count, channels, hidden, levels)
    runner = Runner(lanes, programs, count, order)
    done = [0]

    def run(make):
        def scoped(*refs):
            work = make(*refs)
            done[0] += steps_in(work)
            runner.run(work)

        return scoped

    pl.run_scoped(
        run(feed_forward),
        vmem(2, channels, HIDDEN_AT_ONCE, kind=low),
        vmem(2, HIDDEN_AT_ONCE, channels, kind=low),
        vmem(row_count, HIDDEN_AT_ONCE, kind=low),
        vmem(row_count, HIDDEN_AT_ONCE, kind=low),
        vmem(row_count, HIDDEN_AT_ONCE),
        vmem(HIDDEN_AT_ONCE, channels),
        vmem(channels, HIDDEN_AT_ONCE),
        vmem(128, channels),
        vmem(128, channels),
        vmem(128, LANES),
    )
    cells = states * CHUNKS
    pl.run_scoped(
        run(mixer),
        vmem(2, row_count, LANES),
        vmem(2, row_count, LANES),
        vmem(2, row_count + halo * CHUNKS, LANES),
        vmem(2, cells, LANES),
        vmem(row_count, LANES),
        vmem(row_count, LANES),
        vmem(tiles, cells, LANES),
        vmem(cells, LANES),
        vmem(states, LANES),
        vmem(states, LANES),
        vmem(width, LANES),
    )
    assert done[0] == count
    call_all(runner.lanes())
    call_all(pending)


def work_steps(row_count, channels, hidden, levels):
    tiles, weights = channels // LANES, channels // 256
    first = 2 + 4 * (hidden // HIDDEN_AT_ONCE) + 2 * (row_count // 128) + weights
    second = 6 * tiles + 3 * weights + levels + 6 + 3 * (row_count // 128)
    return first + second + row_count // ROWS_AT_ONCE + 3


def backward(row_count, arrays, plan, order):
    size, line = lax.axis_size("seq"), lax.axis_size("batch")
    bits = [1 << place for place in range(size.bit_length() - 1)]
    channels, hidden = arrays.up_weight.shape
    states = arrays.rate.shape[0]
    tap_count = arrays.taps.shape[0]
    misc_rows = 2 * states + tap_count + 5
    small_rows = misc_rows + -misc_rows % (8 * size)
    full, low = jnp.float32, jnp.bfloat16
    parts = hidden // channels
    lanes = []
    for index, pieces in enumerate(plan):
        columns = channels if index == 6 else channels // 2
        for piece, (flipped, line_first) in enumerate(pieces):
            rows = small_rows if index == 6 else channels
            if rows % (8 * size * line):
                line_first = False
            path = bits[:0:-1] if flipped else bits[1:]
            lane = Lane(rows, columns, path, line_first, index > 2)
            lane.array, lane.part, lane.column = index, piece // 2, piece % 2 * columns
            lanes.append(lane)
    square = ((channels, channels), full)
    wide = ((row_count, channels), full)
    low_wide = ((row_count, channels), low)
    small = ((small_rows, channels), full)
    key_rows = arrays.key_rows.shape[0]
    one = ((states, channels), full)
    scratch = [square] * 3 + [small, ((key_rows, channels), full), wide, wide]
    scratch += [low_wide] * 3 + [((channels, channels), low)]
    scratch += [one] + [((8, channels), full)] * 2 + [((channels // 2, channels // 2), full)] * (STAGES + 1)
    scratch += [one] * (2 * len(bits))
    scratch = [pltpu.VMEM(*shape) for shape in scratch]
    scratch += [buffer for lane in lanes for buffer in lane.buffers(line)]
    copies = sum(lane.copies(line) for lane in lanes)
    counts = [21 + STAGES, len(bits) + 1, len(bits) + 1]
    outs = [((hidden, channels), full), ((channels, hidden), full)] + [square] * 4
    outs += [small, wide, low_wide]
    outs += [((parts, channels, channels), full)] * 2 + [((1, channels, channels), full)]
    found = pl.pallas_call(
        functools.partial(backward_body, row_count, size, line, bits, lanes, order),
        out_shape=[jax.ShapeDtypeStruct(*out) for out in outs],
        in_specs=[pl.BlockSpec(memory_space=pltpu.HBM)] * FAR
        + [pl.BlockSpec(memory_space=pltpu.VMEM)] * (len(BackwardIn._fields) - FAR),
        out_specs=[pl.BlockSpec(memory_space=pltpu.HBM)] * len(outs),
        scratch_shapes=scratch
        + [pltpu.SemaphoreType.DMA((copies,)), pltpu.SemaphoreType.DMA((copies,))]
        + [pltpu.SemaphoreType.REGULAR((copies,))]
        + [pltpu.SemaphoreType.DMA((count,)) for count in counts],
        compiler_params=pltpu.CompilerParams(
            collective_id=0, has_side_effects=True, vmem_limit_bytes=VMEM_LIMIT
        ),
    )(*[getattr(arrays, name) for name in BackwardIn._fields])
    return Results(*found)


def finish_body(row_count, states, tap_count, *refs):
    width = row_count // CHUNKS
    count = 9
    sources, targets = Results(*refs[:count], None, None, None), refs[count:]
    large, (mixed_out, tokens) = targets[:6], targets[6:8]
    (taps, coef, rate, skip, gain_one, bias_one, gain_two, bias_two) = targets[8:16]
    held_small, held_mixed, held_tokens, load_sems, store_sems = targets[16:21]
    passing = targets[21:]
    tiles = held_tokens.shape[0]
    pairs = [(sources.small, held_small), (sources.mixed_out, held_mixed)]
    for tile in range(tiles):
        pairs.append((sources.tokens.at[:, pl.ds(tile * LANES, LANES)], held_tokens.at[tile]))
    loads, stores = [], []
    for source, held, target in zip(sources[:6], passing, large):
        size = PASSING_SIZE // target.shape[1]
        for start in range(0, target.shape[0], size):
            rows = pl.ds(start, size)
            stores.append((held.at[rows, :], target.at[rows, :]))
            loads.append((source.at[rows, :], held.at[rows, :]))
    stores = [pltpu.make_async_copy(*pair, store_sems.at[i]) for i, pair in enumerate(stores)]
    copies = [pltpu.make_async_copy(*pair, load_sems.at[i]) for i, pair in enumerate(pairs + loads)]
    first_large = len(pairs)
    for copy in copies:
        copy.start()
    moves = list(zip(copies[first_large:], stores))

    def move(count):
        for load, store in moves[:count]:
            load.wait()
            store.start()
        del moves[:count]

    copies[0].wait()
    misc = 2 * states
    first = misc + tap_count
    coef[...] = held_small[0:states, :]
    rate[...] = held_small[states:misc, :]
    taps[...] = held_small[misc:first, :]
    for row, target in enumerate((skip, gain_one, bias_one, gain_two, bias_two)):
        target[...] = held_small[first + row, :]
    for copy in copies[1:first_large]:
        copy.wait()

    for chunk in range(CHUNKS):
        rows = slice(chunk * width, (chunk + 1) * width)
        for tile in range(tiles):
            tokens[rows, tile * LANES : (tile + 1) * LANES] = held_tokens.at[tile][
                pl.ds(chunk, width, stride=CHUNKS), :
            ]
        if chunk % 2:
            move(1)
    token = lax.broadcasted_iota(jnp.int32, (128, row_count), 0)
    row = lax.broadcasted_iota(jnp.int32, (128, row_count), 1)
    for i in range(row_count // 128):
        at = token + i * 128
        chosen = row == lax.rem(at, width) * CHUNKS + lax.div(at, width)
        picks = jnp.where(chosen, 1.0, 0.0).astype(jnp.bfloat16)
        mixed_out[i * 128 : (i + 1) * 128, :] = jnp.dot(
            picks, held_mixed[...], preferred_element_type=jnp.float32
        ).astype(jnp.bfloat16)
        move(2)
    move(len(moves))
    for store in stores:
        store.wait()


PASSING_SIZE = 384 * 768


def finish(row_count, states, tap_count, found):
    channels = found.small.shape[1]
    full = jnp.float32
    wide = (row_count, channels)
    shapes = [(array.shape, full) for array in found[:6]]
    shapes += [(wide, jnp.bfloat16), (wide, full), ((tap_count, channels), full)]
    shapes += [((states, channels), full)] * 2 + [((channels,), full)] * 5
    tiles = channels // LANES
    scratch = [(found.small.shape, full), (wide, jnp.bfloat16), ((tiles, row_count, LANES), full)]
    pieces = sum(array.size // PASSING_SIZE for array in found[:6])
    counts = [2 + tiles + pieces, pieces]
    memory = [pltpu.HBM] * 6 + [pltpu.VMEM] * 10
    return pl.pallas_call(
        functools.partial(finish_body, row_count, states, tap_count),
        out_shape=[jax.ShapeDtypeStruct(*shape) for shape in shapes],
        in_specs=[pl.BlockSpec(memory_space=pltpu.HBM)] * 9,
        out_specs=[pl.BlockSpec(memory_space=space) for space in memory],
        scratch_shapes=[pltpu.VMEM(*shape) for shape in scratch]
        + [pltpu.SemaphoreType.DMA((count,)) for count in counts]
        + [pltpu.VMEM(array.shape, full) for array in found[:6]],
        compiler_params=pltpu.CompilerParams(vmem_limit_bytes=VMEM_LIMIT),
    )(*found[:9])


PLAN = [
    [(True, False), (True, False), (True, True), (False, False), (False, False), (True, False), (True, False), (True, False)],
    [(False, False), (True, True), (False, False), (False, True), (False, False), (True, True), (False, True), (False, False)],
    [(True, False), (False, True)],
    [(False, True), (False, False)],
    [(True, False), (False, False)],
    [(False, True), (True, False)],
    [(False, False)],
]
ORDER = [
    25, 25, 25, 25, 25, 25, 25, 25, 25, 25, 25, 25, 8, 25, 25, 25, 25, 9, 1, 0, 25, 25, 8, 25,
    25, 25, 9, 25, 1, 0, 25, 25, 10, 25, 25, 25, 25, 2, 11, 3, 25, 25, 10, 8, 25, 25, 2, 9, 25,
    11, 1, 25, 3, 25, 25, 12, 25, 25, 25, 9, 25, 4, 5, 13, 25, 10, 12, 0, 25, 25, 2, 4, 1, 8,
    25, 5, 9, 13, 25, 25, 10, 25, 25, 2, 14, 25, 25, 7, 6, 15, 3, 25, 14, 11, 2, 7, 5, 25, 9,
    12, 6, 15, 25, 11, 1, 2, 0, 3, 25, 8, 25, 25, 25, 7, 17, 11, 1, 4, 25, 8, 5, 13, 25, 17, 9,
    12, 25, 1, 25, 10, 13, 8, 25, 2, 6, 15, 25, 7, 4, 13, 14, 10, 25, 9, 11, 8, 25, 1, 15, 25,
    2, 14, 10, 0, 13, 9, 25, 11, 6, 3, 25, 25, 25, 25, 18, 19, 16, 25, 14, 0, 5, 1, 18, 8, 13,
    19, 2, 16, 17, 0, 3, 10, 25, 11, 14, 5, 13, 12, 3, 16, 7, 5, 17, 19, 25, 14, 4, 25, 17, 0,
    13, 25, 12, 15, 25, 3, 25, 9, 25, 7, 19, 11, 10, 25, 14, 6, 4, 25, 12, 25, 25, 5, 25, 18,
    17, 15, 0, 25, 7, 25, 12, 25, 9, 25, 2, 25, 4, 3, 25, 14, 25, 17, 6, 5, 13, 25, 7, 15, 25,
    18, 19, 17, 4, 25, 9, 25, 11, 25, 12, 25, 2, 17, 25, 25, 25, 7, 25, 25, 21, 20, 16, 14, 6,
    15, 25, 25, 21, 25, 20, 4, 25, 13, 25, 25, 19, 6, 25, 18, 25, 25, 25, 22, 23, 25, 11, 25,
    25, 25, 25, 22, 20, 15, 25, 2, 23, 25, 25, 25, 25, 25, 17, 25, 25, 25, 21, 6, 25, 25, 25,
    14, 25, 18, 22, 25, 25, 25, 25, 13, 25, 20, 25, 24, 25, 25, 23, 19, 22, 16, 24, 21, 20, 18,
    11, 23, 19, 16, 17, 18, 21, 24, 20, 14, 23, 24, 21, 22, 19, 24, 23, 16, 18, 22, 17, 24, 22,
    16, 20, 22, 21, 20, 23, 22, 16, 18, 21, 24, 23, 22, 20, 18, 24, 21, 22, 18, 24, 23, 22,
]


def on_device(
    tokens,
    norm1_gain,
    norm1_bias,
    query_weight,
    key_weight,
    value_weight,
    shift_taps,
    ssm_coef,
    ssm_rate,
    ssm_skip,
    out_weight,
    norm2_gain,
    norm2_bias,
    up_weight,
    down_weight,
    out_grad,
):
    unused, row_count, channels = tokens.shape
    states = ssm_rate.shape[0]
    tap_count = shift_taps.shape[0]

    arrays = SimpleNamespace(
        tokens=tokens[0],
        token_grads=out_grad[0],
        skip=ssm_skip,
        gain_one=norm1_gain,
        bias_one=norm1_bias,
        gain_two=norm2_gain,
        bias_two=norm2_bias,
        query_weight=query_weight,
        key_weight=key_weight,
        value_weight=value_weight,
        out_weight=out_weight,
        up_weight=up_weight,
        down_weight=down_weight,
        taps=shift_taps,
        rate=ssm_rate,
        coef=ssm_coef,
    )
    vars(arrays).update(forward(row_count, arrays)._asdict())
    found = backward(row_count, arrays, PLAN, ORDER)
    (down, up, out, query, value, key, mixed_out, grad_tokens, *rest) = finish(
        row_count, states, tap_count, found
    )
    (taps, coef, rate, skip, gain_one, bias_one, gain_two, bias_two) = rest
    return (
        mixed_out[None],
        grad_tokens[None],
        gain_one,
        bias_one,
        query,
        key,
        value,
        taps,
        coef,
        rate,
        skip,
        out,
        gain_two,
        bias_two,
        up,
        down,
    )


def solution(mesh):
    placed = (P("batch", "seq", None),) + (P(),) * 14 + (P("batch", "seq", None),)
    return jax.shard_map(
        on_device,
        mesh=mesh,
        in_specs=placed,
        out_specs=(P("batch", "seq", None),) * 2 + (P(),) * 14,
        check_vma=False,
    )
```

```python
import functools
import math
from types import SimpleNamespace
from typing import Any, NamedTuple

import jax
import jax.numpy as jnp
from jax import lax
from jax.experimental import pallas as pl
from jax.experimental.pallas import tpu as pltpu
from jax.sharding import PartitionSpec as P

epsilon = 1e-05
CHUNKS = 16
GROUP = 8
LANES = 128

VMEM_LIMIT = 64 * 2**20
ROWS_AT_ONCE = 64


def standardize(values):
    row_mean = jnp.mean(values, axis=-1, keepdims=True)
    centered = values - row_mean
    spread = jnp.mean(centered * centered, axis=-1, keepdims=True)
    factor = lax.rsqrt(spread + epsilon)
    return centered * factor, factor


def norm_back(grads, gain, standard, factor):
    scaled = grads * gain
    return factor * (
        scaled
        - jnp.mean(scaled, axis=-1, keepdims=True)
        - standard * jnp.mean(scaled * standard, axis=-1, keepdims=True)
    )


def project_back(grads_low, weight):
    return lax.dot_general(
        grads_low, weight, (((1,), (1,)), ((), ())), preferred_element_type=jnp.float32
    )


def weight_grad(rows_low, grads_low):
    return lax.dot_general(
        rows_low, grads_low, (((0,), (0,)), ((), ())), preferred_element_type=jnp.float32
    )


def block(ref, place):
    return ref[place * CHUNKS : (place + 1) * CHUNKS, :]


def chunk_rows(chunk, states):
    return pl.ds(chunk, states, stride=CHUNKS)


def state_sums(width, rows_ref, decay_ref, out_ref, group, places, weight, lead):
    decay = decay_ref[pl.ds(group * GROUP, GROUP), :][:, None, :]
    running = jnp.zeros((GROUP, CHUNKS, LANES), jnp.float32)
    for place in places:
        rows = block(rows_ref, place)
        if weight is not None:
            rows = rows * weight(place)
        running = decay * (running + rows[None]) if lead else decay * running + rows[None]
    return running


def forward_states(width, rows_ref, rate_ref, sums_ref, last_ref, decay_ref):
    states = rate_ref.shape[0]
    decay_ref[...] = jnp.exp(-rate_ref[...])

    def body(group, unused):
        running = state_sums(width, rows_ref, decay_ref, None, group, range(width), None, False)
        sums_ref[pl.ds(group * GROUP * CHUNKS, GROUP * CHUNKS), :] = running.reshape(-1, LANES)
        return unused

    lax.fori_loop(0, states // GROUP, body, 0)
    hop = jnp.exp(-width * rate_ref[...])
    held = jnp.zeros((states, LANES), jnp.float32)
    for chunk in range(CHUNKS):
        held = hop * held + sums_ref[chunk_rows(chunk, states), :]
    last_ref[...] = held


def forward_near(
    width, rows_ref, rate_ref, coef_ref, skip_ref, mixed_ref, kernel_ref, taps_ref
):
    states = rate_ref.shape[0]
    lags = lax.broadcasted_iota(jnp.int32, (8, LANES), 0).astype(jnp.float32)

    def add_states(group, totals):
        members = pl.ds(pl.multiple_of(group * GROUP, GROUP), GROUP)
        rates, coefs = rate_ref[members, :], coef_ref[members, :]
        steps = jnp.exp(-8.0 * rates)
        totals = list(totals)
        for i in range(GROUP):
            term = coefs[i : i + 1] * jnp.exp(-rates[i : i + 1] * lags)
            for place in range(width // 8):
                totals[place] = totals[place] + term
                term = term * steps[i : i + 1]
        return tuple(totals)

    zero = jnp.zeros((8, LANES), jnp.float32)
    totals = lax.fori_loop(0, states // GROUP, add_states, (zero,) * (width // 8))
    kernel_ref[...] = jnp.concatenate(totals, axis=0)
    for lag in range(width):
        taps_ref[lag * CHUNKS : (lag + 1) * CHUNKS, :] = jnp.broadcast_to(
            kernel_ref[lag : lag + 1, :], (CHUNKS, LANES)
        )
    for start in range(0, width, 4):
        sums = [skip_ref[...] * block(rows_ref, start + i) for i in range(4)]
        for place in range(start + 4):
            rows = block(rows_ref, place)
            for i in range(4):
                if start + i >= place:
                    sums[i] = sums[i] + block(taps_ref, start + i - place) * rows
        for i in range(4):
            mixed_ref[(start + i) * CHUNKS : (start + i + 1) * CHUNKS, :] = sums[i]


def forward_far(
    width, sums_ref, entering_ref, rate_ref, coef_ref, mixed_ref, held_ref, decay_ref
):
    states = rate_ref.shape[0]
    decay_ref[...] = jnp.exp(-rate_ref[...])
    hop = jnp.exp(-width * rate_ref[...])
    held = entering_ref[...]
    for chunk in range(CHUNKS):
        held_ref[chunk_rows(chunk, states), :] = held
        held = hop * held + sums_ref[chunk_rows(chunk, states), :]

    def body(group, unused):
        decay = decay_ref[pl.ds(group * GROUP, GROUP), :][:, None, :]
        coef = coef_ref[pl.ds(group * GROUP, GROUP), :][:, None, :]
        term = held_ref[pl.ds(group * GROUP * CHUNKS, GROUP * CHUNKS), :].reshape(
            GROUP, CHUNKS, LANES
        )
        term = term * (coef * decay)
        for place in range(width):
            mixed_ref[place * CHUNKS : (place + 1) * CHUNKS, :] += jnp.sum(term, axis=0)
            if place < width - 1:
                term = term * decay
        return unused

    lax.fori_loop(0, states // GROUP, body, 0)


def backward_states(width, grads_ref, rate_ref, sums_ref, first_ref, decay_ref):
    states = rate_ref.shape[0]
    decay_ref[...] = jnp.exp(-rate_ref[...])

    def body(group, unused):
        running = state_sums(
            width, grads_ref, decay_ref, None, group, range(width - 1, -1, -1), None, True
        )
        sums_ref[pl.ds(group * GROUP * CHUNKS, GROUP * CHUNKS), :] = running.reshape(-1, LANES)
        return unused

    lax.fori_loop(0, states // GROUP, body, 0)
    hop = jnp.exp(-width * rate_ref[...])
    held = jnp.zeros((states, LANES), jnp.float32)
    for chunk in range(CHUNKS - 1, -1, -1):
        held = hop * held + sums_ref[chunk_rows(chunk, states), :]
    first_ref[...] = held


def backward_near(
    width,
    grads_ref,
    rows_ref,
    sums_ref,
    entering_ref,
    rate_ref,
    skip_ref,
    kernel_ref,
    back_ref,
    coef_grad_ref,
    rate_grad_ref,
    decay_ref,
    hop_ref,
    taps_ref,
    after_ref,
    lag_ref,
):
    states = rate_ref.shape[0]
    hop = jnp.exp(-width * rate_ref[...])
    hop_ref[...] = hop
    held = entering_ref[...]
    for chunk in range(CHUNKS - 1, -1, -1):
        after_ref[chunk_rows(chunk, states), :] = held
        held = hop * held + sums_ref[chunk_rows(chunk, states), :]
    for lag in range(width):
        taps_ref[lag * CHUNKS : (lag + 1) * CHUNKS, :] = jnp.broadcast_to(
            kernel_ref[lag : lag + 1, :], (CHUNKS, LANES)
        )
    for start in range(0, width, 4):
        sums = [skip_ref[...] * block(grads_ref, start + i) for i in range(4)]
        for place in range(start, width):
            grads = block(grads_ref, place)
            for i in range(4):
                if place >= start + i:
                    sums[i] = sums[i] + block(taps_ref, place - start - i) * grads
        for i in range(4):
            back_ref[(start + i) * CHUNKS : (start + i + 1) * CHUNKS, :] = sums[i]
    for start in range(0, width, 4):
        sums = [jnp.zeros((CHUNKS, LANES), jnp.float32) for i in range(4)]
        for place in range(start, width):
            grads = block(grads_ref, place)
            for i in range(4):
                if place >= start + i:
                    sums[i] = sums[i] + block(rows_ref, place - start - i) * grads
        for i in range(4):
            lag_ref[start + i : start + i + 1, :] = jnp.sum(sums[i], axis=0, keepdims=True)
    decay_all = decay_ref[...]
    near_coef = jnp.zeros((states, LANES), jnp.float32)
    near_rate = jnp.zeros((states, LANES), jnp.float32)
    for lag in range(width - 1, -1, -1):
        near_coef = near_coef * decay_all + lag_ref[lag : lag + 1, :]
        near_rate = near_rate * decay_all + float(lag) * lag_ref[lag : lag + 1, :]
    coef_grad_ref[...] = near_coef
    rate_grad_ref[...] = near_rate


def backward_far(
    width,
    grads_ref,
    rows_ref,
    sums_ref,
    held_ref,
    coef_ref,
    back_ref,
    coef_grad_ref,
    rate_grad_ref,
    decay_ref,
    hop_ref,
    after_ref,
    groups,
):
    def body(group, unused):
        members = pl.ds(group * GROUP, GROUP)
        cells = pl.ds(group * GROUP * CHUNKS, GROUP * CHUNKS)
        cube = (GROUP, CHUNKS, LANES)
        decay = decay_ref[members, :][:, None, :]
        coef = coef_ref[members, :][:, None, :]
        after = after_ref[cells, :].reshape(cube)
        term = after * coef
        for place in range(width - 1, -1, -1):
            back_ref[place * CHUNKS : (place + 1) * CHUNKS, :] += jnp.sum(term, axis=0)
            if place > 0:
                term = term * decay
        held = held_ref[cells, :].reshape(cube)
        coef_grad_ref[members, :] += jnp.sum(held * sums_ref[cells, :].reshape(cube), axis=1)
        slope = state_sums(
            width,
            rows_ref,
            decay_ref,
            None,
            group,
            range(width),
            lambda place: float(width - 1 - place),
            False,
        )
        total = after * (float(width) * hop_ref[members, :][:, None, :] * held + slope)
        slope = state_sums(
            width,
            grads_ref,
            decay_ref,
            None,
            group,
            range(width - 1, -1, -1),
            lambda place: float(place + 1),
            True,
        )
        total = total + held * slope
        rate_grad_ref[members, :] += jnp.sum(total, axis=1)
        return unused

    lax.fori_loop(groups.start, groups.stop, body, 0)


MESH = pl.DeviceIdType.MESH


def add_rows(out_ref, out_start, a_ref, a_start, b_ref, b_start, rows):
    columns = out_ref.shape[1]
    size = 8
    for option in (16, 24, 32, 48, 64):
        if rows % option == 0 and option * columns <= 64 * 1024:
            size = option

    def body(i, unused):
        at = i * size
        out_ref[pl.ds(pl.multiple_of(out_start + at, 8), size), :] = (
            a_ref[pl.ds(pl.multiple_of(a_start + at, 8), size), :]
            + b_ref[pl.ds(pl.multiple_of(b_start + at, 8), size), :]
        )
        return unused

    lax.fori_loop(0, rows // size, body, 0)


class Lane:
    def __init__(self, rows, columns, bits, line_first, in_place):
        self.rows, self.columns = rows, columns
        self.bits, self.line_first, self.in_place = bits, line_first, in_place

    def buffers(self, line):
        half = self.rows // 2
        unit = half // line if self.line_first else half >> len(self.bits)
        counts = [half]
        size = half // line if self.line_first else half
        for unused in self.bits:
            size //= 2
            counts.append(size)
        counts.append(unit * (line + 1 if self.line_first else max(1, line // 2)))
        return [pltpu.VMEM((count, self.columns), jnp.float32) for count in counts]

    def copies(self, line):
        chain = 4 * line + 3 if self.line_first else line
        return 4 + 2 * len(self.bits) + chain


def lane_steps(
    lane, line, source, target, buffers, stages, semaphores, first_sem, pending
):
    send_sems, recv_sems, free_sems = semaphores
    first, chain = buffers[0], buffers[-1]
    landing = buffers[1:-1]
    acc = source if lane.in_place else first
    me = lax.axis_index("seq")
    z = lax.axis_index("batch")
    half = lane.rows // 2
    core = me % 2
    counter = [first_sem]

    def fresh():
        counter[0] += 1
        return counter[0] - 1

    def remote(src, dst, index, device):
        return pltpu.make_async_remote_copy(
            src_ref=src,
            dst_ref=dst,
            send_sem=send_sems.at[index],
            recv_sem=recv_sems.at[index],
            device_id=device,
            device_id_type=MESH,
        )

    def rows_of(ref, start, count):
        if not isinstance(start, int):
            start = pl.multiple_of(start, 8)
        return ref.at[pl.ds(start, count), :]

    def side(bit):
        return (me // bit) % 2

    def partner(bit):
        return (me + bit * (1 - 2 * side(bit)), z)

    def free(index, device):
        pl.semaphore_signal(
            free_sems.at[index], inc=1, device_id=device, device_id_type=MESH
        )

    def wait_free(index):
        pl.semaphore_wait(free_sems.at[index], 1)

    mine, other = core * half, (1 - core) * half
    base_row = mine if lane.in_place else 0
    swap = remote(rows_of(source, other, half), first, fresh(), partner(1))

    def load():
        place = len(stages) - 1 if lane.stage is None else lane.stage
        return pltpu.make_async_copy(rows_of(source, mine, half), *stages[place])

    def begin():
        swap.start()
        if not lane.in_place and lane.stage is not None:
            load().start()

    def add_swap():
        if lane.in_place:
            swap.wait_recv()
            add_rows(acc, mine, acc, mine, first, 0, half)
        else:
            if lane.stage is None:
                load().start()
            swap.wait_recv()
            load().wait()
            add_rows(acc, 0, acc, 0, stages[-1 if lane.stage is None else lane.stage][0], 0, half)

    pending.append(swap.wait_send)
    steps = [[begin], [add_swap]]

    def join(function):
        steps[-1].append(function)

    def step(function):
        steps.append([function])

    def neighbours_sum(base, size):
        starts, indices = [base], []
        for place, bit in enumerate(lane.bits):
            size //= 2
            start, index = starts[-1], fresh()
            copy = remote(
                rows_of(acc, base_row + start + (1 - side(bit)) * size, size),
                landing[place],
                index,
                partner(bit),
            )
            own = start + side(bit) * size
            join(copy.start)

            def receive(copy=copy, own=own, size=size, place=place, bit=bit, index=index):
                copy.wait()
                free(index, partner(bit))
                add_rows(acc, base_row + own, acc, base_row + own, landing[place], 0, size)

            step(receive)
            starts.append(own)
            indices.append(index)
        return starts, size, indices

    def neighbours_spread(starts, size, indices):
        for place in range(len(lane.bits) - 1, -1, -1):
            rows = rows_of(acc, base_row + starts[place + 1], size)
            copy = remote(rows, rows, fresh(), partner(lane.bits[place]))
            join(functools.partial(wait_free, indices[place]))
            join(copy.start)
            pending.append(copy.wait_send)
            step(copy.wait_recv)
            size *= 2

    if not lane.line_first:
        starts, size, indices = neighbours_sum(0, half)
        at = starts[-1]
        depth = jnp.minimum(z, line - 1 - z)
        lower = z < line // 2
        inward = (me, jnp.where(lower, z + 1, z - 1))
        outward = (me, jnp.where(lower, z - 1, z + 1))
        across = (me, line - 1 - z)
        middle = line // 2 - 1

        def on(level, function):
            def guarded():
                pl.when(depth == level)(function)

            return guarded

        passed = []
        for level in range(middle):
            rows = rows_of(acc, base_row + at, size)
            passed.append(fresh())
            copy = remote(rows, rows_of(chain, level * size, size), passed[-1], inward)
            join(on(level, copy.start))

            def receive(copy=copy, level=level):
                copy.wait_recv()
                add_rows(acc, base_row + at, acc, base_row + at, chain, level * size, size)

            def release(copy=copy, index=passed[-1]):
                copy.wait_send()
                free(index, inward)

            step(on(level + 1, receive))
            join(on(level, release))
        rows = rows_of(acc, base_row + at, size)
        copy = remote(rows, rows_of(chain, middle * size, size), fresh(), across)
        join(on(middle, copy.start))

        def receive_across(copy=copy):
            copy.wait()
            add_rows(acc, base_row + at, acc, base_row + at, chain, middle * size, size)

        step(on(middle, receive_across))
        for level in range(middle - 1, -1, -1):
            rows = rows_of(acc, base_row + at, size)
            copy = remote(rows, rows, fresh(), outward)
            join(on(level + 1, functools.partial(wait_free, passed[level])))
            join(on(level + 1, copy.start))
            pending.append(on(level + 1, copy.wait_send))
            step(on(level, copy.wait_recv))
        neighbours_spread(starts, size, indices)
    else:
        unit = half // line
        slots = [fresh() for unused in range(line + 1)]
        outs = [[fresh() for unused in range(2)] for unused in range(line)]
        spreads = [fresh() for unused in range(line)]

        def on(place, function):
            def guarded():
                pl.when(z == place)(function)

            return guarded

        def beside(place):
            return (me, place - 1 if place > 0 else place + 1)

        def hop(place, member, step_to):
            slot = line if step_to < 0 and member == place - 1 else member
            return remote(
                rows_of(acc, base_row + member * unit, unit),
                rows_of(chain, slot * unit, unit),
                slots[slot],
                (me, place + step_to),
            )

        def arrived(place, slot, member):
            remote(
                rows_of(acc, base_row + member * unit, unit),
                rows_of(chain, slot * unit, unit),
                slots[slot],
                beside(place),
            ).wait_recv()
            row = base_row + member * unit
            add_rows(acc, row, acc, row, chain, slot * unit, unit)

        for turn in range(line - 1):

            def rightward(place=turn):
                for member in range(line - 1, place, -1):
                    if place > 0:
                        arrived(place, member, member)
                    hop(place, member, 1).start()

            def leftward(place=line - 1 - turn):
                for member in range(place):
                    if place < line - 1:
                        arrived(place, member, member)
                    hop(place, member, -1).start()

            if turn > 0:
                step(on(turn, rightward))
            else:
                join(on(turn, rightward))
            join(on(line - 1 - turn, leftward))

        to_right, to_left = fresh(), fresh()

        def collect(place):
            if place > 0:
                arrived(place, place, place)
            if place < line - 1:
                arrived(place, line, place)
            for member in range(line - 1, place, -1):
                hop(place, member, 1).wait_send()
            if place < line - 1:
                free(to_right, (me, place + 1))
            for member in range(place):
                hop(place, member, -1).wait_send()
            if place > 0:
                free(to_left, (me, place - 1))

        def collect_all():
            for place in range(line):
                on(place, functools.partial(collect, place))()

        step(collect_all)

        base = z * unit
        starts, size, indices = neighbours_sum(base, unit)
        neighbours_spread(starts, size, indices)

        def spread_at(place, distance, receive, send):
            members = {place - distance, place + distance}
            for member in sorted(members):
                if not 0 <= member < line:
                    continue
                if receive and distance > 0:
                    remote(
                        rows_of(acc, base_row + member * unit, unit),
                        rows_of(acc, base_row + member * unit, unit),
                        spreads[member],
                        beside(place),
                    ).wait_recv()
                if not send:
                    continue
                for step_to in (1, -1):
                    going = member <= place if step_to > 0 else member >= place
                    if going and 0 <= place + step_to < line:
                        yield member, step_to

        def pass_on(place, member, step_to):
            return pltpu.make_async_remote_copy(
                src_ref=rows_of(acc, base_row + member * unit, unit),
                dst_ref=rows_of(acc, base_row + member * unit, unit),
                send_sem=send_sems.at[outs[member][0 if step_to > 0 else 1]],
                recv_sem=recv_sems.at[spreads[member]],
                device_id=(me, place + step_to),
                device_id_type=MESH,
            )

        for distance in range(line):

            def forward(place, distance):
                if distance == 0 and place > 0:
                    wait_free(to_right)
                if distance == 0 and place < line - 1:
                    wait_free(to_left)
                for member, step_to in spread_at(place, distance, True, True):
                    pass_on(place, member, step_to).start()

            def forward_all(distance=distance):
                for place in range(line):
                    on(place, functools.partial(forward, place, distance))()

            if distance == 0:
                join(forward_all)
            else:
                step(forward_all)

        def gone(place):
            for distance in range(line):
                for member, step_to in spread_at(place, distance, False, True):
                    pass_on(place, member, step_to).wait_send()

        for place in range(line):
            pending.append(on(place, functools.partial(gone, place)))

    keep_index, give_index = fresh(), fresh()
    done = rows_of(acc, base_row, half)
    keep = pltpu.make_async_copy(done, rows_of(target, mine, half), recv_sems.at[keep_index])
    give = remote(done, rows_of(target, mine, half), give_index, partner(1))
    join(keep.start)
    join(give.start)
    pending.append(keep.wait)
    pending.append(give.wait)
    assert counter[0] - first_sem <= lane.copies(line)
    return steps


def turn_order(lengths, order):
    if [order.count(place) for place in range(len(lengths))] == lengths:
        return order
    last = len(lengths) - 1
    turns = range(max(lengths[:-1], default=0))
    lanes = [place for turn in turns for place in range(last) if turn < lengths[place]]
    return [last] * lengths[last] + lanes


class Loop:
    def __init__(self, count, *parts):
        self.count, self.parts = count, parts

    def steps(self):
        return self.count * len(self.parts)


def call_all(functions):
    for function in functions:
        function()


def run_loop(loop, between):
    parts = len(loop.parts)

    def body(i, unused):
        for place, part in enumerate(loop.parts):
            part(i)
            for turn in range(loop.count):
                functions = between[turn * parts + place]
                if functions:
                    pl.when(i == turn)(functools.partial(call_all, functions))
        return unused

    lax.fori_loop(0, loop.count, body, 0)


def give_stages(lanes, order, count):
    free, seen = list(range(count)), [0] * len(lanes)
    for place in order:
        if place == len(lanes) or lanes[place].in_place:
            continue
        seen[place] += 1
        lane = lanes[place]
        if seen[place] == 1:
            lane.stage = free.pop() if free else None
        elif seen[place] == 2 and lane.stage is not None:
            free.append(lane.stage)


class Runner:
    def __init__(self, lanes, programs, count, order):
        lengths = [len(program) for program in programs] + [count]
        self.programs = [list(program) for program in programs]
        self.order = turn_order(lengths, order)
        give_stages(lanes, self.order, STAGES)
        self.work_place = len(programs)
        self.at = 0

    def lanes(self):
        functions = []
        while self.at < len(self.order) and self.order[self.at] != self.work_place:
            functions += self.programs[self.order[self.at]].pop(0)
            self.at += 1
        return functions

    def run(self, work):
        for item in work:
            call_all(self.lanes())
            self.at += 1
            if not isinstance(item, Loop):
                item()
                continue
            between = []
            for unused in range(item.steps() - 1):
                between.append(self.lanes())
                self.at += 1
            run_loop(item, between + [[]])


def steps_in(work):
    return sum(item.steps() if isinstance(item, Loop) else 1 for item in work)


def state_exchange(bits, row_count, rate, totals, arrivals, entering, sends, receives, forward):
    me, z = lax.axis_index("seq"), lax.axis_index("batch")

    def copy(level):
        bit = bits[level]
        return pltpu.make_async_remote_copy(
            src_ref=totals[level],
            dst_ref=arrivals[level],
            send_sem=sends[level],
            recv_sem=receives[level],
            device_id=(me + bit * (1 - 2 * ((me // bit) % 2)), z),
            device_id_type=MESH,
        )

    def arrive(level):
        bit = bits[level]
        copy(level).wait_recv()
        place = me % bit
        after = (me // bit) % 2 == (1 if forward else 0)
        hops = (row_count * (place if forward else bit - 1 - place)).astype(jnp.float32)
        term = jnp.exp(-rate[...] * hops) * arrivals[level][...]
        term = jnp.where(after, term, 0.0)
        entering[...] = term if level == 0 else entering[...] + term
        if level + 1 < len(bits):
            far = jnp.exp(-float(row_count * bit) * rate[...])
            ours, theirs = totals[level][...], arrivals[level][...]
            totals[level + 1][...] = jnp.where(after, ours + far * theirs, theirs + far * ours)
            copy(level + 1).start()

    return copy, arrive


def lane_columns(tile):
    return pl.ds(pl.multiple_of(tile * LANES, LANES), LANES)


def row_block(i, count):
    return pl.ds(pl.multiple_of(i * count, count), count)


SKIP, GAIN_ONE, BIAS_ONE, GAIN_TWO, BIAS_TWO = range(5)


def vector(ref, place):
    return ref[place : place + 1, :]


class ForwardIn(NamedTuple):
    tokens: Any
    token_grads: Any
    skip: Any
    gain_one: Any
    bias_one: Any
    gain_two: Any
    bias_two: Any
    query_weight: Any
    key_weight: Any
    value_weight: Any
    out_weight: Any
    taps: Any
    rate: Any
    coef: Any


class ForwardOut(NamedTuple):
    product: Any
    held: Any
    kernel: Any
    values: Any
    keys_mixed: Any
    key_rows: Any
    queries: Any
    mixed: Any
    gated: Any
    middle: Any
    normed_two: Any
    standard_two: Any
    factor_two: Any
    normed_one: Any
    standard_one: Any
    factor_one: Any
    out_grad: Any
    vectors: Any


def forward_body(row_count, size, bits, *refs):
    width = row_count // CHUNKS
    levels = len(bits)
    taken, outs = len(ForwardIn._fields), len(ForwardOut._fields)
    given = ForwardIn(*refs[:taken])
    results = ForwardOut(*refs[taken : taken + outs])
    own = ForwardOut(*refs[taken + outs : taken + 2 * outs])
    refs = refs[taken + 2 * outs :]
    brought, refs = refs[:4], refs[4:]
    sums, taps, decay, entering, edge_out, edge_in = refs[:6]
    totals, arrivals = refs[6 : 6 + levels], refs[6 + levels : 6 + 2 * levels]
    sends, receives, keeps = refs[-3:]
    vectors = own.vectors
    rate, coef, skip = given.rate, given.coef, vectors.at[0:1]
    channels = rate.shape[1]
    tiles = channels // LANES
    tap_count = given.taps.shape[0]
    halo = tap_count - 1
    low = jnp.bfloat16
    me, z = lax.axis_index("seq"), lax.axis_index("batch")
    barrier = pltpu.get_barrier_semaphore()

    def greet(device):
        pl.semaphore_signal(barrier, inc=1, device_id=device, device_id_type=MESH)

    for bit in bits:
        greet((me + bit * (1 - 2 * ((me // bit) % 2)), z))
    pl.when(me > 0)(lambda: greet((me - 1, z)))
    pl.when(me < size - 1)(lambda: greet((me + 1, z)))

    kept = ForwardOut(
        *[
            pltpu.make_async_copy(own[i], results[i], keeps.at[i])
            for i in range(len(ForwardOut._fields))
        ]
    )

    def half_exchange(part):
        size_of = channels // 2
        here = pl.ds(part * size_of, size_of)
        first = part * levels
        return state_exchange(
            bits,
            row_count,
            rate.at[:, here],
            [total.at[:, here] for total in totals],
            [arrival.at[:, here] for arrival in arrivals],
            entering.at[:, here],
            [sends.at[first + level] for level in range(levels)],
            [receives.at[first + level] for level in range(levels)],
            True,
        )

    halves = [half_exchange(0), half_exchange(1)]

    def begin_half(part):
        return halves[part][0](0).start

    def arrive_half(part, level):
        return functools.partial(halves[part][1], level)

    def edge(device):
        return pltpu.make_async_remote_copy(
            src_ref=edge_out,
            dst_ref=edge_in,
            send_sem=sends.at[2 * levels],
            recv_sem=receives.at[2 * levels],
            device_id=(device, z),
            device_id_type=MESH,
        )

    def reordered(rows, i):
        shape = (128, row_count)
        row = i * 128 + lax.broadcasted_iota(jnp.int32, shape, 0)
        token = lax.rem(row, CHUNKS) * width + lax.div(row, CHUNKS)
        chosen = lax.broadcasted_iota(jnp.int32, shape, 1) == token
        picks = jnp.where(chosen, 1.0, 0.0).astype(low)
        return jnp.dot(picks, rows[...], preferred_element_type=jnp.float32)

    far = (given.key_weight, given.value_weight, given.query_weight, given.out_weight)
    weights = [
        pltpu.make_async_copy(far[i], brought[i], keeps.at[len(ForwardOut._fields) + i])
        for i in range(4)
    ]
    for weight in weights:
        weight.start()

    def norm_rows(i):
        rows = row_block(i, 128)
        inputs = reordered(given.tokens, i)
        own.middle[rows, :] = inputs
        standard, factor = standardize(inputs)
        own.standard_one[rows, :] = standard
        own.factor_one[rows, :] = jnp.broadcast_to(factor, (128, LANES))
        own.normed_one[rows, :] = (
            standard * vector(vectors, GAIN_ONE) + vector(vectors, BIAS_ONE)
        ).astype(low)

    def grad_rows(i):
        own.out_grad[row_block(i, 128), :] = reordered(given.token_grads, i).astype(low)

    def project_to(target, weight, lead):
        def body(i):
            cols = row_block(i, 256)
            target[lead : lead + row_count, cols] = jnp.dot(
                own.normed_one[...], weight[:, cols], preferred_element_type=jnp.float32
            )

        return Loop(channels // 256, body)

    lead = halo * CHUNKS

    def send_edge():
        edge_out[...] = jnp.zeros(edge_out.shape, jnp.float32)
        for i in range(halo):
            row = lead + (width - halo + i) * CHUNKS + CHUNKS - 1
            edge_out[i : i + 1, :] = own.key_rows[row : row + 1, :]
        pl.semaphore_wait(
            barrier, levels + jnp.where(me > 0, 1, 0) + jnp.where(me < size - 1, 1, 0)
        )
        pl.when(me < size - 1)(edge(me + 1).start)

        @pl.when(me == 0)
        def at_start():
            edge_in[...] = jnp.zeros(edge_in.shape, jnp.float32)

    def take_edge():
        pl.when(me > 0)(edge(me - 1).wait_recv)

    def states_tile(tile):
        here = lane_columns(tile)
        keys, tap = own.key_rows, given.taps
        for i in range(halo):
            row = lead + (width - halo + i) * CHUNKS
            rows = keys[row : row + CHUNKS, here]
            keys[i * CHUNKS : (i + 1) * CHUNKS, here] = jnp.concatenate(
                [edge_in[i : i + 1, here], rows[: CHUNKS - 1]], axis=0
            )
        total = tap[0:1, here] * keys[lead : lead + row_count, here]
        for offset in range(1, tap_count):
            start = lead - offset * CHUNKS
            total = total + tap[offset : offset + 1, here] * keys[start : start + row_count, here]
        own.keys_mixed[:, here] = total
        own.product[:, here] = total * own.values[:, here]
        forward_states(
            width,
            own.product.at[:, here],
            rate.at[:, here],
            sums.at[tile],
            totals[0].at[:, here],
            decay,
        )

    def near_tile(tile):
        here = lane_columns(tile)
        forward_near(
            width,
            own.product.at[:, here],
            rate.at[:, here],
            coef.at[:, here],
            skip.at[:, here],
            own.mixed.at[:, here],
            own.kernel.at[:, here],
            taps,
        )

    def far_tile(tile):
        here = lane_columns(tile)
        forward_far(
            width,
            sums.at[tile],
            entering.at[:, here],
            rate.at[:, here],
            coef.at[:, here],
            own.mixed.at[:, here],
            own.held.at[tile],
            decay,
        )

    def out_rows(i):
        rows = row_block(i, 128)
        gated = (own.queries[rows, :] * own.mixed[rows, :]).astype(low)
        own.gated[rows, :] = gated
        middle = own.middle[rows, :] + jnp.dot(
            gated, brought[3][...], preferred_element_type=jnp.float32
        )
        own.middle[rows, :] = middle
        standard, factor = standardize(middle)
        own.standard_two[rows, :] = standard
        own.factor_two[rows, :] = jnp.broadcast_to(factor, (128, LANES))
        own.normed_two[rows, :] = (
            standard * vector(vectors, GAIN_TWO) + vector(vectors, BIAS_TWO)
        ).astype(low)

    def loop(item, between=()):
        between = list(between)
        run_loop(item, between + [[]] * (item.steps() - len(between)))

    def keep_all(*copies):
        for one in copies:
            one.start()

    vectors[...] = jnp.zeros(vectors.shape, jnp.float32)
    singles = (given.skip, given.gain_one, given.bias_one, given.gain_two, given.bias_two)
    for place, single in enumerate(singles):
        vectors[place : place + 1, :] = single[...][None]
    keep_all(kept.vectors)
    loop(Loop(row_count // 128, norm_rows))
    keep_all(kept.standard_one, kept.factor_one, kept.normed_one)
    weights[0].wait()
    loop(project_to(own.key_rows, brought[0], lead))
    send_edge()
    weights[1].wait()
    loop(project_to(own.values, brought[1], 0))
    keep_all(kept.values)
    take_edge()
    between = [[] for unused in range(tiles)]
    between[tiles // 2 - 1].append(begin_half(0))
    between[tiles - 2].append(arrive_half(0, 0))
    loop(Loop(tiles, states_tile), between)
    begin_half(1)()
    keep_all(kept.key_rows, kept.keys_mixed, kept.product)
    weights[2].wait()
    loop(project_to(own.queries, brought[2], 0))
    keep_all(kept.queries)
    arrive_half(1, 0)()
    if levels > 1:
        arrive_half(0, 1)()
    loop(Loop(row_count // 128, grad_rows))
    keep_all(kept.out_grad)
    between = [[] for unused in range(tiles)]
    for level in range(1, levels):
        if level + 1 < levels:
            between[max(0, level * tiles // levels - 1)].append(arrive_half(0, level + 1))
            between[max(0, level * tiles // levels - 1)].insert(0, arrive_half(1, level))
        else:
            between[tiles - 1].append(arrive_half(1, level))
    loop(Loop(tiles, near_tile), between)
    keep_all(kept.kernel)
    loop(Loop(tiles, far_tile))
    keep_all(kept.mixed, kept.held)
    weights[3].wait()
    loop(Loop(row_count // 128, out_rows))
    keep_all(kept.gated, kept.middle, kept.normed_two, kept.standard_two, kept.factor_two)
    for copy, unused in halves:
        for level in range(levels):
            copy(level).wait_send()
    pl.when(me < size - 1)(edge(me + 1).wait_send)
    for one in kept:
        one.wait()


def forward(row_count, arrays):
    size = lax.axis_size("seq")
    bits = [1 << place for place in range(size.bit_length() - 1)]
    states, channels = arrays.rate.shape
    tiles, width = channels // LANES, row_count // CHUNKS
    halo = arrays.taps.shape[0] - 1
    full, low = jnp.float32, jnp.bfloat16
    square = ((row_count, channels), full)
    low_square = ((row_count, channels), low)
    thin = ((row_count, LANES), full)
    held = ((tiles, states * CHUNKS, LANES), full)
    outs = ForwardOut(
        product=square,
        held=held,
        kernel=((width, channels), full),
        values=square,
        keys_mixed=square,
        key_rows=((row_count + halo * CHUNKS, channels), full),
        queries=square,
        mixed=square,
        gated=low_square,
        middle=square,
        normed_two=low_square,
        standard_two=square,
        factor_two=thin,
        normed_one=low_square,
        standard_one=square,
        factor_one=thin,
        out_grad=low_square,
        vectors=((8, channels), full),
    )
    square_low = (channels, channels)
    weights = [(square_low, low)] * 4
    scratch = list(outs) + weights + [held, thin, ((states, LANES), full), ((states, channels), full)]
    scratch += [((8, channels), full)] * 2 + [((states, channels), full)] * (2 * len(bits))
    counts = [2 * len(bits) + 1, 2 * len(bits) + 1, len(outs) + 4]
    found = pl.pallas_call(
        functools.partial(forward_body, row_count, size, bits),
        out_shape=[jax.ShapeDtypeStruct(*out) for out in outs],
        in_specs=[
            pl.BlockSpec(memory_space=pltpu.HBM if shape == square_low else pltpu.VMEM)
            for shape in (getattr(arrays, name).shape for name in ForwardIn._fields)
        ],
        out_specs=[pl.BlockSpec(memory_space=pltpu.HBM)] * len(outs),
        scratch_shapes=[pltpu.VMEM(*shape) for shape in scratch]
        + [pltpu.SemaphoreType.DMA((count,)) for count in counts],
        compiler_params=pltpu.CompilerParams(
            collective_id=1, has_side_effects=True, vmem_limit_bytes=VMEM_LIMIT
        ),
    )(*[getattr(arrays, name) for name in ForwardIn._fields])
    return ForwardOut(*found)


class BackwardIn(NamedTuple):
    up_weight: Any
    down_weight: Any
    out_weight: Any
    query_weight: Any
    key_weight: Any
    value_weight: Any
    product: Any
    held: Any
    values: Any
    keys_mixed: Any
    key_rows: Any
    queries: Any
    mixed: Any
    gated: Any
    middle: Any
    standard_two: Any
    factor_two: Any
    standard_one: Any
    factor_one: Any
    rate: Any
    coef: Any
    vectors: Any
    taps: Any
    kernel: Any
    out_grad: Any
    normed_one: Any
    normed_two: Any


FAR = 19


class Results(NamedTuple):
    down: Any
    up: Any
    out: Any
    query: Any
    value: Any
    key: Any
    small: Any
    tokens: Any
    mixed_out: Any
    own_down: Any
    own_up: Any
    own_out: Any


HIDDEN_AT_ONCE = 256
STAGES = 3


def gelu_pair(values):
    slope = math.sqrt(2.0 / math.pi)
    squared = values * values
    bent = jnp.tanh(slope * (values + 0.044715 * (values * squared)))
    half = 0.5 * (1.0 + bent)
    steep = 0.5 * values * (1.0 - bent * bent) * (slope * (1.0 + 3.0 * 0.044715 * squared))
    return values * half, half + steep


def backward_body(row_count, size, line, bits, lanes, order, *refs):
    width = row_count // CHUNKS
    given = BackwardIn(*refs[: len(BackwardIn._fields)])
    rest = list(refs[len(given) :])

    def take(count):
        taken = rest[:count]
        del rest[:count]
        return taken

    results = Results(*take(len(Results._fields)))
    semaphores = rest[-6:-3]
    load_sems, swap_send, swap_recv = rest[-3:]
    del rest[-6:]
    (grad_query, grad_value, grad_key, small) = take(4)
    (shifted, total, grad_middle) = take(3)
    (grad_queries, values_low, keys_low, weight) = take(4)
    (entering, edge_out, edge_in) = take(3)
    stages = [(ref, load_sems.at[20 + i]) for i, ref in enumerate(take(STAGES + 1))]
    levels = len(bits)
    totals, arrivals = take(levels), take(levels)

    me = lax.axis_index("seq")
    z = lax.axis_index("batch")
    channels = small.shape[1]
    tiles = channels // LANES
    rate, coef = given.rate, given.coef
    states = rate.shape[0]
    tap_count = given.taps.shape[0]
    halo = tap_count - 1
    hidden = given.up_weight.shape[1]
    low, full = jnp.bfloat16, jnp.float32
    misc = 2 * states

    barrier = pltpu.get_barrier_semaphore()

    def greet(device):
        pl.semaphore_signal(barrier, inc=1, device_id=device, device_id_type=MESH)

    for bit in bits:
        greet((me + bit * (1 - 2 * ((me // bit) % 2)), z))
    pl.when(z > 0)(lambda: greet((me, z - 1)))
    pl.when(z < line - 1)(lambda: greet((me, z + 1)))
    pl.when(me > 0)(lambda: greet((me - 1, z)))
    pl.when(me < size - 1)(lambda: greet((me + 1, z)))
    pl.semaphore_wait(
        barrier,
        len(bits)
        + jnp.where(z > 0, 1, 0)
        + jnp.where(z < line - 1, 1, 0)
        + jnp.where(me > 0, 1, 0)
        + jnp.where(me < size - 1, 1, 0),
    )

    def local(source, target, place):
        return pltpu.make_async_copy(source, target, load_sems.at[place])

    def fetch(*triples):
        copies = [local(*triple) for triple in triples]
        for copy in copies:
            copy.start()
        for copy in copies:
            copy.wait()

    def add_small(row, value):
        small[row : row + 1, :] += jnp.sum(value, axis=0, keepdims=True)

    def half_exchange(part):
        size_of = channels // 2
        here = pl.ds(part * size_of, size_of)
        first = part * levels
        return state_exchange(
            bits,
            row_count,
            rate.at[:, here],
            [ref.at[:, here] for ref in totals],
            [ref.at[:, here] for ref in arrivals],
            entering.at[:, here],
            [swap_send.at[first + level] for level in range(levels)],
            [swap_recv.at[first + level] for level in range(levels)],
            False,
        )

    halves = [half_exchange(0), half_exchange(1)]

    def edge(device):
        return pltpu.make_async_remote_copy(
            src_ref=edge_out,
            dst_ref=edge_in,
            send_sem=swap_send.at[2 * levels],
            recv_sem=swap_recv.at[2 * levels],
            device_id=(device, z),
            device_id_type=MESH,
        )

    steps = hidden // HIDDEN_AT_ONCE
    per_block = channels // HIDDEN_AT_ONCE
    held_weight = local(given.out_weight, weight, 7)
    held_standard = local(given.standard_two, shifted.at[:row_count], 8)
    held_gated = local(given.gated, values_low, 9)
    held_middle = local(given.middle, total, 10)
    out_rows = local(keys_low, results.mixed_out, 10)

    def feed_forward(
        up_tile, down_tile, active, grad_low, slope, down_sum, up_sum, block_a, block_b, thin
    ):
        def weights(step):
            here = row_block(step, HIDDEN_AT_ONCE)
            slot = step % 2
            return (
                local(given.up_weight.at[:, here], up_tile.at[slot], slot),
                local(given.down_weight.at[here, :], down_tile.at[slot], 2 + slot),
            )

        def sums(step):
            part = step // per_block
            here = row_block(step % per_block, HIDDEN_AT_ONCE)
            return (
                local(down_sum, results.own_down.at[part, here, :], 4),
                local(up_sum, results.own_up.at[part, :, here], 5),
            )

        def start():
            for copy in weights(0):
                copy.start()
            for copy in (held_middle, held_weight, held_standard, held_gated):
                copy.start()
            small[...] = jnp.zeros(small.shape, full)
            grad_middle[...] = jnp.zeros(grad_middle.shape, full)
            held_middle.wait()

        def part_one(step):
            slot = step % 2
            for copy in weights(step):
                copy.wait()

            @pl.when(step + 1 < steps)
            def following():
                for copy in weights(step + 1):
                    copy.start()

            before = jnp.dot(
                given.normed_two[...], up_tile[slot], preferred_element_type=full
            )
            after, steep = gelu_pair(before)
            active[...] = after.astype(low)
            slope[...] = steep

        def part_two(step):
            slot = step % 2
            total[...] += jnp.dot(active[...], down_tile[slot], preferred_element_type=full)
            grads = project_back(given.out_grad[...], down_tile[slot])
            grad_low[...] = (grads * slope[...]).astype(low)

        def part_three(step):
            @pl.when(step > 0)
            def previous():
                for copy in sums(step - 1):
                    copy.wait()

            down_sum[...] = weight_grad(active[...], given.out_grad[...])
            up_sum[...] = weight_grad(given.normed_two[...], grad_low[...])
            for copy in sums(step):
                copy.start()

        def part_four(step):
            grad_middle[...] += project_back(grad_low[...], up_tile[step % 2])

        def finish():
            for copy in sums(steps - 1):
                copy.wait()
            keys_low[...] = total[...].astype(low)
            out_rows.start()
            held_standard.wait()
            held_weight.wait()
            held_gated.wait()
            out_rows.wait()

        def norm_two(i):
            rows = row_block(i, 128)
            fetch((given.factor_two.at[rows, :], thin, 11))
            grads, standard = grad_middle[rows, :], shifted[rows, :]
            add_small(misc + tap_count + 3, grads * standard)
            add_small(misc + tap_count + 4, grads)
            back = given.out_grad[rows, :].astype(full) + norm_back(
                grads, vector(given.vectors, GAIN_TWO), standard, thin[:, 0:1]
            )
            grad_middle[rows, :] = back
            keys_low[rows, :] = back.astype(low)

        def out_sum(i):
            here = row_block(i, 256)
            down_sum[...] = weight_grad(values_low[:, here], keys_low[...])
            fetch((down_sum, results.own_out.at[0, here, :], 4))

        def gate(i):
            rows = row_block(i, 128)
            fetch(
                (given.mixed.at[rows, :], block_a, 11),
                (given.queries.at[rows, :], block_b, 12),
            )
            grads = project_back(keys_low[rows, :], weight[...])
            grad_queries[rows, :] = (grads * block_a[...]).astype(low)
            total[rows, :] = grads * block_b[...]

        return [
            start,
            Loop(steps, part_one, part_two, part_three, part_four),
            finish,
            Loop(row_count // 128, norm_two),
            Loop(channels // 256, out_sum),
            Loop(row_count // 128, gate),
        ]

    def weight_sum(target, grads):
        def body(i):
            rows = row_block(i, 256)
            target[rows, :] = weight_grad(given.normed_one[:, rows], grads[...])

        return Loop(channels // 256, body)

    back = shifted

    def mixer(
        rows_tile, keys_tile, other, held_tile, back_tile, taps, sums, after, decay, hop, lag
    ):
        def tile_loads(tile):
            here, slot = lane_columns(tile), tile % 2
            return (
                local(given.product.at[:, here], rows_tile.at[slot], 10 + slot),
                local(given.held.at[tile], held_tile.at[slot], 12 + slot),
                local(given.values.at[:, here], other.at[slot, pl.ds(0, row_count)], 14 + slot),
                local(given.keys_mixed.at[:, here], keys_tile.at[slot], 16 + slot),
            )

        def key_loads(tile):
            slot = tile % 2
            return local(given.key_rows.at[:, lane_columns(tile)], other.at[slot], 14 + slot)

        def first_tile(tile):
            here = lane_columns(tile)
            backward_states(
                width,
                total.at[:, here],
                rate.at[:, here],
                sums.at[tile],
                totals[0].at[:, here],
                decay,
            )
            pl.when(tile == tiles // 2 - 1)(halves[0][0](0).start)

        def start_tiles():
            for copy in tile_loads(0):
                copy.start()
            halves[1][0](0).start()

        def near(tile):
            here, slot = lane_columns(tile), tile % 2
            pl.when(tile == tiles // 2)(functools.partial(halves[1][1], levels - 1))
            for copy in tile_loads(tile):
                copy.wait()

            @pl.when(tile + 1 < tiles)
            def following():
                for copy in tile_loads(tile + 1):
                    copy.start()

            decay[...] = jnp.exp(-rate[:, here])
            backward_near(
                width,
                total.at[:, here],
                rows_tile.at[slot],
                sums.at[tile],
                entering.at[:, here],
                rate.at[:, here],
                given.vectors.at[0:1, here],
                given.kernel.at[:, here],
                back_tile,
                small.at[0:states, here],
                small.at[states:misc, here],
                decay,
                hop,
                taps,
                after,
                lag,
            )

        def far(half):
            def part(tile):
                here, slot = lane_columns(tile), tile % 2
                groups = states // GROUP // 2
                backward_far(
                    width,
                    total.at[:, here],
                    rows_tile.at[slot],
                    sums.at[tile],
                    held_tile.at[slot],
                    coef.at[:, here],
                    back_tile,
                    small.at[0:states, here],
                    small.at[states:misc, here],
                    decay,
                    hop,
                    after,
                    range(half * groups, (half + 1) * groups),
                )

            return part

        def end(tile):
            here, slot = lane_columns(tile), tile % 2
            row = misc + tap_count
            small[row : row + 1, here] = jnp.sum(
                total[:, here] * rows_tile[slot], axis=0, keepdims=True
            )
            small[states:misc, here] = -coef[:, here] * small[states:misc, here]
            shifted[0:row_count, here] = back_tile[...] * other[slot, 0:row_count, :]
            values_low[:, here] = (back_tile[...] * keys_tile[slot]).astype(low)

        held_ones = local(given.standard_one, total, 7)
        held_factor = local(given.factor_one, back_tile, 8)

        def send_edge():
            key_loads(0).start()
            held_ones.start()
            held_factor.start()
            edge_out[...] = jnp.zeros(edge_out.shape, full)
            for place in range(halo):
                row = place * CHUNKS
                edge_out[place : place + 1, :] = shifted[row : row + 1, :]
            pl.when(me > 0)(edge(me - 1).start)

            @pl.when(me == size - 1)
            def at_end():
                edge_in[...] = jnp.zeros(edge_in.shape, full)

        def take_edge():
            pl.when(me < size - 1)(edge(me + 1).wait_recv)

        def keys_part(tile):
            here, slot = lane_columns(tile), tile % 2
            key_loads(tile).wait()

            @pl.when(tile + 1 < tiles)
            def following():
                key_loads(tile + 1).start()

            for place in range(halo):
                rows = shifted[place * CHUNKS : (place + 1) * CHUNKS, here]
                start = row_count + place * CHUNKS
                shifted[start : start + CHUNKS, here] = jnp.concatenate(
                    [rows[1:], edge_in[place : place + 1, here]], axis=0
                )
            tap = given.taps
            sum_rows = tap[0:1, here] * shifted[0:row_count, here]
            for offset in range(1, tap_count):
                start = offset * CHUNKS
                sum_rows = sum_rows + tap[offset : offset + 1, here] * (
                    shifted[start : start + row_count, here]
                )
            keys_low[:, here] = sum_rows.astype(low)
            grads = shifted[0:row_count, here]
            for offset in range(tap_count):
                start = (halo - offset) * CHUNKS
                small[misc + offset : misc + offset + 1, here] = jnp.sum(
                    grads * other[slot, start : start + row_count, :], axis=0, keepdims=True
                )

        def back_sum(index, grads):
            def body(i):
                rows = row_block(i, 128)
                term = project_back(grads[rows, :], weight[...])
                back[rows, :] = term if index == 0 else back[rows, :] + term

            return Loop(row_count // 128, body)

        def before_norm():
            held_ones.wait()
            held_factor.wait()

        def norm_one(i):
            rows = row_block(i, ROWS_AT_ONCE)
            grads, standard = back[rows, :], total[rows, :]
            add_small(misc + tap_count + 1, grads * standard)
            add_small(misc + tap_count + 2, grads)
            grad_middle[rows, :] += norm_back(
                grads, vector(given.vectors, GAIN_ONE), standard, back_tile[rows, 0:1]
            )

        tokens_out = local(grad_middle, results.tokens, 9)
        work = [Loop(tiles, first_tile), start_tiles]
        work.append(weight_sum(grad_query, grad_queries))
        for level in range(levels):
            work.append(functools.partial(halves[0][1], level))
            if level < levels - 1:
                work.append(functools.partial(halves[1][1], level))
        work.append(Loop(tiles, near, far(0), far(1), end))
        work.append(send_edge)
        work.append(weight_sum(grad_value, values_low))
        work.append(take_edge)
        work.append(Loop(tiles, keys_part))
        work.append(weight_sum(grad_key, keys_low))
        chain = (
            (given.query_weight, grad_queries),
            (given.key_weight, keys_low),
            (given.value_weight, values_low),
        )
        for index, (source, grads) in enumerate(chain):
            work.append(functools.partial(fetch, (source, weight, 0)))
            work.append(back_sum(index, grads))
        work.append(before_norm)
        work.append(Loop(row_count // ROWS_AT_ONCE, norm_one))
        work.append(tokens_out.start)
        work.append(tokens_out.wait)
        return work

    def block_of(lane):
        cols = pl.ds(lane.column, lane.columns)
        if lane.array == 0:
            target = results.down.at[pl.ds(lane.part * channels, channels), cols]
            return results.own_down.at[lane.part, :, cols], target
        if lane.array == 1:
            target = results.up.at[:, pl.ds(lane.part * channels + lane.column, lane.columns)]
            return results.own_up.at[lane.part, :, cols], target
        if lane.array == 2:
            return results.own_out.at[0, :, cols], results.out.at[:, cols]
        source = (grad_query, grad_value, grad_key, small)[lane.array - 3]
        return source.at[:, cols], results[lane.array].at[:, cols]

    pending = [copy(level).wait_send for copy, unused in halves for level in range(levels)]
    pending.append(lambda: pl.when(me > 0)(edge(me - 1).wait_send))
    programs = []
    start = 0
    for lane in lanes:
        source, target = block_of(lane)
        programs.append(
            lane_steps(
                lane,
                line,
                source,
                target,
                take(len(lane.buffers(line))),
                stages,
                semaphores,
                start,
                pending,
            )
        )
        start += lane.copies(line)

    def vmem(*shape, kind=full):
        return pltpu.VMEM(shape, kind)

    count = work_steps(row_count, channels, hidden, levels)
    runner = Runner(lanes, programs, count, order)
    done = [0]

    def run(make):
        def scoped(*refs):
            work = make(*refs)
            done[0] += steps_in(work)
            runner.run(work)

        return scoped

    pl.run_scoped(
        run(feed_forward),
        vmem(2, channels, HIDDEN_AT_ONCE, kind=low),
        vmem(2, HIDDEN_AT_ONCE, channels, kind=low),
        vmem(row_count, HIDDEN_AT_ONCE, kind=low),
        vmem(row_count, HIDDEN_AT_ONCE, kind=low),
        vmem(row_count, HIDDEN_AT_ONCE),
        vmem(HIDDEN_AT_ONCE, channels),
        vmem(channels, HIDDEN_AT_ONCE),
        vmem(128, channels),
        vmem(128, channels),
        vmem(128, LANES),
    )
    cells = states * CHUNKS
    pl.run_scoped(
        run(mixer),
        vmem(2, row_count, LANES),
        vmem(2, row_count, LANES),
        vmem(2, row_count + halo * CHUNKS, LANES),
        vmem(2, cells, LANES),
        vmem(row_count, LANES),
        vmem(row_count, LANES),
        vmem(tiles, cells, LANES),
        vmem(cells, LANES),
        vmem(states, LANES),
        vmem(states, LANES),
        vmem(width, LANES),
    )
    assert done[0] == count
    call_all(runner.lanes())
    call_all(pending)


def work_steps(row_count, channels, hidden, levels):
    tiles, weights = channels // LANES, channels // 256
    first = 2 + 4 * (hidden // HIDDEN_AT_ONCE) + 2 * (row_count // 128) + weights
    second = 6 * tiles + 3 * weights + 2 * levels + 5 + 3 * (row_count // 128)
    return first + second + row_count // ROWS_AT_ONCE + 3


def backward(row_count, arrays, plan, order):
    size, line = lax.axis_size("seq"), lax.axis_size("batch")
    bits = [1 << place for place in range(size.bit_length() - 1)]
    channels, hidden = arrays.up_weight.shape
    states = arrays.rate.shape[0]
    tap_count = arrays.taps.shape[0]
    misc_rows = 2 * states + tap_count + 5
    small_rows = misc_rows + -misc_rows % (8 * size)
    full, low = jnp.float32, jnp.bfloat16
    parts = hidden // channels
    lanes = []
    for index, pieces in enumerate(plan):
        columns = channels if index == 6 else channels // 2
        for piece, (flipped, line_first) in enumerate(pieces):
            rows = small_rows if index == 6 else channels
            if rows % (8 * size * line):
                line_first = False
            path = bits[:0:-1] if flipped else bits[1:]
            lane = Lane(rows, columns, path, line_first, index > 2)
            lane.array, lane.part, lane.column = index, piece // 2, piece % 2 * columns
            lanes.append(lane)
    square = ((channels, channels), full)
    wide = ((row_count, channels), full)
    low_wide = ((row_count, channels), low)
    small = ((small_rows, channels), full)
    key_rows = arrays.key_rows.shape[0]
    one = ((states, channels), full)
    scratch = [square] * 3 + [small, ((key_rows, channels), full), wide, wide]
    scratch += [low_wide] * 3 + [((channels, channels), low)]
    scratch += [one] + [((8, channels), full)] * 2 + [((channels // 2, channels // 2), full)] * (STAGES + 1)
    scratch += [one] * (2 * len(bits))
    scratch = [pltpu.VMEM(*shape) for shape in scratch]
    scratch += [buffer for lane in lanes for buffer in lane.buffers(line)]
    copies = sum(lane.copies(line) for lane in lanes)
    counts = [21 + STAGES, 2 * len(bits) + 1, 2 * len(bits) + 1]
    outs = [((hidden, channels), full), ((channels, hidden), full)] + [square] * 4
    outs += [small, wide, low_wide]
    outs += [((parts, channels, channels), full)] * 2 + [((1, channels, channels), full)]
    found = pl.pallas_call(
        functools.partial(backward_body, row_count, size, line, bits, lanes, order),
        out_shape=[jax.ShapeDtypeStruct(*out) for out in outs],
        in_specs=[pl.BlockSpec(memory_space=pltpu.HBM)] * FAR
        + [pl.BlockSpec(memory_space=pltpu.VMEM)] * (len(BackwardIn._fields) - FAR),
        out_specs=[pl.BlockSpec(memory_space=pltpu.HBM)] * len(outs),
        scratch_shapes=scratch
        + [pltpu.SemaphoreType.DMA((copies,)), pltpu.SemaphoreType.DMA((copies,))]
        + [pltpu.SemaphoreType.REGULAR((copies,))]
        + [pltpu.SemaphoreType.DMA((count,)) for count in counts],
        compiler_params=pltpu.CompilerParams(
            collective_id=0, has_side_effects=True, vmem_limit_bytes=VMEM_LIMIT
        ),
    )(*[getattr(arrays, name) for name in BackwardIn._fields])
    return Results(*found)


def finish_body(row_count, states, tap_count, *refs):
    width = row_count // CHUNKS
    count = 9
    sources, targets = Results(*refs[:count], None, None, None), refs[count:]
    large, (mixed_out, tokens) = targets[:6], targets[6:8]
    (taps, coef, rate, skip, gain_one, bias_one, gain_two, bias_two) = targets[8:16]
    held_small, held_mixed, held_tokens, load_sems, store_sems = targets[16:21]
    passing = targets[21:]
    tiles = held_tokens.shape[0]
    pairs = [(sources.small, held_small), (sources.mixed_out, held_mixed)]
    for tile in range(tiles):
        pairs.append((sources.tokens.at[:, pl.ds(tile * LANES, LANES)], held_tokens.at[tile]))
    loads, stores = [], []
    for source, held, target in zip(sources[:6], passing, large):
        size = PASSING_SIZE // target.shape[1]
        for start in range(0, target.shape[0], size):
            rows = pl.ds(start, size)
            stores.append((held.at[rows, :], target.at[rows, :]))
            loads.append((source.at[rows, :], held.at[rows, :]))
    stores = [pltpu.make_async_copy(*pair, store_sems.at[i]) for i, pair in enumerate(stores)]
    copies = [pltpu.make_async_copy(*pair, load_sems.at[i]) for i, pair in enumerate(pairs + loads)]
    first_large = len(pairs)
    for copy in copies:
        copy.start()
    moves = list(zip(copies[first_large:], stores))

    def move(count):
        for load, store in moves[:count]:
            load.wait()
            store.start()
        del moves[:count]

    copies[0].wait()
    misc = 2 * states
    first = misc + tap_count
    coef[...] = held_small[0:states, :]
    rate[...] = held_small[states:misc, :]
    taps[...] = held_small[misc:first, :]
    for row, target in enumerate((skip, gain_one, bias_one, gain_two, bias_two)):
        target[...] = held_small[first + row, :]
    for copy in copies[1:first_large]:
        copy.wait()

    for chunk in range(CHUNKS):
        rows = slice(chunk * width, (chunk + 1) * width)
        for tile in range(tiles):
            tokens[rows, tile * LANES : (tile + 1) * LANES] = held_tokens.at[tile][
                pl.ds(chunk, width, stride=CHUNKS), :
            ]
        if chunk % 2:
            move(1)
    token = lax.broadcasted_iota(jnp.int32, (128, row_count), 0)
    row = lax.broadcasted_iota(jnp.int32, (128, row_count), 1)
    for i in range(row_count // 128):
        at = token + i * 128
        chosen = row == lax.rem(at, width) * CHUNKS + lax.div(at, width)
        picks = jnp.where(chosen, 1.0, 0.0).astype(jnp.bfloat16)
        mixed_out[i * 128 : (i + 1) * 128, :] = jnp.dot(
            picks, held_mixed[...], preferred_element_type=jnp.float32
        ).astype(jnp.bfloat16)
        move(2)
    move(len(moves))
    for store in stores:
        store.wait()


PASSING_SIZE = 384 * 768


def finish(row_count, states, tap_count, found):
    channels = found.small.shape[1]
    full = jnp.float32
    wide = (row_count, channels)
    shapes = [(array.shape, full) for array in found[:6]]
    shapes += [(wide, jnp.bfloat16), (wide, full), ((tap_count, channels), full)]
    shapes += [((states, channels), full)] * 2 + [((channels,), full)] * 5
    tiles = channels // LANES
    scratch = [(found.small.shape, full), (wide, jnp.bfloat16), ((tiles, row_count, LANES), full)]
    pieces = sum(array.size // PASSING_SIZE for array in found[:6])
    counts = [2 + tiles + pieces, pieces]
    memory = [pltpu.HBM] * 6 + [pltpu.VMEM] * 10
    return pl.pallas_call(
        functools.partial(finish_body, row_count, states, tap_count),
        out_shape=[jax.ShapeDtypeStruct(*shape) for shape in shapes],
        in_specs=[pl.BlockSpec(memory_space=pltpu.HBM)] * 9,
        out_specs=[pl.BlockSpec(memory_space=space) for space in memory],
        scratch_shapes=[pltpu.VMEM(*shape) for shape in scratch]
        + [pltpu.SemaphoreType.DMA((count,)) for count in counts]
        + [pltpu.VMEM(array.shape, full) for array in found[:6]],
        compiler_params=pltpu.CompilerParams(vmem_limit_bytes=VMEM_LIMIT),
    )(*found[:9])


PLAN = [
    [(False, False), (True, False), (True, False), (True, True), (True, False), (True, True), (True, True), (True, False)],
    [(True, False), (True, True), (False, True), (False, True), (False, False), (False, False), (True, False), (False, False)],
    [(False, False), (False, True)],
    [(False, False), (True, True)],
    [(True, False), (False, False)],
    [(True, False), (False, False)],
    [(False, False)],
]
ORDER = [
    25, 25, 25, 25, 25, 25, 25, 25, 25, 25, 25, 25, 8, 25, 25, 25, 25, 9, 1, 0, 25, 25, 8, 25,
    25, 25, 9, 25, 1, 0, 25, 25, 25, 25, 25, 25, 3, 2, 11, 25, 25, 8, 25, 25, 25, 9, 3, 25, 2,
    11, 0, 25, 25, 12, 25, 1, 25, 9, 8, 25, 25, 13, 4, 5, 25, 12, 25, 25, 25, 1, 13, 3, 2, 9, 4,
    25, 5, 25, 25, 0, 25, 14, 25, 25, 9, 15, 12, 3, 6, 7, 25, 11, 14, 25, 15, 4, 13, 3, 6, 7,
    25, 8, 12, 2, 11, 25, 9, 25, 1, 25, 14, 8, 25, 15, 16, 11, 17, 25, 1, 13, 5, 25, 9, 8, 4, 3,
    16, 17, 25, 14, 25, 1, 11, 0, 5, 25, 7, 8, 25, 15, 9, 3, 25, 6, 11, 0, 5, 25, 16, 25, 8, 12,
    11, 25, 1, 6, 2, 0, 5, 25, 25, 25, 7, 25, 18, 19, 3, 25, 16, 25, 13, 10, 11, 5, 12, 18, 6,
    4, 19, 25, 10, 2, 25, 1, 5, 13, 12, 0, 17, 3, 2, 6, 18, 4, 25, 25, 13, 14, 25, 17, 5, 25,
    15, 0, 25, 25, 9, 12, 4, 2, 25, 18, 6, 17, 25, 7, 25, 14, 25, 13, 16, 25, 25, 12, 11, 25,
    25, 15, 4, 6, 2, 14, 25, 9, 17, 25, 19, 25, 25, 15, 7, 25, 13, 16, 25, 9, 4, 25, 25, 6, 11,
    7, 17, 14, 25, 25, 15, 19, 16, 17, 25, 25, 25, 25, 25, 21, 20, 10, 7, 3, 21, 11, 14, 20, 5,
    10, 15, 19, 16, 18, 25, 25, 17, 25, 25, 25, 6, 25, 25, 3, 25, 25, 25, 22, 23, 25, 21, 7, 5,
    25, 25, 25, 25, 22, 25, 18, 23, 25, 25, 20, 16, 25, 25, 25, 19, 17, 25, 25, 25, 25, 25, 25,
    21, 6, 25, 25, 3, 25, 25, 25, 23, 25, 25, 24, 5, 25, 25, 21, 20, 10, 22, 19, 24, 18, 23, 10,
    17, 20, 21, 18, 22, 10, 6, 19, 23, 20, 10, 17, 24, 19, 22, 23, 21, 24, 20, 18, 24, 10, 21,
    22, 19, 24, 20, 23, 10, 21, 22, 20, 19, 23, 24, 22, 10, 24, 19, 23, 10, 22, 24,
]


def on_device(
    tokens,
    norm1_gain,
    norm1_bias,
    query_weight,
    key_weight,
    value_weight,
    shift_taps,
    ssm_coef,
    ssm_rate,
    ssm_skip,
    out_weight,
    norm2_gain,
    norm2_bias,
    up_weight,
    down_weight,
    out_grad,
):
    unused, row_count, channels = tokens.shape
    states = ssm_rate.shape[0]
    tap_count = shift_taps.shape[0]

    arrays = SimpleNamespace(
        tokens=tokens[0],
        token_grads=out_grad[0],
        skip=ssm_skip,
        gain_one=norm1_gain,
        bias_one=norm1_bias,
        gain_two=norm2_gain,
        bias_two=norm2_bias,
        query_weight=query_weight,
        key_weight=key_weight,
        value_weight=value_weight,
        out_weight=out_weight,
        up_weight=up_weight,
        down_weight=down_weight,
        taps=shift_taps,
        rate=ssm_rate,
        coef=ssm_coef,
    )
    vars(arrays).update(forward(row_count, arrays)._asdict())
    found = backward(row_count, arrays, PLAN, ORDER)
    (down, up, out, query, value, key, mixed_out, grad_tokens, *rest) = finish(
        row_count, states, tap_count, found
    )
    (taps, coef, rate, skip, gain_one, bias_one, gain_two, bias_two) = rest
    return (
        mixed_out[None],
        grad_tokens[None],
        gain_one,
        bias_one,
        query,
        key,
        value,
        taps,
        coef,
        rate,
        skip,
        out,
        gain_two,
        bias_two,
        up,
        down,
    )


def solution(mesh):
    placed = (P("batch", "seq", None),) + (P(),) * 14 + (P("batch", "seq", None),)
    return jax.shard_map(
        on_device,
        mesh=mesh,
        in_specs=placed,
        out_specs=(P("batch", "seq", None),) * 2 + (P(),) * 14,
        check_vma=False,
    )
```
